256 devices in a mesh: tm: 8 (over z_lo, core), view: 8 (over z_hi, y), space: 4 (over x).
Axes of the slice: x: 4, y: 4, z: 8 (z_hi: 2, z_lo: 4; z = z_hi * 4 + z_lo), core: 2. Of those that a mesh axis runs over, the one named last changes fastest.
Arguments:
- latents: bfloat16 [8, 8, 512, 768], P('view', 'tm', 'space'), may hold values from -6 to 6
- cotangent: bfloat16 [8, 8, 512, 768], P('view', 'tm', 'space'), may hold values from -6 to 6
- w_qkv_space: bfloat16 [3, 768, 768], P(None, 'space'), may hold values from -1 to 1
- w_out_space: bfloat16 [768, 768], P('space'), may hold values from -0.21875 to 0.21875
- w_qkv_view: bfloat16 [3, 768, 768], P(None, 'space'), may hold values from -1 to 1
- w_out_view: bfloat16 [768, 768], P('space'), may hold values from -0.21875 to 0.21875
- w_qkv_time: bfloat16 [3, 768, 768], P(None, 'space'), may hold values from -1 to 1
- w_out_time: bfloat16 [768, 768], P('space'), may hold values from -0.21875 to 0.21875
Outputs:
- grad_latents: bfloat16 [8, 8, 512, 768], P('view', 'tm', 'space')
The draws below stay inside these ranges and needn't reach their ends.
All inputs are finite; a program needn't handle non-finite values.
Results may differ from the reference program's by a relative error of at most 0.025.
Values may be sent and summed in bfloat16 or wider, within the bound.
A program may use at most 128 MiB of HBM per device.

```python
import jax
import jax.numpy as jnp
from jax import lax

D = 768
HEADS = 12
HEAD_DIM = 64
SEQ = 512
VIEWS = 8
FRAMES = 8


def projection(key, boost_low, boost_high):
    first, second, third = jax.random.split(key, 3)
    drawn = jax.random.truncated_normal(first, -4.0, 4.0, (3, D, D), jnp.float32) * D ** (-0.5)
    shared = jax.random.truncated_normal(second, -4.0, 4.0, (1, D, D), jnp.float32) * D ** (-0.5)
    strength = jnp.repeat(jax.random.uniform(third, (HEADS,), jnp.float32, boost_low, boost_high), D // HEADS)
    aligned = shared * strength[None, :, None] + drawn[:2]
    joined = jnp.concatenate([aligned, drawn[2:]], axis=0)
    return jnp.clip(joined, -1.0, 1.0).astype(jnp.bfloat16)


def draw_w_qkv_space(key, part):
    key = jax.random.fold_in(key, 11)
    return projection(key, 0.0, 0.0)


def draw_w_qkv_view(key, part):
    key = jax.random.fold_in(key, 12)
    return projection(key, 0.0, 0.0)


def draw_w_qkv_time(key, part):
    key = jax.random.fold_in(key, 13)
    return projection(key, 0.0, 0.0)


def block_scale(stream_key, extent, cuts, low, high):
    factor_of, own = 1.0, jax.random.fold_in(stream_key, 6)
    for axis_at, blocks in cuts:
        draws = jnp.exp(jax.random.uniform(jax.random.fold_in(own, axis_at), (blocks,), jnp.float32, low / len(cuts), high / len(cuts)))
        factor_of = factor_of * jnp.repeat(draws, extent[axis_at] // blocks).reshape([-1 if axis == axis_at else 1 for axis in range(len(extent))])
    return factor_of


def noise(key, shape, width, bound, cuts=(), dtype=jnp.bfloat16):
    values = jax.random.normal(key, shape, jnp.float32) * width
    if len(cuts) > 0:
        values = block_scale(key, shape, cuts, -0.22, 0.18) * values
    return jnp.clip(values, min=-bound, max=bound).astype(dtype)


def setup_inputs(seed: int = 0) -> dict:
    key_of = jax.random.split(jax.random.key(seed), 9)
    return {
        "latents": noise(key_of[0], (VIEWS, FRAMES, SEQ, D), 1.0, 6.0, ((0, 8), (1, 8), (2, 4))),
        "cotangent": noise(key_of[1], (VIEWS, FRAMES, SEQ, D), 1.0, 6.0, ((0, 8), (1, 8), (2, 4))),
        "w_qkv_space": draw_w_qkv_space(jax.random.fold_in(key_of[8], 71), 0),
        "w_out_space": noise(key_of[3], (D, D), D ** -0.5, 0.21875, ((0, 4),)),
        "w_qkv_view": draw_w_qkv_view(jax.random.fold_in(key_of[8], 71), 0),
        "w_out_view": noise(key_of[5], (D, D), D ** -0.5, 0.21875, ((0, 4),)),
        "w_qkv_time": draw_w_qkv_time(jax.random.fold_in(key_of[8], 71), 0),
        "w_out_time": noise(key_of[7], (D, D), D ** -0.5, 0.21875, ((0, 4),)),
    }


def rms_rows(stream):
    values = stream.astype(jnp.float32)
    factor = lax.rsqrt(lax.optimization_barrier(jnp.mean(values * values, axis=-1, keepdims=True)) + 1e-06)
    return (values * factor, factor)

def frame_shares(packed):
    scale = packed.shape[-1] ** (-0.5)
    scores = jnp.einsum('qhe,khe->hqk', packed[:, 0].astype(jnp.float32), packed[:, 1].astype(jnp.float32)) * scale
    top = lax.optimization_barrier(jnp.max(scores, axis=-1, keepdims=True))
    expo = jnp.exp(scores - top)
    return expo / lax.optimization_barrier(jnp.sum(expo, axis=-1, keepdims=True))

def frame_forward(packed):
    rounded = frame_shares(packed).astype(jnp.bfloat16)
    return jnp.einsum('hqk,khe->qhe', rounded.astype(jnp.float32), packed[:, 2].astype(jnp.float32)).astype(jnp.bfloat16)

def frame_backward(items):
    packed, output, out_grad = items
    scale = packed.shape[-1] ** (-0.5)
    shares = frame_shares(packed)
    rounded = shares.astype(jnp.bfloat16)
    grad_f = out_grad.astype(jnp.float32)
    row_dot = lax.optimization_barrier(jnp.sum(grad_f * output.astype(jnp.float32), axis=-1))
    share_grad = jnp.einsum('qhe,khe->hqk', grad_f, packed[:, 2].astype(jnp.float32))
    score_grad = shares * (share_grad - row_dot.T[:, :, None])
    rounded_grad = score_grad.astype(jnp.bfloat16).astype(jnp.float32)
    query_grad = jnp.einsum('hqk,khe->qhe', rounded_grad, packed[:, 1].astype(jnp.float32)) * scale
    key_grad = jnp.einsum('hqk,qhe->khe', rounded_grad, packed[:, 0].astype(jnp.float32)) * scale
    value_grad = jnp.einsum('hqk,qhe->khe', rounded.astype(jnp.float32), grad_f)
    return jnp.stack([query_grad, key_grad, value_grad], axis=1).astype(jnp.bfloat16)

def small_forward(queries, key_rows, value_rows):
    scale = queries.shape[-1] ** (-0.5)
    scores = jnp.einsum('athe,bthe->abth', queries.astype(jnp.float32), key_rows.astype(jnp.float32)) * scale
    top = lax.optimization_barrier(jnp.max(scores, axis=1, keepdims=True))
    expo = jnp.exp(scores - top)
    shares = expo / lax.optimization_barrier(jnp.sum(expo, axis=1, keepdims=True))
    output = jnp.einsum('abth,bthe->athe', shares, value_rows.astype(jnp.float32)).astype(jnp.bfloat16)
    return (output, shares)

def small_backward(queries, key_rows, value_rows, output, out_grad, shares):
    scale = queries.shape[-1] ** (-0.5)
    grad_f = out_grad.astype(jnp.float32)
    row_dot = lax.optimization_barrier(jnp.sum(grad_f * output.astype(jnp.float32), axis=-1))
    share_grad = jnp.einsum('athe,bthe->abth', grad_f, value_rows.astype(jnp.float32))
    score_grad = shares * (share_grad - row_dot[:, None])
    query_grad = jnp.einsum('abth,bthe->athe', score_grad, key_rows.astype(jnp.float32)) * scale
    key_grad = jnp.einsum('abth,athe->bthe', score_grad, queries.astype(jnp.float32)) * scale
    value_grad = jnp.einsum('abth,athe->bthe', shares, grad_f)
    return (query_grad, key_grad, value_grad)

def space_forward(packed):
    frames = packed.reshape(VIEWS * FRAMES, SEQ, 3, HEADS, HEAD_DIM)
    return lax.map(frame_forward, frames).reshape(VIEWS, FRAMES, SEQ, HEADS, HEAD_DIM)

def space_backward(packed, output, out_grad):
    frames = packed.reshape(VIEWS * FRAMES, SEQ, 3, HEADS, HEAD_DIM)
    outs = output.reshape(VIEWS * FRAMES, SEQ, HEADS, HEAD_DIM)
    grads = out_grad.reshape(VIEWS * FRAMES, SEQ, HEADS, HEAD_DIM)
    return lax.map(frame_backward, (frames, outs, grads)).reshape(VIEWS, FRAMES, SEQ, 3, HEADS, HEAD_DIM)

def axis_forward(packed):
    count = packed.shape[0]
    flat = packed.reshape(count, -1, 3, HEADS, HEAD_DIM)
    output, shares = small_forward(flat[:, :, 0], flat[:, :, 1], flat[:, :, 2])
    return output.reshape(packed.shape[:3] + (HEADS, HEAD_DIM))

def axis_backward(packed, output, out_grad):
    count = packed.shape[0]
    flat = packed.reshape(count, -1, 3, HEADS, HEAD_DIM)
    outs = output.reshape(count, -1, HEADS, HEAD_DIM)
    grads = out_grad.reshape(count, -1, HEADS, HEAD_DIM)
    recomputed, shares = small_forward(flat[:, :, 0], flat[:, :, 1], flat[:, :, 2])
    query_grad, key_grad, value_grad = small_backward(flat[:, :, 0], flat[:, :, 1], flat[:, :, 2], outs, grads, shares)
    return jnp.stack([query_grad, key_grad, value_grad], axis=2).astype(jnp.bfloat16).reshape(packed.shape)

def view_forward(packed):
    return axis_forward(packed)

def view_backward(packed, output, out_grad):
    return axis_backward(packed, output, out_grad)

def time_forward(packed):
    moved = jnp.transpose(packed, (1, 0, 2, 3, 4, 5))
    return jnp.transpose(axis_forward(moved), (1, 0, 2, 3, 4))

def time_backward(packed, output, out_grad):
    moved = jnp.transpose(packed, (1, 0, 2, 3, 4, 5))
    result = axis_backward(moved, jnp.transpose(output, (1, 0, 2, 3, 4)), jnp.transpose(out_grad, (1, 0, 2, 3, 4)))
    return jnp.transpose(result, (1, 0, 2, 3, 4, 5))

def reference(latents, cotangent, w_qkv_space, w_out_space, w_qkv_view, w_out_view, w_qkv_time, w_out_time):
    layers = ((w_qkv_space, w_out_space, space_forward, space_backward), (w_qkv_view, w_out_view, view_forward, view_backward), (w_qkv_time, w_out_time, time_forward, time_backward))
    stream = latents
    saved_all = []
    for position in range(3):
        w_qkv, w_out, forward, backward = layers[position]
        normed, factor = rms_rows(stream)
        packed = jnp.dot(normed.astype(jnp.bfloat16).reshape(-1, D), w_qkv.reshape(3 * D, D).T, preferred_element_type=jnp.float32)
        packed = packed.astype(jnp.bfloat16).reshape(VIEWS, FRAMES, SEQ, 3, HEADS, HEAD_DIM)
        output = forward(packed)
        saved_all.append((stream, packed, output))
        if position < 2:
            term = jnp.dot(output.reshape(-1, D), w_out, preferred_element_type=jnp.float32).reshape(VIEWS, FRAMES, SEQ, D)
            stream = (stream.astype(jnp.float32) + term).astype(jnp.bfloat16)
    upstream = cotangent
    for position in (2, 1, 0):
        w_qkv, w_out, forward, backward = layers[position]
        earlier, packed, output = saved_all[position]
        out_grad = jnp.dot(upstream.reshape(-1, D), w_out.T, preferred_element_type=jnp.float32)
        out_grad = out_grad.astype(jnp.bfloat16).reshape(VIEWS, FRAMES, SEQ, HEADS, HEAD_DIM)
        packed_grad = backward(packed, output, out_grad)
        normed_grad = jnp.dot(packed_grad.reshape(-1, 3 * D), w_qkv.reshape(3 * D, D), preferred_element_type=jnp.float32)
        normed_grad = normed_grad.reshape(VIEWS, FRAMES, SEQ, D)
        normed, factor = rms_rows(earlier)
        inner = lax.optimization_barrier(jnp.mean(normed_grad * normed, axis=-1, keepdims=True))
        upstream = (upstream.astype(jnp.float32) + factor * (normed_grad - normed * inner)).astype(jnp.bfloat16)
    return upstream
```

```python
import jax
import jax.numpy as jnp
from jax import lax
from jax.experimental import pallas as pl
from jax.experimental.pallas import tpu as pltpu
from jax.sharding import PartitionSpec as P

MESH = pl.DeviceIdType.MESH
BF = jnp.bfloat16
F32 = jnp.float32
NN = ((1,), (0,))
NT = ((1,), (1,))
TN = ((0,), (0,))

D = 768
TOK = 128
NSP = 4
NV = 8
NT_ = 8
CH = 16
HD = 64
LH = 3
LW = LH * HD
GH = 4
GW = GH * HD
GROUPS = D // GW
SCALE = HD**-0.5
NSEM = 208


def dot(a, b, dims):
    return lax.dot_general(a, b, (dims, ((), ())), preferred_element_type=F32)


def rms(values):
    factor = lax.rsqrt(jnp.mean(values * values, axis=-1, keepdims=True) + 1e-06)
    return values * factor, factor


def finish(upstream, earlier, normed_grad):
    normed, factor = rms(earlier.astype(F32))
    inner = jnp.mean(normed_grad * normed, axis=-1, keepdims=True)
    return (upstream.astype(F32) + factor * (normed_grad - normed * inner)).astype(BF)


def softmax0(scores):
    top = jnp.max(scores, axis=0, keepdims=True)
    expo = jnp.exp(scores - top)
    return expo * (1.0 / jnp.sum(expo, axis=0, keepdims=True))


def head_masks(rows):
    head = lax.broadcasted_iota(jnp.int32, (rows, TOK), 0) // HD
    return [(head == h).astype(F32).astype(BF) for h in range(rows // HD)]


def stacked(values, masks):
    return jnp.concatenate([values * m for m in masks], axis=1)


def per_head(left, right):
    heads = left.shape[0] // HD
    return jnp.concatenate(
        [
            dot(left[h * HD : (h + 1) * HD], right[:, h * TOK : (h + 1) * TOK], NN)
            for h in range(heads)
        ],
        axis=0,
    )


def body(
    x_in, cot_in, wqs_in, wos_in, wqv_in, wov_in, wqt_in, wot_in,
    out_ref,
    x_ref, cot_ref, wqs_ref,
    nb, k_nat, v_nat, qts, kvt, pts, gts, ogts, dqt, ats, att,
    xb, x2, xt, x3, c1, c2, ut, u2, uv, u3, ogs, og, rsend, rs, rf,
    bias, kt_v, vt_v, qts_v, pt_v,
    wos, wqv, wov, wqt, wot,
    send_sem, recv_sem, local_sem,
):
    t = lax.axis_index("tm")
    v = lax.axis_index("view")
    s = lax.axis_index("space")
    core = lax.rem(t, 2)
    sibling = t + 1 - 2 * core
    y = lax.rem(v, 4)
    half = lax.rem(y, 2)
    step = 1 - 2 * core
    y_next = v - y + lax.rem(y + step + 4, 4)
    s_next = lax.rem(s + step + 4, 4)
    s_prev = lax.rem(s - step + 4, 4)

    def plus(me, k, n):
        return lax.rem(me + k + n, n)

    sent = []
    count = [0]

    def ticket():
        count[0] += 1
        return count[0] - 1

    def push(src, dst, axis, index, number):
        to = {axis: index} if isinstance(axis, str) else dict(zip(axis, index))
        copy = pltpu.make_async_remote_copy(
            src_ref=src,
            dst_ref=dst,
            send_sem=send_sem.at[number],
            recv_sem=recv_sem.at[number],
            device_id=to,
            device_id_type=MESH,
        )
        copy.start()
        sent.append(copy)

    def landed(dst, number, axis, index):
        to = {axis: index} if isinstance(axis, str) else dict(zip(axis, index))
        pltpu.make_async_remote_copy(
            src_ref=dst,
            dst_ref=dst,
            send_sem=send_sem.at[number],
            recv_sem=recv_sem.at[number],
            device_id=to,
            device_id_type=MESH,
        ).wait_recv()

    def rows(owner, c, h, size):
        return pl.ds(pl.multiple_of(owner * LW + c * 96 + h * 48, 16), size)

    class Gather:
        def __init__(self, shard, full, number):
            self.shard, self.full = shard, full
            self.x1 = [ticket(), ticket()]
            self.x2 = ticket()
            self.ys = [ticket() for _ in range(3)]
            self.sib = [ticket() for _ in range(3)]
            self.others = [plus(s, -1, 4), plus(s, 1, 4), plus(s, 2, 4)]
            self.own = pltpu.make_async_copy(
                shard, full.at[:, pl.ds(pl.multiple_of(s * LW, 16), LW), :], local_sem.at[number]
            )

        def piece(self, owner, c, h, size=48):
            return self.full.at[:, rows(owner, c, h, size), :]

        def a(self):
            self.own.start()
            mine = self.shard.at[:, pl.ds(pl.multiple_of(core * 96 + half * 48, 16), 48), :]
            there = self.piece(s, core, half)
            push(mine, there, "space", plus(s, 1, 4), self.x1[0])
            push(mine, there, "space", plus(s, -1, 4), self.x1[1])

        def b(self):
            for at in range(2):
                landed(self.piece(self.others[at], core, half), self.x1[at], "space", self.others[at])
            far = self.piece(s_prev, core, half)
            push(far, far, "space", s_next, self.x2)
            for at in range(2):
                part = self.piece(self.others[at], core, half)
                push(part, part, "view", y_next, self.ys[at])

        def c(self):
            part = self.piece(self.others[2], core, half)
            landed(part, self.x2, "space", s_prev)
            push(part, part, "view", y_next, self.ys[2])

        def d(self):
            for at in range(3):
                landed(self.piece(self.others[at], core, 1 - half), self.ys[at], "view", y_next)
                part = self.piece(self.others[at], core, 0, 96)
                push(part, part, "tm", sibling, self.sib[at])

        def e(self):
            for at in range(3):
                landed(self.piece(self.others[at], 1 - core, 0, 96), self.sib[at], "tm", sibling)
            self.own.wait()

    g_os = Gather(wos_in, wos, 0)
    g_qv = Gather(wqv_in, wqv, 1)
    g_ov = Gather(wov_in, wov, 2)
    g_qt = Gather(wqt_in, wqt, 3)
    g_ot = Gather(wot_in, wot, 4)

    loads = [
        pltpu.make_async_copy(src, dst, local_sem.at[5 + at])
        for at, (src, dst) in enumerate(((x_in, x_ref), (wqs_in, wqs_ref), (cot_in, cot_ref)))
    ]
    for copy in loads:
        copy.start()

    barrier = pltpu.get_barrier_semaphore()
    for k in range(NSP):
        for j in range(NV):
            if k or j:
                pl.semaphore_signal(
                    barrier,
                    inc=1,
                    device_id={"view": plus(v, j, NV), "space": plus(s, k, NSP)},
                    device_id_type=MESH,
                )
    for k in range(1, NT_):
        pl.semaphore_signal(barrier, inc=1, device_id={"tm": plus(t, k, NT_)}, device_id_type=MESH)

    loads[0].wait()
    x_rows = x_ref[...].reshape(TOK, D)
    normed, _ = rms(x_rows.astype(F32))
    nb[0] = normed.astype(BF)
    key_at = lax.broadcasted_iota(jnp.int32, (TOK, GH * TOK), 0)
    query_at = lax.broadcasted_iota(jnp.int32, (TOK, GH * TOK), 1)
    bias[...] = jnp.where(lax.rem(key_at, CH) == lax.rem(query_at, CH), 0.0, -1e30)
    lmask = head_masks(LW)
    gmask = head_masks(GW)
    pl.semaphore_wait(barrier, NSP * NV + NT_ - 2)

    halves = [slice(0, TOK // 2), slice(TOK // 2, TOK)]
    n_num = [{k: ticket() for k in range(1, NSP)} for _ in halves]
    for h, part in enumerate(halves):
        for k in (1, 3):
            push(nb.at[0, part], nb.at[k, part], "space", plus(s, k, NSP), n_num[h][k])
    loads[1].wait()
    loads[2].wait()
    g_os.a()
    order = (4, 3, 5, 2, 6, 1, 7)
    x2_num = [ticket() for _ in range(NV)]
    c1_num = [ticket() for _ in range(NV)]
    for j in order:
        to = plus(v, j, NV)
        push(x_ref.at[to], xb.at[j], "view", to, x2_num[j])
    for j in order:
        to = plus(v, j, NV)
        push(cot_ref.at[to], c1.at[j], "view", to, c1_num[j])
    xb[0] = x_ref[v]
    c1[0] = cot_ref[v]

    def project_space(k):
        tokens = nb[k]
        packed = dot(wqs_ref[...], tokens, NT)
        at = slice(k * TOK, (k + 1) * TOK)
        query = packed[:LW].astype(BF) * jnp.asarray(SCALE, BF)
        qts[:, k * LH * TOK : (k + 1) * LH * TOK] = stacked(query, lmask)
        kvt[:, at] = packed[LW:].astype(BF)
        k_nat[at, :] = jnp.transpose(packed[LW : 2 * LW]).astype(BF)
        v_nat[at, :] = jnp.transpose(packed[2 * LW :]).astype(BF)

    project_space(0)
    for h, part in enumerate(halves):
        for k in (1, 3):
            landed(nb.at[k, part], n_num[h][k], "space", plus(s, -k, NSP))
        push(nb.at[1 + 2 * core, part], nb.at[2, part], "space", s_next, n_num[h][2])
    g_qv.a()
    project_space(1)
    project_space(3)
    g_os.b()
    for h, part in enumerate(halves):
        landed(nb.at[2, part], n_num[h][2], "space", plus(s, 2, NSP))
    project_space(2)

    a_num = [[ticket() for _ in range(NV)] for _ in range(NSP)]

    def attend_space(k):
        at = slice(k * LH * TOK, (k + 1) * LH * TOK)
        shares = softmax0(dot(k_nat[...], qts[:, at], NN)).astype(BF)
        pts[:, at] = shares
        out = jnp.transpose(per_head(kvt[LW:, :], shares)).astype(BF)
        ats[k] = out.reshape(NV, CH, LW)
        for j in order + (0,):
            to = (plus(v, j, NV), plus(s, -k, NSP))
            if k or j:
                push(ats.at[k, to[0]], att.at[s, j], ("view", "space"), to, a_num[k][j])
            else:
                att[pl.ds(s, 1), 0:1] = ats[0:1, pl.ds(v, 1)]

    attend_space(2)
    g_qv.b()
    g_os.c()
    g_ov.a()
    g_ot.a()
    attend_space(1)
    attend_space(3)
    g_qv.c()
    g_ov.b()
    g_ot.b()
    attend_space(0)
    g_os.d()
    g_qt.a()
    g_ov.c()
    g_ot.c()

    def slot_of(view):
        return lax.rem(v - view + NV, NV)

    c2_num = [ticket() for _ in range(NT_)]
    for k in range(1, NV):
        landed(c1.at[k], c1_num[k], "view", plus(v, -k, NV))
    for j in range(1, NT_):
        to = plus(t, j, NT_)
        push(c1.at[slot_of(to)], c2.at[j], "tm", to, c2_num[j])
    c2[0] = c1[slot_of(t)]
    g_qv.d()
    g_ov.d()
    g_ot.d()
    g_os.e()

    for j in range(1, NV):
        landed(xb.at[j], x2_num[j], "view", plus(v, -j, NV))
    for k in (2, 1, 3, 0):
        for j in range(NV):
            if k or j:
                group = plus(s, k, NSP)
                landed(att.at[group, j], a_num[k][j], ("view", "space"), (plus(v, -j, NV), group))
    term = dot(att[0].reshape(TOK, LW), wos[0, :LW, :], NN)
    for h in range(1, NSP):
        term += dot(att[h].reshape(TOK, LW), wos[0, h * LW : (h + 1) * LW, :], NN)
    x2[...] = (xb[...].reshape(TOK, D).astype(F32) + term).astype(BF).reshape(NV, CH, D)
    g_qt.b()
    rows_view = x2[...].reshape(TOK, D)
    normed, _ = rms(rows_view.astype(F32))
    tokens = normed.astype(BF)
    g_qv.e()

    def attend_small(w, g):
        lanes = slice(g * GW, (g + 1) * GW)
        query = dot(w[0, lanes, :], tokens, NT).astype(BF) * jnp.asarray(SCALE, BF)
        key_t = dot(w[1, lanes, :], tokens, NT).astype(BF)
        value_t = dot(w[2, lanes, :], tokens, NT).astype(BF)
        queries = stacked(query, gmask)
        shares = softmax0(dot(key_t, queries, TN) + bias[...]).astype(BF)
        return queries, key_t, value_t, shares

    def backward_small(w, g, queries, key_t, value_t, shares, out_grad):
        lanes = slice(g * GW, (g + 1) * GW)
        grads = stacked(out_grad, gmask)
        share_grad = dot(value_t, grads, TN)
        wide = shares.astype(F32)
        row_dot = jnp.sum(wide * share_grad, axis=0, keepdims=True)
        score_grad = (wide * (share_grad - row_dot)).astype(BF)
        query_grad = (per_head(key_t, score_grad) * SCALE).astype(BF)
        key_grad = dot(score_grad, queries, NT).astype(BF)
        value_grad = dot(shares, grads, NT).astype(BF)
        total = dot(query_grad, w[0, lanes, :], TN)
        total += dot(key_grad, w[1, lanes, :], NN)
        return total + dot(value_grad, w[2, lanes, :], NN)

    outs = []
    for g in range(GROUPS):
        queries, key_t, value_t, shares = attend_small(wqv, g)
        qts_v[g], kt_v[g], vt_v[g], pt_v[g] = queries, key_t, value_t, shares
        outs.append(per_head(value_t, shares).astype(BF))
        if g == 1:
            g_qt.c()
    g_ov.e()
    term = dot(jnp.concatenate(outs, axis=0), wov[0], TN)
    xt[...] = (rows_view.astype(F32) + term).astype(BF).reshape(NV, CH, D)

    x3_num = [ticket() for _ in range(NT_)]
    for j in range(1, NT_):
        to = plus(t, j, NT_)
        push(xt.at[slot_of(to)], x3.at[j], "tm", to, x3_num[j])
    x3[0] = xt[slot_of(t)]
    g_qt.d()
    for j in range(1, NT_):
        landed(c2.at[j], c2_num[j], "tm", plus(t, -j, NT_))
    for j in range(1, NT_):
        landed(x3.at[j], x3_num[j], "tm", plus(t, -j, NT_))
    rows_time = x3[...].reshape(TOK, D)
    normed, _ = rms(rows_time.astype(F32))
    tokens = normed.astype(BF)
    upstream = c2[...].reshape(TOK, D)
    g_qt.e()
    g_ot.e()

    total = jnp.zeros((TOK, D), F32)
    for g in range(GROUPS):
        queries, key_t, value_t, shares = attend_small(wqt, g)
        out_grad = dot(wot[0, g * GW : (g + 1) * GW, :], upstream, NT).astype(BF)
        total += backward_small(wqt, g, queries, key_t, value_t, shares, out_grad)
    ut[...] = finish(upstream, rows_time, total).reshape(NT_, CH, D)

    u2_num = [ticket() for _ in range(NT_)]
    here = slot_of(t)
    for j in range(1, NT_):
        push(ut.at[j], u2.at[here], "tm", plus(t, -j, NT_), u2_num[j])
    u2[pl.ds(here, 1)] = ut[0:1]
    for j in range(1, NT_):
        landed(u2.at[slot_of(plus(t, j, NT_))], u2_num[j], "tm", plus(t, j, NT_))
    upstream = u2[...].reshape(TOK, D)
    total = jnp.zeros((TOK, D), F32)
    for g in range(GROUPS):
        out_grad = dot(wov[0, g * GW : (g + 1) * GW, :], upstream, NT).astype(BF)
        total += backward_small(wqv, g, qts_v[g], kt_v[g], vt_v[g], pt_v[g], out_grad)
    upstream = finish(upstream, x2[...].reshape(TOK, D), total)
    uv[...] = upstream.reshape(NV, CH, D)

    out_grad = dot(wos[0], upstream, NT)
    for h in range(NSP):
        part = jnp.transpose(out_grad[h * LW : (h + 1) * LW]).astype(BF)
        ogs[h] = part.reshape(NV, CH, LW)
    og_num = [[ticket() for _ in range(NV)] for _ in range(NSP)]
    for k in (2, 1, 3, 0):
        for j in order + (0,):
            to = (plus(v, -j, NV), plus(s, k, NSP))
            if k or j:
                push(ogs.at[to[1], j], og.at[k, v], ("view", "space"), to, og_num[k][j])
    og[0:1, pl.ds(v, 1)] = ogs[pl.ds(s, 1), 0:1]
    u3_num = [ticket() for _ in range(NV)]
    for j in order:
        push(uv.at[j], u3.at[v], "view", plus(v, -j, NV), u3_num[j])
    u3[pl.ds(v, 1)] = uv[0:1]

    def backward_space(k):
        at = slice(k * LH * TOK, (k + 1) * LH * TOK)
        out_grad = og[k].reshape(TOK, LW)
        grads = jnp.concatenate([out_grad * m for m in nmask], axis=0)
        ogts[at, :] = grads
        share_grad = dot(v_nat[...], grads, NT)
        wide = pts[:, at].astype(F32)
        row_dot = jnp.sum(wide * share_grad, axis=0, keepdims=True)
        score_grad = (wide * (share_grad - row_dot)).astype(BF)
        gts[:, at] = score_grad
        dqt[k] = (per_head(kvt[:LW, :], score_grad) * SCALE).astype(BF)

    head_at = lax.broadcasted_iota(jnp.int32, (TOK, LW), 1) // HD
    nmask = [(head_at == h).astype(F32).astype(BF) for h in range(LH)]
    for k in (0, 1, 3, 2):
        for j in range(NV):
            if k or j:
                frm = (plus(v, j, NV), plus(s, -k, NSP))
                landed(og.at[k, frm[0]], og_num[k][j], ("view", "space"), frm)
        backward_space(k)

    def partial_sums(k):
        at = pl.ds(pl.multiple_of(k * TOK, TOK), TOK)
        key_grad = dot(gts[at, :], qts[...], NT).astype(BF)
        value_grad = dot(pts[at, :], ogts[...], NN).astype(BF)
        part = dot(dqt[k], wqs_ref[:LW, :], TN)
        part += dot(key_grad, wqs_ref[LW : 2 * LW, :], NN)
        return part + dot(value_grad, wqs_ref[2 * LW :, :], NN)

    rf_num, near_num, late_num = ticket(), ticket(), ticket()
    rsend[0] = partial_sums(2).astype(BF)
    push(rsend.at[0], rf, "space", s_next, rf_num)
    rsend[1] = partial_sums(1 + 2 * core).astype(BF)
    push(rsend.at[1], rs.at[0], "space", s_prev, near_num)
    late = partial_sums(3 - 2 * core)
    landed(rf, rf_num, "space", s_prev)
    rsend[2] = (late + rf[...].astype(F32)).astype(BF)
    push(rsend.at[2], rs.at[1], "space", s_next, late_num)
    total = partial_sums(0)
    landed(rs.at[0], near_num, "space", s_next)
    total += rs[0].astype(F32)
    landed(rs.at[1], late_num, "space", s_prev)
    total += rs[1].astype(F32)
    for j in range(1, NV):
        landed(u3.at[plus(v, j, NV)], u3_num[j], "view", plus(v, j, NV))
    out_ref[...] = finish(u3[...].reshape(TOK, D), x_ref[...].reshape(TOK, D), total)

    for copy in sent:
        copy.wait_send()


def on_device(latents, cotangent, wqs, wos, wqv, wov, wqt, wot):
    vmem = pl.BlockSpec(memory_space=pltpu.VMEM)
    hbm = pl.BlockSpec(memory_space=pltpu.HBM)

    def buf(*shape, dtype=BF):
        return pltpu.VMEM(shape, dtype)

    wide = NSP * LH * TOK
    out = pl.pallas_call(
        body,
        out_shape=jax.ShapeDtypeStruct((TOK, D), BF),
        in_specs=[hbm] * 8,
        out_specs=vmem,
        scratch_shapes=[
            buf(NV, CH, D),
            buf(NV, CH, D),
            buf(3 * LW, D),
            buf(NSP, TOK, D),
            buf(NSP * TOK, LW),
            buf(NSP * TOK, LW),
            buf(LW, wide),
            buf(2 * LW, NSP * TOK),
            buf(NSP * TOK, wide),
            buf(NSP * TOK, wide),
            buf(wide, LW),
            buf(NSP, LW, TOK),
            buf(NSP, NV, CH, LW),
            buf(NSP, NV, CH, LW),
        ]
        + [buf(NV, CH, D)] * 10
        + [
            buf(NSP, NV, CH, LW),
            buf(NSP, NV, CH, LW),
            buf(3, TOK, D),
            buf(2, TOK, D),
            buf(TOK, D),
            buf(TOK, GH * TOK, dtype=F32),
            buf(GROUPS, GW, TOK),
            buf(GROUPS, GW, TOK),
            buf(GROUPS, GW, GH * TOK),
            buf(GROUPS, TOK, GH * TOK),
            buf(1, D, D),
            buf(3, D, D),
            buf(1, D, D),
            buf(3, D, D),
            buf(1, D, D),
            pltpu.SemaphoreType.DMA((NSEM,)),
            pltpu.SemaphoreType.DMA((NSEM,)),
            pltpu.SemaphoreType.DMA((8,)),
        ],
        compiler_params=pltpu.CompilerParams(
            collective_id=0, has_side_effects=True, vmem_limit_bytes=60 * 1024 * 1024
        ),
        name="block_backward",
    )(
        latents.reshape(NV, CH, D),
        cotangent.reshape(NV, CH, D),
        wqs.reshape(3 * LW, D),
        wos[None],
        wqv,
        wov[None],
        wqt,
        wot[None],
    )
    return out[None, None]


def solution(mesh):
    in_specs = (
        P("view", "tm", "space", None),
        P("view", "tm", "space", None),
        P(None, "space", None),
        P("space", None),
        P(None, "space", None),
        P("space", None),
        P(None, "space", None),
        P("space", None),
    )
    return jax.shard_map(
        on_device,
        mesh=mesh,
        in_specs=in_specs,
        out_specs=P("view", "tm", "space", None),
        check_vma=False,
    )
```

```python
import jax
import jax.numpy as jnp
from jax import lax
from jax.experimental import pallas as pl
from jax.experimental.pallas import tpu as pltpu
from jax.sharding import PartitionSpec as P

MESH = pl.DeviceIdType.MESH
BF = jnp.bfloat16
F32 = jnp.float32
NN = ((1,), (0,))
NT = ((1,), (1,))
TN = ((0,), (0,))

D = 768
TOK = 128
NSP = 4
NV = 8
NT_ = 8
CH = 16
HD = 64
LH = 3
LW = LH * HD
GH = 4
GW = GH * HD
GROUPS = D // GW
SCALE = HD**-0.5
NSEM = 208


def dot(a, b, dims):
    return lax.dot_general(a, b, (dims, ((), ())), preferred_element_type=F32)


def rms(values):
    factor = lax.rsqrt(jnp.mean(values * values, axis=-1, keepdims=True) + 1e-06)
    return values * factor, factor


def finish(upstream, earlier, normed_grad):
    normed, factor = rms(earlier.astype(F32))
    inner = jnp.mean(normed_grad * normed, axis=-1, keepdims=True)
    return (upstream.astype(F32) + factor * (normed_grad - normed * inner)).astype(BF)


def softmax0(scores):
    top = jnp.max(scores, axis=0, keepdims=True)
    expo = jnp.exp(scores - top)
    return expo * (1.0 / jnp.sum(expo, axis=0, keepdims=True))


def head_masks(rows):
    head = lax.broadcasted_iota(jnp.int32, (rows, TOK), 0) // HD
    return [(head == h).astype(F32).astype(BF) for h in range(rows // HD)]


def stacked(values, masks):
    return jnp.concatenate([values * m for m in masks], axis=1)


def per_head(left, right):
    heads = left.shape[0] // HD
    return jnp.concatenate(
        [
            dot(left[h * HD : (h + 1) * HD], right[:, h * TOK : (h + 1) * TOK], NN)
            for h in range(heads)
        ],
        axis=0,
    )


def body(
    x_in, cot_in, wqs_in, wos_in, wqv_in, wov_in, wqt_in, wot_in,
    out_ref,
    x_ref, cot_ref, wqs_ref,
    nb, k_nat, v_nat, qts, kvt, pts, gts, ogts, dqt, ats, att,
    xb, x2, xt, x3, c1, c2, ut, u2, uv, u3, ogs, og, rsend, rs, rf,
    bias, kt_v, vt_v, qts_v, pt_v,
    wos, wqv, wov, wqt, wot,
    send_sem, recv_sem, local_sem,
):
    t = lax.axis_index("tm")
    v = lax.axis_index("view")
    s = lax.axis_index("space")
    core = lax.rem(t, 2)
    sibling = t + 1 - 2 * core
    y = lax.rem(v, 4)
    half = lax.rem(y, 2)
    step = 1 - 2 * core
    y_next = v - y + lax.rem(y + step + 4, 4)
    s_next = lax.rem(s + step + 4, 4)
    s_prev = lax.rem(s - step + 4, 4)

    def plus(me, k, n):
        return lax.rem(me + k + n, n)

    bits = [t % 2, t // 2 % 2, t // 4]

    def paired(m):
        return t + sum((1 - 2 * bits[at]) * 2**at for at in range(3) if m >> at & 1)

    tm_order = (6, 7, 4, 5, 2, 3, 1)
    sent = []
    count = [0]

    def ticket():
        count[0] += 1
        return count[0] - 1

    def push(src, dst, axis, index, number):
        to = {axis: index} if isinstance(axis, str) else dict(zip(axis, index))
        copy = pltpu.make_async_remote_copy(
            src_ref=src,
            dst_ref=dst,
            send_sem=send_sem.at[number],
            recv_sem=recv_sem.at[number],
            device_id=to,
            device_id_type=MESH,
        )
        copy.start()
        sent.append(copy)

    def landed(dst, number, axis, index):
        to = {axis: index} if isinstance(axis, str) else dict(zip(axis, index))
        pltpu.make_async_remote_copy(
            src_ref=dst,
            dst_ref=dst,
            send_sem=send_sem.at[number],
            recv_sem=recv_sem.at[number],
            device_id=to,
            device_id_type=MESH,
        ).wait_recv()

    def rows(owner, c, h, size):
        return pl.ds(pl.multiple_of(owner * LW + c * 96 + h * 48, 16), size)

    class Gather:
        def __init__(self, shard, full, number):
            self.shard, self.full = shard, full
            self.x1 = [ticket(), ticket()]
            self.x2 = ticket()
            self.ys = [ticket() for _ in range(3)]
            self.sib = [ticket() for _ in range(3)]
            self.others = [plus(s, -1, 4), plus(s, 1, 4), plus(s, 2, 4)]
            self.own = pltpu.make_async_copy(
                shard, full.at[:, pl.ds(pl.multiple_of(s * LW, 16), LW), :], local_sem.at[number]
            )

        def piece(self, owner, c, h, size=48):
            return self.full.at[:, rows(owner, c, h, size), :]

        def a(self):
            self.own.start()
            mine = self.shard.at[:, pl.ds(pl.multiple_of(core * 96 + half * 48, 16), 48), :]
            there = self.piece(s, core, half)
            push(mine, there, "space", plus(s, 1, 4), self.x1[0])
            push(mine, there, "space", plus(s, -1, 4), self.x1[1])

        def b(self):
            for at in range(2):
                landed(self.piece(self.others[at], core, half), self.x1[at], "space", self.others[at])
            far = self.piece(s_prev, core, half)
            push(far, far, "space", s_next, self.x2)
            for at in range(2):
                part = self.piece(self.others[at], core, half)
                push(part, part, "view", y_next, self.ys[at])

        def c(self):
            part = self.piece(self.others[2], core, half)
            landed(part, self.x2, "space", s_prev)
            push(part, part, "view", y_next, self.ys[2])

        def d(self):
            for at in range(3):
                landed(self.piece(self.others[at], core, 1 - half), self.ys[at], "view", y_next)
                part = self.piece(self.others[at], core, 0, 96)
                push(part, part, "tm", sibling, self.sib[at])

        def e(self):
            for at in range(3):
                landed(self.piece(self.others[at], 1 - core, 0, 96), self.sib[at], "tm", sibling)
            self.own.wait()

    g_os = Gather(wos_in, wos, 0)
    g_qv = Gather(wqv_in, wqv, 1)
    g_ov = Gather(wov_in, wov, 2)
    g_qt = Gather(wqt_in, wqt, 3)
    g_ot = Gather(wot_in, wot, 4)

    loads = [
        pltpu.make_async_copy(src, dst, local_sem.at[5 + at])
        for at, (src, dst) in enumerate(((x_in, x_ref), (wqs_in, wqs_ref), (cot_in, cot_ref)))
    ]
    for copy in loads:
        copy.start()

    barrier = pltpu.get_barrier_semaphore()
    for k in range(NSP):
        for j in range(NV):
            if k or j:
                pl.semaphore_signal(
                    barrier,
                    inc=1,
                    device_id={"view": plus(v, j, NV), "space": plus(s, k, NSP)},
                    device_id_type=MESH,
                )
    for k in range(1, NT_):
        pl.semaphore_signal(barrier, inc=1, device_id={"tm": plus(t, k, NT_)}, device_id_type=MESH)

    loads[0].wait()
    x_rows = x_ref[...].reshape(TOK, D)
    normed, _ = rms(x_rows.astype(F32))
    nb[0] = normed.astype(BF)
    key_at = lax.broadcasted_iota(jnp.int32, (TOK, GH * TOK), 0)
    query_at = lax.broadcasted_iota(jnp.int32, (TOK, GH * TOK), 1)
    bias[...] = jnp.where(lax.rem(key_at, CH) == lax.rem(query_at, CH), 0.0, -1e30)
    lmask = head_masks(LW)
    gmask = head_masks(GW)
    pl.semaphore_wait(barrier, NSP * NV + NT_ - 2)

    halves = [slice(0, TOK // 2), slice(TOK // 2, TOK)]
    n_num = [{k: ticket() for k in range(1, NSP)} for _ in halves]
    for h, part in enumerate(halves):
        for k in (1, 3):
            push(nb.at[0, part], nb.at[k, part], "space", plus(s, k, NSP), n_num[h][k])
    loads[1].wait()
    loads[2].wait()
    g_os.a()
    order = (4, 3, 5, 2, 6, 1, 7)
    x2_num = [ticket() for _ in range(NV)]
    c1_num = [ticket() for _ in range(NV)]
    for j in order:
        to = plus(v, j, NV)
        push(x_ref.at[to], xb.at[j], "view", to, x2_num[j])
    for j in order:
        to = plus(v, j, NV)
        push(cot_ref.at[to], c1.at[j], "view", to, c1_num[j])
    xb[0] = x_ref[v]
    c1[0] = cot_ref[v]

    def project_space(k):
        tokens = nb[k]
        packed = dot(wqs_ref[...], tokens, NT)
        at = slice(k * TOK, (k + 1) * TOK)
        query = packed[:LW].astype(BF) * jnp.asarray(SCALE, BF)
        qts[:, k * LH * TOK : (k + 1) * LH * TOK] = stacked(query, lmask)
        kvt[:, at] = packed[LW:].astype(BF)
        k_nat[at, :] = jnp.transpose(packed[LW : 2 * LW]).astype(BF)
        v_nat[at, :] = jnp.transpose(packed[2 * LW :]).astype(BF)

    project_space(0)
    for h, part in enumerate(halves):
        for k in (1, 3):
            landed(nb.at[k, part], n_num[h][k], "space", plus(s, -k, NSP))
        push(nb.at[1 + 2 * core, part], nb.at[2, part], "space", s_next, n_num[h][2])
    g_qv.a()
    project_space(1)
    project_space(3)
    g_os.b()
    for h, part in enumerate(halves):
        landed(nb.at[2, part], n_num[h][2], "space", plus(s, 2, NSP))
    project_space(2)

    a_num = [[ticket() for _ in range(NV)] for _ in range(NSP)]

    def attend_space(k):
        at = slice(k * LH * TOK, (k + 1) * LH * TOK)
        shares = softmax0(dot(k_nat[...], qts[:, at], NN)).astype(BF)
        pts[:, at] = shares
        out = jnp.transpose(per_head(kvt[LW:, :], shares)).astype(BF)
        ats[k] = out.reshape(NV, CH, LW)
        for j in order + (0,):
            to = (plus(v, j, NV), plus(s, -k, NSP))
            if k or j:
                push(ats.at[k, to[0]], att.at[s, j], ("view", "space"), to, a_num[k][j])
            else:
                att[pl.ds(s, 1), 0:1] = ats[0:1, pl.ds(v, 1)]

    attend_space(2)
    g_qv.b()
    g_os.c()
    g_ov.a()
    attend_space(1)
    g_ot.a()
    attend_space(3)
    g_qv.c()
    g_ov.b()
    g_qt.a()
    attend_space(0)
    g_os.d()
    g_ov.c()
    g_ot.b()

    def slot_of(view):
        return lax.rem(v - view + NV, NV)

    g_qv.d()
    g_ov.d()
    g_os.e()

    for j in range(1, NV):
        landed(xb.at[j], x2_num[j], "view", plus(v, -j, NV))
    for k in (2, 1, 3, 0):
        for j in range(NV):
            if k or j:
                group = plus(s, k, NSP)
                landed(att.at[group, j], a_num[k][j], ("view", "space"), (plus(v, -j, NV), group))
    c2_num = [ticket() for _ in range(NT_)]
    for k in range(1, NV):
        landed(c1.at[k], c1_num[k], "view", plus(v, -k, NV))
    for m in tm_order:
        push(c1.at[slot_of(paired(m))], c2.at[m], "tm", paired(m), c2_num[m])
    c2[0] = c1[slot_of(t)]
    g_ot.c()
    g_qt.b()
    term = dot(att[0].reshape(TOK, LW), wos[0, :LW, :], NN)
    for h in range(1, NSP):
        term += dot(att[h].reshape(TOK, LW), wos[0, h * LW : (h + 1) * LW, :], NN)
    x2[...] = (xb[...].reshape(TOK, D).astype(F32) + term).astype(BF).reshape(NV, CH, D)
    rows_view = x2[...].reshape(TOK, D)
    normed, _ = rms(rows_view.astype(F32))
    tokens = normed.astype(BF)
    g_qv.e()

    def attend_small(w, g):
        lanes = slice(g * GW, (g + 1) * GW)
        query = dot(w[0, lanes, :], tokens, NT).astype(BF) * jnp.asarray(SCALE, BF)
        key_t = dot(w[1, lanes, :], tokens, NT).astype(BF)
        value_t = dot(w[2, lanes, :], tokens, NT).astype(BF)
        queries = stacked(query, gmask)
        shares = softmax0(dot(key_t, queries, TN) + bias[...]).astype(BF)
        return queries, key_t, value_t, shares

    def backward_small(w, g, queries, key_t, value_t, shares, out_grad):
        lanes = slice(g * GW, (g + 1) * GW)
        grads = stacked(out_grad, gmask)
        share_grad = dot(value_t, grads, TN)
        wide = shares.astype(F32)
        row_dot = jnp.sum(wide * share_grad, axis=0, keepdims=True)
        score_grad = (wide * (share_grad - row_dot)).astype(BF)
        query_grad = (per_head(key_t, score_grad) * SCALE).astype(BF)
        key_grad = dot(score_grad, queries, NT).astype(BF)
        value_grad = dot(shares, grads, NT).astype(BF)
        total = dot(query_grad, w[0, lanes, :], TN)
        total += dot(key_grad, w[1, lanes, :], NN)
        return total + dot(value_grad, w[2, lanes, :], NN)

    outs = []
    for g in range(GROUPS):
        queries, key_t, value_t, shares = attend_small(wqv, g)
        qts_v[g], kt_v[g], vt_v[g], pt_v[g] = queries, key_t, value_t, shares
        outs.append(per_head(value_t, shares).astype(BF))
        if g == 0:
            g_ot.d()
            g_qt.c()
    g_ov.e()
    term = dot(jnp.concatenate(outs, axis=0), wov[0], TN)
    xt[...] = (rows_view.astype(F32) + term).astype(BF).reshape(NV, CH, D)

    x3_num = [ticket() for _ in range(NT_)]
    for m in tm_order:
        push(xt.at[slot_of(paired(m))], x3.at[m], "tm", paired(m), x3_num[m])
    x3[0] = xt[slot_of(t)]
    g_qt.d()
    g_ot.e()
    for m in tm_order:
        landed(c2.at[m], c2_num[m], "tm", paired(m))
    upstream = c2[...].reshape(TOK, D)
    out_grads = dot(wot[0], upstream, NT).astype(BF)
    for m in tm_order:
        landed(x3.at[m], x3_num[m], "tm", paired(m))
    rows_time = x3[...].reshape(TOK, D)
    normed, _ = rms(rows_time.astype(F32))
    tokens = normed.astype(BF)
    g_qt.e()

    total = jnp.zeros((TOK, D), F32)
    for g in range(GROUPS):
        queries, key_t, value_t, shares = attend_small(wqt, g)
        out_grad = out_grads[g * GW : (g + 1) * GW]
        total += backward_small(wqt, g, queries, key_t, value_t, shares, out_grad)
    ut[...] = finish(upstream, rows_time, total).reshape(NT_, CH, D)

    u2_num = [ticket() for _ in range(NT_)]
    here = slot_of(t)
    for m in tm_order:
        push(ut.at[m], u2.at[here], "tm", paired(m), u2_num[m])
    u2[pl.ds(here, 1)] = ut[0:1]
    for m in tm_order:
        landed(u2.at[slot_of(paired(m))], u2_num[m], "tm", paired(m))
    upstream = u2[...].reshape(TOK, D)
    total = jnp.zeros((TOK, D), F32)
    for g in range(GROUPS):
        out_grad = dot(wov[0, g * GW : (g + 1) * GW, :], upstream, NT).astype(BF)
        total += backward_small(wqv, g, qts_v[g], kt_v[g], vt_v[g], pt_v[g], out_grad)
    upstream = finish(upstream, x2[...].reshape(TOK, D), total)
    uv[...] = upstream.reshape(NV, CH, D)

    out_grad = dot(wos[0], upstream, NT)
    for h in range(NSP):
        part = jnp.transpose(out_grad[h * LW : (h + 1) * LW]).astype(BF)
        ogs[h] = part.reshape(NV, CH, LW)
    og_num = [[ticket() for _ in range(NV)] for _ in range(NSP)]
    for k in (2, 1, 3, 0):
        for j in order + (0,):
            to = (plus(v, -j, NV), plus(s, k, NSP))
            if k or j:
                push(ogs.at[to[1], j], og.at[k, v], ("view", "space"), to, og_num[k][j])
    og[0:1, pl.ds(v, 1)] = ogs[pl.ds(s, 1), 0:1]
    def backward_space(k):
        at = slice(k * LH * TOK, (k + 1) * LH * TOK)
        out_grad = og[k].reshape(TOK, LW)
        grads = jnp.concatenate([out_grad * m for m in nmask], axis=0)
        ogts[at, :] = grads
        share_grad = dot(v_nat[...], grads, NT)
        wide = pts[:, at].astype(F32)
        row_dot = jnp.sum(wide * share_grad, axis=0, keepdims=True)
        score_grad = (wide * (share_grad - row_dot)).astype(BF)
        gts[:, at] = score_grad
        dqt[k] = (per_head(kvt[:LW, :], score_grad) * SCALE).astype(BF)

    head_at = lax.broadcasted_iota(jnp.int32, (TOK, LW), 1) // HD
    nmask = [(head_at == h).astype(F32).astype(BF) for h in range(LH)]
    u3_num = [ticket() for _ in range(NV)]
    for k in (0, 1, 3, 2):
        for j in range(NV):
            if k or j:
                frm = (plus(v, j, NV), plus(s, -k, NSP))
                landed(og.at[k, frm[0]], og_num[k][j], ("view", "space"), frm)
        if k == 2:
            for j in order:
                push(uv.at[j], u3.at[v], "view", plus(v, -j, NV), u3_num[j])
        backward_space(k)
    u3[pl.ds(v, 1)] = uv[0:1]

    def partial_sums(k):
        at = pl.ds(pl.multiple_of(k * TOK, TOK), TOK)
        key_grad = dot(gts[at, :], qts[...], NT).astype(BF)
        value_grad = dot(pts[at, :], ogts[...], NN).astype(BF)
        part = dot(dqt[k], wqs_ref[:LW, :], TN)
        part += dot(key_grad, wqs_ref[LW : 2 * LW, :], NN)
        return part + dot(value_grad, wqs_ref[2 * LW :, :], NN)

    rf_num, near_num, late_num = ticket(), ticket(), ticket()
    rsend[0] = partial_sums(2).astype(BF)
    push(rsend.at[0], rf, "space", s_next, rf_num)
    rsend[1] = partial_sums(1 + 2 * core).astype(BF)
    push(rsend.at[1], rs.at[0], "space", s_prev, near_num)
    late = partial_sums(3 - 2 * core)
    landed(rf, rf_num, "space", s_prev)
    rsend[2] = (late + rf[...].astype(F32)).astype(BF)
    push(rsend.at[2], rs.at[1], "space", s_next, late_num)
    total = partial_sums(0)
    landed(rs.at[0], near_num, "space", s_next)
    total += rs[0].astype(F32)
    landed(rs.at[1], late_num, "space", s_prev)
    total += rs[1].astype(F32)
    for j in range(1, NV):
        landed(u3.at[plus(v, j, NV)], u3_num[j], "view", plus(v, j, NV))
    out_ref[...] = finish(u3[...].reshape(TOK, D), x_ref[...].reshape(TOK, D), total)

    for copy in sent:
        copy.wait_send()


def on_device(latents, cotangent, wqs, wos, wqv, wov, wqt, wot):
    vmem = pl.BlockSpec(memory_space=pltpu.VMEM)
    hbm = pl.BlockSpec(memory_space=pltpu.HBM)

    def buf(*shape, dtype=BF):
        return pltpu.VMEM(shape, dtype)

    wide = NSP * LH * TOK
    out = pl.pallas_call(
        body,
        out_shape=jax.ShapeDtypeStruct((TOK, D), BF),
        in_specs=[hbm] * 8,
        out_specs=vmem,
        scratch_shapes=[
            buf(NV, CH, D),
            buf(NV, CH, D),
            buf(3 * LW, D),
            buf(NSP, TOK, D),
            buf(NSP * TOK, LW),
            buf(NSP * TOK, LW),
            buf(LW, wide),
            buf(2 * LW, NSP * TOK),
            buf(NSP * TOK, wide),
            buf(NSP * TOK, wide),
            buf(wide, LW),
            buf(NSP, LW, TOK),
            buf(NSP, NV, CH, LW),
            buf(NSP, NV, CH, LW),
        ]
        + [buf(NV, CH, D)] * 10
        + [
            buf(NSP, NV, CH, LW),
            buf(NSP, NV, CH, LW),
            buf(3, TOK, D),
            buf(2, TOK, D),
            buf(TOK, D),
            buf(TOK, GH * TOK, dtype=F32),
            buf(GROUPS, GW, TOK),
            buf(GROUPS, GW, TOK),
            buf(GROUPS, GW, GH * TOK),
            buf(GROUPS, TOK, GH * TOK),
            buf(1, D, D),
            buf(3, D, D),
            buf(1, D, D),
            buf(3, D, D),
            buf(1, D, D),
            pltpu.SemaphoreType.DMA((NSEM,)),
            pltpu.SemaphoreType.DMA((NSEM,)),
            pltpu.SemaphoreType.DMA((8,)),
        ],
        compiler_params=pltpu.CompilerParams(
            collective_id=0, has_side_effects=True, vmem_limit_bytes=60 * 1024 * 1024
        ),
        name="block_backward",
    )(
        latents.reshape(NV, CH, D),
        cotangent.reshape(NV, CH, D),
        wqs.reshape(3 * LW, D),
        wos[None],
        wqv,
        wov[None],
        wqt,
        wot[None],
    )
    return out[None, None]


def solution(mesh):
    in_specs = (
        P("view", "tm", "space", None),
        P("view", "tm", "space", None),
        P(None, "space", None),
        P("space", None),
        P(None, "space", None),
        P("space", None),
        P(None, "space", None),
        P("space", None),
    )
    return jax.shard_map(
        on_device,
        mesh=mesh,
        in_specs=in_specs,
        out_specs=P("view", "tm", "space", None),
        check_vma=False,
    )
```

```python
import jax
import jax.numpy as jnp
from jax import lax
from jax.experimental import pallas as pl
from jax.experimental.pallas import tpu as pltpu
from jax.sharding import PartitionSpec as P

MESH = pl.DeviceIdType.MESH
BF = jnp.bfloat16
F32 = jnp.float32
NN = ((1,), (0,))
NT = ((1,), (1,))
TN = ((0,), (0,))

D = 768
TOK = 128
NSP = 4
NV = 8
NT_ = 8
CH = 16
HD = 64
LH = 3
LW = LH * HD
SCALE = HD**-0.5
NSEM = 208


def dot(a, b, dims):
    return lax.dot_general(a, b, (dims, ((), ())), preferred_element_type=F32)


def rms(values):
    factor = lax.rsqrt(jnp.mean(values * values, axis=-1, keepdims=True) + 1e-06)
    return values * factor, factor


def finish(upstream, earlier, normed_grad):
    normed, factor = rms(earlier.astype(F32))
    inner = jnp.mean(normed_grad * normed, axis=-1, keepdims=True)
    return (upstream.astype(F32) + factor * (normed_grad - normed * inner)).astype(BF)


def softmax0(scores):
    top = jnp.max(scores, axis=0, keepdims=True)
    expo = jnp.exp(scores - top)
    return expo * (1.0 / jnp.sum(expo, axis=0, keepdims=True))


def head_masks(rows):
    head = lax.broadcasted_iota(jnp.int32, (rows, TOK), 0) // HD
    return [(head == h).astype(F32).astype(BF) for h in range(rows // HD)]


def stacked(values, masks):
    return jnp.concatenate([values * m for m in masks], axis=1)


def per_head(left, right):
    heads = left.shape[0] // HD
    return jnp.concatenate(
        [
            dot(left[h * HD : (h + 1) * HD], right[:, h * TOK : (h + 1) * TOK], NN)
            for h in range(heads)
        ],
        axis=0,
    )


def body(
    x_in, cot_in, wqs_in, wos_in, wqv_in, wov_in, wqt_in, wot_in,
    out_ref,
    x_ref, cot_ref, wqs_ref,
    nb, k_nat, v_nat, qts, kvt, pts, gts, ogts, dqt, ats, att,
    xb, x2, xt, x3, c1, c2, ut, u2, uv, u3, ogs, og, rsend, rs, rf,
    bias, kt_v, vt_v, qts_v, pt_v,
    wos, wqv, wov, wqt, wot,
    send_sem, recv_sem, local_sem,
):
    t = lax.axis_index("tm")
    v = lax.axis_index("view")
    s = lax.axis_index("space")
    core = lax.rem(t, 2)
    sibling = t + 1 - 2 * core
    y = lax.rem(v, 4)
    half = lax.rem(y, 2)
    step = 1 - 2 * core
    y_next = v - y + lax.rem(y + step + 4, 4)
    s_next = lax.rem(s + step + 4, 4)
    s_prev = lax.rem(s - step + 4, 4)

    def plus(me, k, n):
        return lax.rem(me + k + n, n)

    bits = [t % 2, t // 2 % 2, t // 4]

    def paired(m):
        return t + sum((1 - 2 * bits[at]) * 2**at for at in range(3) if m >> at & 1)

    tm_order = (6, 7, 4, 5, 2, 3, 1)
    sent = []
    count = [0]

    def ticket():
        count[0] += 1
        return count[0] - 1

    def push(src, dst, axis, index, number):
        to = {axis: index} if isinstance(axis, str) else dict(zip(axis, index))
        copy = pltpu.make_async_remote_copy(
            src_ref=src,
            dst_ref=dst,
            send_sem=send_sem.at[number],
            recv_sem=recv_sem.at[number],
            device_id=to,
            device_id_type=MESH,
        )
        copy.start()
        sent.append(copy)

    def landed(dst, number, axis, index):
        to = {axis: index} if isinstance(axis, str) else dict(zip(axis, index))
        pltpu.make_async_remote_copy(
            src_ref=dst,
            dst_ref=dst,
            send_sem=send_sem.at[number],
            recv_sem=recv_sem.at[number],
            device_id=to,
            device_id_type=MESH,
        ).wait_recv()

    def rows(owner, c, h, size):
        return pl.ds(pl.multiple_of(owner * LW + c * 96 + h * 48, 16), size)

    class Gather:
        def __init__(self, shard, full, number):
            self.shard, self.full = shard, full
            self.x1 = [ticket(), ticket()]
            self.x2 = ticket()
            self.ys = [ticket() for _ in range(3)]
            self.sib = [ticket() for _ in range(3)]
            self.others = [plus(s, -1, 4), plus(s, 1, 4), plus(s, 2, 4)]
            self.own = pltpu.make_async_copy(
                shard, full.at[:, pl.ds(pl.multiple_of(s * LW, 16), LW), :], local_sem.at[number]
            )

        def piece(self, owner, c, h, size=48):
            return self.full.at[:, rows(owner, c, h, size), :]

        def a(self):
            self.own.start()
            mine = self.shard.at[:, pl.ds(pl.multiple_of(core * 96 + half * 48, 16), 48), :]
            there = self.piece(s, core, half)
            push(mine, there, "space", plus(s, 1, 4), self.x1[0])
            push(mine, there, "space", plus(s, -1, 4), self.x1[1])

        def b(self):
            for at in range(2):
                landed(self.piece(self.others[at], core, half), self.x1[at], "space", self.others[at])
            far = self.piece(s_prev, core, half)
            push(far, far, "space", s_next, self.x2)
            for at in range(2):
                part = self.piece(self.others[at], core, half)
                push(part, part, "view", y_next, self.ys[at])

        def c(self):
            part = self.piece(self.others[2], core, half)
            landed(part, self.x2, "space", s_prev)
            push(part, part, "view", y_next, self.ys[2])

        def d(self, which):
            for at in which:
                landed(self.piece(self.others[at], core, 1 - half), self.ys[at], "view", y_next)
                part = self.piece(self.others[at], core, 0, 96)
                push(part, part, "tm", sibling, self.sib[at])

        def ready(self, turn):
            if turn == 0:
                self.own.wait()
            else:
                at = turn - 1
                landed(self.piece(self.others[at], 1 - core, 0, 96), self.sib[at], "tm", sibling)

    NEAR, FAR = (0, 1), (2,)
    turns = [s, plus(s, -1, 4), plus(s, 1, 4), plus(s, 2, 4)]

    def group_rows(turn):
        return pl.ds(pl.multiple_of(turns[turn] * LW, 16), LW)

    g_os = Gather(wos_in, wos, 0)
    g_qv = Gather(wqv_in, wqv, 1)
    g_ov = Gather(wov_in, wov, 2)
    g_qt = Gather(wqt_in, wqt, 3)
    g_ot = Gather(wot_in, wot, 4)

    loads = [
        pltpu.make_async_copy(src, dst, local_sem.at[5 + at])
        for at, (src, dst) in enumerate(((x_in, x_ref), (wqs_in, wqs_ref), (cot_in, cot_ref)))
    ]
    for copy in loads:
        copy.start()

    barrier = pltpu.get_barrier_semaphore()
    for k in range(NSP):
        for j in range(NV):
            if k or j:
                pl.semaphore_signal(
                    barrier,
                    inc=1,
                    device_id={"view": plus(v, j, NV), "space": plus(s, k, NSP)},
                    device_id_type=MESH,
                )
    for k in range(1, NT_):
        pl.semaphore_signal(barrier, inc=1, device_id={"tm": plus(t, k, NT_)}, device_id_type=MESH)

    loads[0].wait()
    x_rows = x_ref[...].reshape(TOK, D)
    normed, _ = rms(x_rows.astype(F32))
    nb[0] = normed.astype(BF)
    key_at = lax.broadcasted_iota(jnp.int32, (TOK, LH * TOK), 0)
    query_at = lax.broadcasted_iota(jnp.int32, (TOK, LH * TOK), 1)
    bias[...] = jnp.where(lax.rem(key_at, CH) == lax.rem(query_at, CH), 0.0, -1e30)
    lmask = head_masks(LW)
    pl.semaphore_wait(barrier, NSP * NV + NT_ - 2)

    halves = [slice(0, TOK // 2), slice(TOK // 2, TOK)]
    n_num = [{k: ticket() for k in range(1, NSP)} for _ in halves]
    for h, part in enumerate(halves):
        for k in (1, 3):
            push(nb.at[0, part], nb.at[k, part], "space", plus(s, k, NSP), n_num[h][k])
    loads[1].wait()
    loads[2].wait()
    g_os.a()
    order = (4, 3, 5, 2, 6, 1, 7)
    x2_num = [ticket() for _ in range(NV)]
    c1_num = [ticket() for _ in range(NV)]
    for j in order:
        to = plus(v, j, NV)
        push(x_ref.at[to], xb.at[j], "view", to, x2_num[j])
    for j in order:
        to = plus(v, j, NV)
        push(cot_ref.at[to], c1.at[j], "view", to, c1_num[j])
    xb[0] = x_ref[v]
    c1[0] = cot_ref[v]

    def project_space(k):
        tokens = nb[k]
        packed = dot(wqs_ref[...], tokens, NT)
        at = slice(k * TOK, (k + 1) * TOK)
        query = packed[:LW].astype(BF) * jnp.asarray(SCALE, BF)
        qts[:, k * LH * TOK : (k + 1) * LH * TOK] = stacked(query, lmask)
        kvt[:, at] = packed[LW:].astype(BF)
        k_nat[at, :] = jnp.transpose(packed[LW : 2 * LW]).astype(BF)
        v_nat[at, :] = jnp.transpose(packed[2 * LW :]).astype(BF)

    project_space(0)
    for h, part in enumerate(halves):
        for k in (1, 3):
            landed(nb.at[k, part], n_num[h][k], "space", plus(s, -k, NSP))
        push(nb.at[1 + 2 * core, part], nb.at[2, part], "space", s_next, n_num[h][2])
    g_qv.a()
    project_space(1)
    project_space(3)
    g_os.b()
    for h, part in enumerate(halves):
        landed(nb.at[2, part], n_num[h][2], "space", plus(s, 2, NSP))
    project_space(2)

    a_num = [[ticket() for _ in range(NV)] for _ in range(NSP)]

    def attend_space(k):
        at = slice(k * LH * TOK, (k + 1) * LH * TOK)
        shares = softmax0(dot(k_nat[...], qts[:, at], NN)).astype(BF)
        pts[:, at] = shares
        out = jnp.transpose(per_head(kvt[LW:, :], shares)).astype(BF)
        ats[k] = out.reshape(NV, CH, LW)
        for j in order + (0,):
            to = (plus(v, j, NV), plus(s, -k, NSP))
            if k or j:
                push(ats.at[k, to[0]], att.at[s, j], ("view", "space"), to, a_num[k][j])
            else:
                att[pl.ds(s, 1), 0:1] = ats[0:1, pl.ds(v, 1)]

    attend_space(2)
    g_qv.b()
    g_os.c()
    g_ov.a()
    attend_space(1)
    g_ot.a()
    attend_space(3)
    g_qv.c()
    g_ov.b()
    g_qt.a()
    attend_space(0)
    g_os.d(NEAR)
    g_ov.c()
    g_ot.b()
    g_qv.d(NEAR)
    g_os.d(FAR)

    def slot_of(view):
        return lax.rem(v - view + NV, NV)

    for j in range(1, NV):
        landed(xb.at[j], x2_num[j], "view", plus(v, -j, NV))
    total = xb[...].reshape(TOK, D).astype(F32)
    for turn, k in enumerate((0, 3, 1, 2)):
        for j in range(NV):
            if k or j:
                frm = (plus(v, -j, NV), plus(s, k, NSP))
                landed(att.at[frm[1], j], a_num[k][j], ("view", "space"), frm)
    g_qv.d(FAR)
    c2_num = [ticket() for _ in range(NT_)]
    for k in range(1, NV):
        landed(c1.at[k], c1_num[k], "view", plus(v, -k, NV))
    for m in tm_order:
        push(c1.at[slot_of(paired(m))], c2.at[m], "tm", paired(m), c2_num[m])
    c2[0] = c1[slot_of(t)]
    g_ot.c()
    g_qt.b()
    for turn in range(NSP):
        g_os.ready(turn)
        total += dot(att[turns[turn]].reshape(TOK, LW), wos[0, group_rows(turn), :], NN)
    x2[...] = total.astype(BF).reshape(NV, CH, D)
    rows_view = x2[...].reshape(TOK, D)
    normed, _ = rms(rows_view.astype(F32))
    tokens = normed.astype(BF)
    g_ov.d(NEAR)

    def attend_small(w, turn):
        at = group_rows(turn)
        query = dot(w[0, at, :], tokens, NT).astype(BF) * jnp.asarray(SCALE, BF)
        key_t = dot(w[1, at, :], tokens, NT).astype(BF)
        value_t = dot(w[2, at, :], tokens, NT).astype(BF)
        queries = stacked(query, lmask)
        shares = softmax0(dot(key_t, queries, TN) + bias[...]).astype(BF)
        return queries, key_t, value_t, shares

    def backward_small(w, turn, queries, key_t, value_t, shares, out_grad):
        at = group_rows(turn)
        grads = stacked(out_grad, lmask)
        share_grad = dot(value_t, grads, TN)
        wide = shares.astype(F32)
        row_dot = jnp.sum(wide * share_grad, axis=0, keepdims=True)
        score_grad = (wide * (share_grad - row_dot)).astype(BF)
        query_grad = (per_head(key_t, score_grad) * SCALE).astype(BF)
        key_grad = dot(score_grad, queries, NT).astype(BF)
        value_grad = dot(shares, grads, NT).astype(BF)
        total = dot(query_grad, w[0, at, :], TN)
        total += dot(key_grad, w[1, at, :], NN)
        return total + dot(value_grad, w[2, at, :], NN)

    total = rows_view.astype(F32)
    for turn in range(NSP):
        g_qv.ready(turn)
        queries, key_t, value_t, shares = attend_small(wqv, turn)
        qts_v[turn], kt_v[turn], vt_v[turn], pt_v[turn] = queries, key_t, value_t, shares
        out = per_head(value_t, shares).astype(BF)
        g_ov.ready(turn)
        total += dot(out, wov[0, group_rows(turn), :], TN)
        if turn == 0:
            g_ov.d(FAR)
            g_ot.d(NEAR)
        if turn == 1:
            g_qt.c()
            g_ot.d(FAR)
        if turn == 2:
            g_qt.d(NEAR)
    xt[...] = total.astype(BF).reshape(NV, CH, D)

    x3_num = [ticket() for _ in range(NT_)]
    for m in tm_order:
        push(xt.at[slot_of(paired(m))], x3.at[m], "tm", paired(m), x3_num[m])
    x3[0] = xt[slot_of(t)]
    g_qt.d(FAR)
    for m in tm_order:
        landed(c2.at[m], c2_num[m], "tm", paired(m))
    upstream = c2[...].reshape(TOK, D)
    out_grads = []
    for turn in range(NSP):
        g_ot.ready(turn)
        out_grads.append(dot(wot[0, group_rows(turn), :], upstream, NT).astype(BF))
    for m in tm_order:
        landed(x3.at[m], x3_num[m], "tm", paired(m))
    rows_time = x3[...].reshape(TOK, D)
    normed, _ = rms(rows_time.astype(F32))
    tokens = normed.astype(BF)

    total = jnp.zeros((TOK, D), F32)
    for turn in range(NSP):
        g_qt.ready(turn)
        total += backward_small(wqt, turn, *attend_small(wqt, turn), out_grads[turn])
    ut[...] = finish(upstream, rows_time, total).reshape(NT_, CH, D)

    u2_num = [ticket() for _ in range(NT_)]
    here = slot_of(t)
    for m in tm_order:
        push(ut.at[m], u2.at[here], "tm", paired(m), u2_num[m])
    u2[pl.ds(here, 1)] = ut[0:1]
    for m in tm_order:
        landed(u2.at[slot_of(paired(m))], u2_num[m], "tm", paired(m))
    upstream = u2[...].reshape(TOK, D)
    total = jnp.zeros((TOK, D), F32)
    for turn in range(NSP):
        out_grad = dot(wov[0, group_rows(turn), :], upstream, NT).astype(BF)
        saved = (qts_v[turn], kt_v[turn], vt_v[turn], pt_v[turn])
        total += backward_small(wqv, turn, *saved, out_grad)
    upstream = finish(upstream, x2[...].reshape(TOK, D), total)
    uv[...] = upstream.reshape(NV, CH, D)

    out_grad = dot(wos[0], upstream, NT)
    for h in range(NSP):
        part = jnp.transpose(out_grad[h * LW : (h + 1) * LW]).astype(BF)
        ogs[h] = part.reshape(NV, CH, LW)
    og_num = [[ticket() for _ in range(NV)] for _ in range(NSP)]
    for k in (2, 1, 3, 0):
        for j in order + (0,):
            to = (plus(v, -j, NV), plus(s, k, NSP))
            if k or j:
                push(ogs.at[to[1], j], og.at[k, v], ("view", "space"), to, og_num[k][j])
    og[0:1, pl.ds(v, 1)] = ogs[pl.ds(s, 1), 0:1]
    def backward_space(k):
        at = slice(k * LH * TOK, (k + 1) * LH * TOK)
        out_grad = og[k].reshape(TOK, LW)
        grads = jnp.concatenate([out_grad * m for m in nmask], axis=0)
        ogts[at, :] = grads
        share_grad = dot(v_nat[...], grads, NT)
        wide = pts[:, at].astype(F32)
        row_dot = jnp.sum(wide * share_grad, axis=0, keepdims=True)
        score_grad = (wide * (share_grad - row_dot)).astype(BF)
        gts[:, at] = score_grad
        dqt[k] = (per_head(kvt[:LW, :], score_grad) * SCALE).astype(BF)

    head_at = lax.broadcasted_iota(jnp.int32, (TOK, LW), 1) // HD
    nmask = [(head_at == h).astype(F32).astype(BF) for h in range(LH)]
    u3_num = [ticket() for _ in range(NV)]
    for k in (0, 1, 3, 2):
        for j in range(NV):
            if k or j:
                frm = (plus(v, j, NV), plus(s, -k, NSP))
                landed(og.at[k, frm[0]], og_num[k][j], ("view", "space"), frm)
        if k == 2:
            for j in order:
                push(uv.at[j], u3.at[v], "view", plus(v, -j, NV), u3_num[j])
        backward_space(k)
    u3[pl.ds(v, 1)] = uv[0:1]

    def partial_sums(k):
        at = pl.ds(pl.multiple_of(k * TOK, TOK), TOK)
        key_grad = dot(gts[at, :], qts[...], NT).astype(BF)
        value_grad = dot(pts[at, :], ogts[...], NN).astype(BF)
        part = dot(dqt[k], wqs_ref[:LW, :], TN)
        part += dot(key_grad, wqs_ref[LW : 2 * LW, :], NN)
        return part + dot(value_grad, wqs_ref[2 * LW :, :], NN)

    rf_num, near_num, late_num = ticket(), ticket(), ticket()
    rsend[0] = partial_sums(2).astype(BF)
    push(rsend.at[0], rf, "space", s_next, rf_num)
    rsend[1] = partial_sums(1 + 2 * core).astype(BF)
    push(rsend.at[1], rs.at[0], "space", s_prev, near_num)
    late = partial_sums(3 - 2 * core)
    landed(rf, rf_num, "space", s_prev)
    rsend[2] = (late + rf[...].astype(F32)).astype(BF)
    push(rsend.at[2], rs.at[1], "space", s_next, late_num)
    total = partial_sums(0)
    landed(rs.at[0], near_num, "space", s_next)
    total += rs[0].astype(F32)
    landed(rs.at[1], late_num, "space", s_prev)
    total += rs[1].astype(F32)
    for j in range(1, NV):
        landed(u3.at[plus(v, j, NV)], u3_num[j], "view", plus(v, j, NV))
    out_ref[...] = finish(u3[...].reshape(TOK, D), x_ref[...].reshape(TOK, D), total)

    for copy in sent:
        copy.wait_send()


def on_device(latents, cotangent, wqs, wos, wqv, wov, wqt, wot):
    vmem = pl.BlockSpec(memory_space=pltpu.VMEM)
    hbm = pl.BlockSpec(memory_space=pltpu.HBM)

    def buf(*shape, dtype=BF):
        return pltpu.VMEM(shape, dtype)

    wide = NSP * LH * TOK
    out = pl.pallas_call(
        body,
        out_shape=jax.ShapeDtypeStruct((TOK, D), BF),
        in_specs=[hbm] * 8,
        out_specs=vmem,
        scratch_shapes=[
            buf(NV, CH, D),
            buf(NV, CH, D),
            buf(3 * LW, D),
            buf(NSP, TOK, D),
            buf(NSP * TOK, LW),
            buf(NSP * TOK, LW),
            buf(LW, wide),
            buf(2 * LW, NSP * TOK),
            buf(NSP * TOK, wide),
            buf(NSP * TOK, wide),
            buf(wide, LW),
            buf(NSP, LW, TOK),
            buf(NSP, NV, CH, LW),
            buf(NSP, NV, CH, LW),
        ]
        + [buf(NV, CH, D)] * 10
        + [
            buf(NSP, NV, CH, LW),
            buf(NSP, NV, CH, LW),
            buf(3, TOK, D),
            buf(2, TOK, D),
            buf(TOK, D),
            buf(TOK, LH * TOK, dtype=F32),
            buf(NSP, LW, TOK),
            buf(NSP, LW, TOK),
            buf(NSP, LW, LH * TOK),
            buf(NSP, TOK, LH * TOK),
            buf(1, D, D),
            buf(3, D, D),
            buf(1, D, D),
            buf(3, D, D),
            buf(1, D, D),
            pltpu.SemaphoreType.DMA((NSEM,)),
            pltpu.SemaphoreType.DMA((NSEM,)),
            pltpu.SemaphoreType.DMA((8,)),
        ],
        compiler_params=pltpu.CompilerParams(
            collective_id=0, has_side_effects=True, vmem_limit_bytes=60 * 1024 * 1024
        ),
        name="block_backward",
    )(
        latents.reshape(NV, CH, D),
        cotangent.reshape(NV, CH, D),
        wqs.reshape(3 * LW, D),
        wos[None],
        wqv,
        wov[None],
        wqt,
        wot[None],
    )
    return out[None, None]


def solution(mesh):
    in_specs = (
        P("view", "tm", "space", None),
        P("view", "tm", "space", None),
        P(None, "space", None),
        P("space", None),
        P(None, "space", None),
        P("space", None),
        P(None, "space", None),
        P("space", None),
    )
    return jax.shard_map(
        on_device,
        mesh=mesh,
        in_specs=in_specs,
        out_specs=P("view", "tm", "space", None),
        check_vma=False,
    )
```

```python
import jax
import jax.numpy as jnp
from jax import lax
from jax.experimental import pallas as pl
from jax.experimental.pallas import tpu as pltpu
from jax.sharding import PartitionSpec as P

MESH = pl.DeviceIdType.MESH
BF = jnp.bfloat16
F32 = jnp.float32
NN = ((1,), (0,))
NT = ((1,), (1,))
TN = ((0,), (0,))

D = 768
TOK = 128
NSP = 4
NV = 8
NT_ = 8
CH = 16
HD = 64
LH = 3
LW = LH * HD
GH = 4
GW = GH * HD
GROUPS = D // GW
SCALE = HD**-0.5
NSEM = 64


def dot(a, b, dims):
    return lax.dot_general(a, b, (dims, ((), ())), preferred_element_type=F32)


def rms(values):
    factor = lax.rsqrt(jnp.mean(values * values, axis=-1, keepdims=True) + 1e-06)
    return values * factor, factor


def finish(upstream, earlier, normed_grad):
    normed, factor = rms(earlier.astype(F32))
    inner = jnp.mean(normed_grad * normed, axis=-1, keepdims=True)
    return (upstream.astype(F32) + factor * (normed_grad - normed * inner)).astype(BF)


def softmax0(scores):
    top = jnp.max(scores, axis=0, keepdims=True)
    expo = jnp.exp(scores - top)
    return expo * (1.0 / jnp.sum(expo, axis=0, keepdims=True))


def head_masks(rows):
    head = lax.broadcasted_iota(jnp.int32, (rows, TOK), 0) // HD
    return [(head == h).astype(F32).astype(BF) for h in range(rows // HD)]


def stacked(values, masks):
    return jnp.concatenate([values * m for m in masks], axis=1)


def per_head(left, right):
    heads = left.shape[0] // HD
    return jnp.concatenate(
        [
            dot(left[h * HD : (h + 1) * HD], right[:, h * TOK : (h + 1) * TOK], NN)
            for h in range(heads)
        ],
        axis=0,
    )


def body(
    x_in, cot_in, wqs_in, wos_in, wqv_in, wov_in, wqt_in, wot_in,
    out_ref,
    xc, wqs_ref,
    nb, k_nat, v_nat, qts, kvt, pts, gts, ogts, dqt, ats, att,
    xb, x2, xt, x3, c2, ut, u2, uv, u3, ogs, og, rsend, rs, rf,
    bias, kt_v, vt_v, qts_v, pt_v,
    whole,
    send_sem, recv_sem, local_sem,
):
    t = lax.axis_index("tm")
    v = lax.axis_index("view")
    s = lax.axis_index("space")
    core = lax.rem(t, 2)
    sibling = t + 1 - 2 * core
    y = lax.rem(v, 4)
    half = lax.rem(y, 2)
    step = 1 - 2 * core
    y_next = v - y + lax.rem(y + step + 4, 4)
    s_next = lax.rem(s + step + 4, 4)
    s_prev = lax.rem(s - step + 4, 4)

    def plus(me, k, n):
        return lax.rem(me + k + n, n)

    bits = [t % 2, t // 2 % 2, t // 4]

    def paired(m):
        return t + sum((1 - 2 * bits[at]) * 2**at for at in range(3) if m >> at & 1)

    tm_order = (6, 7, 4, 5, 2, 3, 1)
    left = []
    count = [0]

    def ticket():
        count[0] += 1
        return count[0] - 1

    def remote(src, dst, axis, index, number, arrival):
        to = {axis: index} if isinstance(axis, str) else dict(zip(axis, index))
        return pltpu.make_async_remote_copy(
            src_ref=src,
            dst_ref=dst,
            send_sem=send_sem.at[number],
            recv_sem=recv_sem.at[arrival],
            device_id=to,
            device_id_type=MESH,
        )

    def push(src, dst, axis, index, number, arrival):
        remote(src, dst, axis, index, number, arrival).start()

    def landed(ref, arrival):
        remote(ref, ref, "tm", sibling, 0, arrival).wait_recv()

    def sending(ref):
        left.append((ref, ticket()))
        return left[-1][1]

    def rows(owner, c, h, size):
        return pl.ds(pl.multiple_of(owner * LW + c * 96 + h * 48, 16), size)

    class Gather:
        def __init__(self, first, end):
            self.first, self.end = first, end
            self.others = [plus(s, -1, 4), plus(s, 1, 4), plus(s, 2, 4)]
            self.out = [sending(self.bytes_of(size)) for size in (96, 48, 144, 288)]
            self.near, self.far, self.y_near, self.y_far, self.sib = [ticket() for _ in range(5)]

        def bytes_of(self, size):
            return whole.at[self.first : self.end, 0:size, :]

        def piece(self, owner, c, h, size=48):
            return whole.at[self.first : self.end, rows(owner, c, h, size), :]

        def a(self):
            mine = self.piece(s, core, half)
            push(mine, mine, "space", plus(s, 1, 4), self.out[0], self.near)
            push(mine, mine, "space", plus(s, -1, 4), self.out[0], self.near)

        def b(self):
            landed(self.bytes_of(96), self.near)
            far = self.piece(s_prev, core, half)
            push(far, far, "space", s_next, self.out[1], self.far)
            for at in range(2):
                part = self.piece(self.others[at], core, half)
                push(part, part, "view", y_next, self.out[2], self.y_near)

        def c(self):
            landed(self.bytes_of(48), self.far)
            part = self.piece(self.others[2], core, half)
            push(part, part, "view", y_next, self.out[2], self.y_far)

        def d(self):
            landed(self.bytes_of(96), self.y_near)
            for at in range(3):
                if at == 2:
                    landed(self.bytes_of(48), self.y_far)
                part = self.piece(self.others[at], core, 0, 96)
                push(part, part, "tm", sibling, self.out[3], self.sib)

        def e(self):
            landed(self.bytes_of(288), self.sib)

    g_a, g_b, g_c = Gather(0, 4), Gather(4, 6), Gather(6, 9)
    wos, wqv, wov = whole.at[0:1], whole.at[1:4], whole.at[4:5]
    wot, wqt = whole.at[5:6], whole.at[6:9]
    own = pl.ds(pl.multiple_of(s * LW, 16), LW)

    loads = [
        pltpu.make_async_copy(src, dst, local_sem.at[at])
        for at, (src, dst) in enumerate(
            (
                (x_in, xc.at[:, 0]),
                (wqs_in, wqs_ref),
                (cot_in, xc.at[:, 1]),
                (wos_in, wos.at[:, own, :]),
                (wqv_in, wqv.at[:, own, :]),
                (wov_in, wov.at[:, own, :]),
                (wot_in, wot.at[:, own, :]),
                (wqt_in, wqt.at[:, own, :]),
            )
        )
    ]
    for copy in loads:
        copy.start()

    barrier = pltpu.get_barrier_semaphore()
    for k in range(NSP):
        for j in range(NV):
            if k or j:
                pl.semaphore_signal(
                    barrier,
                    inc=1,
                    device_id={"view": plus(v, j, NV), "space": plus(s, k, NSP)},
                    device_id_type=MESH,
                )
    for k in range(1, NT_):
        pl.semaphore_signal(barrier, inc=1, device_id={"tm": plus(t, k, NT_)}, device_id_type=MESH)

    loads[0].wait()
    x_rows = xc[:, 0].reshape(TOK, D)
    normed, _ = rms(x_rows.astype(F32))
    nb[0] = normed.astype(BF)
    key_at = lax.broadcasted_iota(jnp.int32, (TOK, GH * TOK), 0)
    query_at = lax.broadcasted_iota(jnp.int32, (TOK, GH * TOK), 1)
    bias[...] = jnp.where(lax.rem(key_at, CH) == lax.rem(query_at, CH), 0.0, -1e30)
    lmask = head_masks(LW)
    gmask = head_masks(GW)
    pl.semaphore_wait(barrier, NSP * NV + NT_ - 2)

    halves = [slice(0, TOK // 2), slice(TOK // 2, TOK)]
    n_near, n_far = [ticket() for _ in halves], [ticket() for _ in halves]
    n_out = sending(nb.at[0:2]), sending(nb.at[0])
    for h, part in enumerate(halves):
        for k in (1, 3):
            push(nb.at[0, part], nb.at[k, part], "space", plus(s, k, NSP), n_out[0], n_near[h])
    for copy in loads[1:]:
        copy.wait()
    order = (4, 3, 5, 2, 6, 1, 7)
    x2_num, x2_out = ticket(), sending(xb.at[1:NV])
    for j in order:
        to = plus(v, j, NV)
        push(xc.at[to], xb.at[j], "view", to, x2_out, x2_num)
    xb[0] = xc[v]

    def project_space(k):
        tokens = nb[k]
        packed = dot(wqs_ref[...], tokens, NT)
        at = slice(k * TOK, (k + 1) * TOK)
        query = packed[:LW].astype(BF) * jnp.asarray(SCALE, BF)
        qts[:, k * LH * TOK : (k + 1) * LH * TOK] = stacked(query, lmask)
        kvt[:, at] = packed[LW:].astype(BF)
        k_nat[at, :] = jnp.transpose(packed[LW : 2 * LW]).astype(BF)
        v_nat[at, :] = jnp.transpose(packed[2 * LW :]).astype(BF)

    project_space(0)
    for h, part in enumerate(halves):
        landed(nb.at[0], n_near[h])
        push(nb.at[1 + 2 * core, part], nb.at[2, part], "space", s_next, n_out[1], n_far[h])
    g_a.a()
    project_space(1)
    project_space(3)
    for h, part in enumerate(halves):
        landed(nb.at[2, part], n_far[h])
    project_space(2)

    a_num = [ticket() for _ in range(NSP)]
    a_out = sending(ats.at[0, 1:NV]), sending(ats.at[1:NSP])

    def attend_space(k):
        at = slice(k * LH * TOK, (k + 1) * LH * TOK)
        shares = softmax0(dot(k_nat[...], qts[:, at], NN)).astype(BF)
        pts[:, at] = shares
        out = jnp.transpose(per_head(kvt[LW:, :], shares)).astype(BF)
        ats[k] = out.reshape(NV, CH, LW)
        for j in order + (0,):
            to = (plus(v, j, NV), plus(s, -k, NSP))
            if k or j:
                push(ats.at[k, to[0]], att.at[s, j], ("view", "space"), to, a_out[min(k, 1)], a_num[k])
            else:
                att[pl.ds(s, 1), 0:1] = ats[0:1, pl.ds(v, 1)]

    attend_space(2)
    g_a.b()
    g_b.a()
    attend_space(1)
    attend_space(3)
    g_a.c()
    g_b.b()
    g_c.a()
    attend_space(0)
    g_b.c()
    g_a.d()

    def slot_of(view):
        return lax.rem(v - view + NV, NV)

    g_b.d()
    landed(xb.at[1:NV], x2_num)
    for k in (2, 1, 3):
        landed(att.at[plus(s, k, NSP)], a_num[k])
    landed(att.at[s, 1:NV], a_num[0])
    c2_num, c2_out = ticket(), sending(c2.at[1:NT_])
    for m in tm_order:
        push(xb.at[slot_of(paired(m)), 1], c2.at[m], "tm", paired(m), c2_out, c2_num)
    c2[0] = xb[slot_of(t), 1]
    g_c.b()
    g_a.e()
    term = dot(att[0].reshape(TOK, LW), wos[0, :LW, :], NN)
    for h in range(1, NSP):
        term += dot(att[h].reshape(TOK, LW), wos[0, h * LW : (h + 1) * LW, :], NN)
    x2[...] = (xb[:, 0].reshape(TOK, D).astype(F32) + term).astype(BF).reshape(NV, CH, D)
    rows_view = x2[...].reshape(TOK, D)
    normed, _ = rms(rows_view.astype(F32))
    tokens = normed.astype(BF)

    def attend_small(w, g):
        lanes = slice(g * GW, (g + 1) * GW)
        query = dot(w[0, lanes, :], tokens, NT).astype(BF) * jnp.asarray(SCALE, BF)
        key_t = dot(w[1, lanes, :], tokens, NT).astype(BF)
        value_t = dot(w[2, lanes, :], tokens, NT).astype(BF)
        queries = stacked(query, gmask)
        shares = softmax0(dot(key_t, queries, TN) + bias[...]).astype(BF)
        return queries, key_t, value_t, shares

    def backward_small(w, g, queries, key_t, value_t, shares, out_grad):
        lanes = slice(g * GW, (g + 1) * GW)
        grads = stacked(out_grad, gmask)
        share_grad = dot(value_t, grads, TN)
        wide = shares.astype(F32)
        row_dot = jnp.sum(wide * share_grad, axis=0, keepdims=True)
        score_grad = (wide * (share_grad - row_dot)).astype(BF)
        query_grad = (per_head(key_t, score_grad) * SCALE).astype(BF)
        key_grad = dot(score_grad, queries, NT).astype(BF)
        value_grad = dot(shares, grads, NT).astype(BF)
        total = dot(query_grad, w[0, lanes, :], TN)
        total += dot(key_grad, w[1, lanes, :], NN)
        return total + dot(value_grad, w[2, lanes, :], NN)

    outs = []
    for g in range(GROUPS):
        queries, key_t, value_t, shares = attend_small(wqv, g)
        qts_v[g], kt_v[g], vt_v[g], pt_v[g] = queries, key_t, value_t, shares
        outs.append(per_head(value_t, shares).astype(BF))
        if g == 0:
            g_c.c()
    g_b.e()
    term = dot(jnp.concatenate(outs, axis=0), wov[0], TN)
    xt[...] = (rows_view.astype(F32) + term).astype(BF).reshape(NV, CH, D)

    x3_num, x3_out = ticket(), sending(x3.at[1:NT_])
    for m in tm_order:
        push(xt.at[slot_of(paired(m))], x3.at[m], "tm", paired(m), x3_out, x3_num)
    x3[0] = xt[slot_of(t)]
    g_c.d()
    landed(c2.at[1:NT_], c2_num)
    upstream = c2[...].reshape(TOK, D)
    out_grads = dot(wot[0], upstream, NT).astype(BF)
    landed(x3.at[1:NT_], x3_num)
    g_c.e()
    rows_time = x3[...].reshape(TOK, D)
    normed, _ = rms(rows_time.astype(F32))
    tokens = normed.astype(BF)

    total = jnp.zeros((TOK, D), F32)
    for g in range(GROUPS):
        queries, key_t, value_t, shares = attend_small(wqt, g)
        out_grad = out_grads[g * GW : (g + 1) * GW]
        total += backward_small(wqt, g, queries, key_t, value_t, shares, out_grad)
    ut[...] = finish(upstream, rows_time, total).reshape(NT_, CH, D)

    u2_num, u2_out = ticket(), sending(ut.at[1:NT_])
    here = slot_of(t)
    for m in tm_order:
        push(ut.at[m], u2.at[here], "tm", paired(m), u2_out, u2_num)
    u2[pl.ds(here, 1)] = ut[0:1]
    landed(u2.at[1:NT_], u2_num)
    upstream = u2[...].reshape(TOK, D)
    total = jnp.zeros((TOK, D), F32)
    for g in range(GROUPS):
        out_grad = dot(wov[0, g * GW : (g + 1) * GW, :], upstream, NT).astype(BF)
        total += backward_small(wqv, g, qts_v[g], kt_v[g], vt_v[g], pt_v[g], out_grad)
    upstream = finish(upstream, x2[...].reshape(TOK, D), total)
    uv[...] = upstream.reshape(NV, CH, D)

    out_grad = dot(wos[0], upstream, NT)
    for h in range(NSP):
        part = jnp.transpose(out_grad[h * LW : (h + 1) * LW]).astype(BF)
        ogs[h] = part.reshape(NV, CH, LW)
    og_num = [ticket() for _ in range(NSP)]
    og_out = sending(ogs.at[0, 1:NV]), sending(ogs.at[1:NSP])
    for k in (2, 1, 3, 0):
        for j in order + (0,):
            to = (plus(v, -j, NV), plus(s, k, NSP))
            if k or j:
                push(ogs.at[to[1], j], og.at[k, v], ("view", "space"), to, og_out[min(k, 1)], og_num[k])
    og[0:1, pl.ds(v, 1)] = ogs[pl.ds(s, 1), 0:1]
    def backward_space(k):
        at = slice(k * LH * TOK, (k + 1) * LH * TOK)
        out_grad = og[k].reshape(TOK, LW)
        grads = jnp.concatenate([out_grad * m for m in nmask], axis=0)
        ogts[at, :] = grads
        share_grad = dot(v_nat[...], grads, NT)
        wide = pts[:, at].astype(F32)
        row_dot = jnp.sum(wide * share_grad, axis=0, keepdims=True)
        score_grad = (wide * (share_grad - row_dot)).astype(BF)
        gts[:, at] = score_grad
        dqt[k] = (per_head(kvt[:LW, :], score_grad) * SCALE).astype(BF)

    head_at = lax.broadcasted_iota(jnp.int32, (TOK, LW), 1) // HD
    nmask = [(head_at == h).astype(F32).astype(BF) for h in range(LH)]
    u3_num, u3_out = ticket(), sending(uv.at[1:NV])
    for k in (0, 1, 3, 2):
        landed(og.at[k] if k else og.at[0, 1:NV], og_num[k])
        if k == 2:
            for j in order:
                push(uv.at[j], u3.at[v], "view", plus(v, -j, NV), u3_out, u3_num)
        backward_space(k)
    u3[pl.ds(v, 1)] = uv[0:1]

    def partial_sums(k):
        at = pl.ds(pl.multiple_of(k * TOK, TOK), TOK)
        key_grad = dot(gts[at, :], qts[...], NT).astype(BF)
        value_grad = dot(pts[at, :], ogts[...], NN).astype(BF)
        part = dot(dqt[k], wqs_ref[:LW, :], TN)
        part += dot(key_grad, wqs_ref[LW : 2 * LW, :], NN)
        return part + dot(value_grad, wqs_ref[2 * LW :, :], NN)

    rf_num, near_num, late_num = ticket(), ticket(), ticket()
    rs_out = sending(rsend)
    rsend[0] = partial_sums(2).astype(BF)
    push(rsend.at[0], rf, "space", s_next, rs_out, rf_num)
    rsend[1] = partial_sums(1 + 2 * core).astype(BF)
    push(rsend.at[1], rs.at[0], "space", s_prev, rs_out, near_num)
    late = partial_sums(3 - 2 * core)
    landed(rf, rf_num)
    rsend[2] = (late + rf[...].astype(F32)).astype(BF)
    push(rsend.at[2], rs.at[1], "space", s_next, rs_out, late_num)
    total = partial_sums(0)
    landed(rs.at[0], near_num)
    total += rs[0].astype(F32)
    landed(rs.at[1], late_num)
    total += rs[1].astype(F32)
    landed(u3.at[1:NV], u3_num)
    out_ref[...] = finish(u3[...].reshape(TOK, D), xc[:, 0].reshape(TOK, D), total)

    for ref, number in left:
        remote(ref, ref, "tm", sibling, number, 0).wait_send()


def on_device(latents, cotangent, wqs, wos, wqv, wov, wqt, wot):
    vmem = pl.BlockSpec(memory_space=pltpu.VMEM)
    hbm = pl.BlockSpec(memory_space=pltpu.HBM)

    def buf(*shape, dtype=BF):
        return pltpu.VMEM(shape, dtype)

    wide = NSP * LH * TOK
    out = pl.pallas_call(
        body,
        out_shape=jax.ShapeDtypeStruct((TOK, D), BF),
        in_specs=[hbm] * 8,
        out_specs=vmem,
        scratch_shapes=[
            buf(NV, 2, CH, D),
            buf(3 * LW, D),
            buf(NSP, TOK, D),
            buf(NSP * TOK, LW),
            buf(NSP * TOK, LW),
            buf(LW, wide),
            buf(2 * LW, NSP * TOK),
            buf(NSP * TOK, wide),
            buf(NSP * TOK, wide),
            buf(wide, LW),
            buf(NSP, LW, TOK),
            buf(NSP, NV, CH, LW),
            buf(NSP, NV, CH, LW),
        ]
        + [buf(NV, 2, CH, D)]
        + [buf(NV, CH, D)] * 8
        + [
            buf(NSP, NV, CH, LW),
            buf(NSP, NV, CH, LW),
            buf(3, TOK, D),
            buf(2, TOK, D),
            buf(TOK, D),
            buf(TOK, GH * TOK, dtype=F32),
            buf(GROUPS, GW, TOK),
            buf(GROUPS, GW, TOK),
            buf(GROUPS, GW, GH * TOK),
            buf(GROUPS, TOK, GH * TOK),
            buf(9, D, D),
            pltpu.SemaphoreType.DMA((NSEM,)),
            pltpu.SemaphoreType.DMA((NSEM,)),
            pltpu.SemaphoreType.DMA((8,)),
        ],
        compiler_params=pltpu.CompilerParams(
            collective_id=0, has_side_effects=True, vmem_limit_bytes=60 * 1024 * 1024
        ),
        name="block_backward",
    )(
        latents.reshape(NV, CH, D),
        cotangent.reshape(NV, CH, D),
        wqs.reshape(3 * LW, D),
        wos[None],
        wqv,
        wov[None],
        wqt,
        wot[None],
    )
    return out[None, None]


def solution(mesh):
    in_specs = (
        P("view", "tm", "space", None),
        P("view", "tm", "space", None),
        P(None, "space", None),
        P("space", None),
        P(None, "space", None),
        P("space", None),
        P(None, "space", None),
        P("space", None),
    )
    return jax.shard_map(
        on_device,
        mesh=mesh,
        in_specs=in_specs,
        out_specs=P("view", "tm", "space", None),
        check_vma=False,
    )
```

```python
import jax
import jax.numpy as jnp
from jax import lax
from jax.experimental import pallas as pl
from jax.experimental.pallas import tpu as pltpu
from jax.sharding import PartitionSpec as P

MESH = pl.DeviceIdType.MESH
BF = jnp.bfloat16
F32 = jnp.float32
NN = ((1,), (0,))
NT = ((1,), (1,))
TN = ((0,), (0,))

D = 768
TOK = 128
NSP = 4
NV = 8
NT_ = 8
CH = 16
HD = 64
LH = 3
LW = LH * HD
GH = 4
GW = GH * HD
GROUPS = D // GW
SCALE = HD**-0.5
NSEM = 64


def dot(a, b, dims):
    return lax.dot_general(a, b, (dims, ((), ())), preferred_element_type=F32)


def rms(values):
    factor = lax.rsqrt(jnp.mean(values * values, axis=-1, keepdims=True) + 1e-06)
    return values * factor, factor


def finish(upstream, earlier, normed_grad):
    normed, factor = rms(earlier.astype(F32))
    inner = jnp.mean(normed_grad * normed, axis=-1, keepdims=True)
    return (upstream.astype(F32) + factor * (normed_grad - normed * inner)).astype(BF)


def softmax0(scores):
    top = jnp.max(scores, axis=0, keepdims=True)
    expo = jnp.exp(scores - top)
    return expo * (1.0 / jnp.sum(expo, axis=0, keepdims=True))


def head_masks(rows):
    head = lax.broadcasted_iota(jnp.int32, (rows, TOK), 0) // HD
    return [(head == h).astype(F32).astype(BF) for h in range(rows // HD)]


def stacked(values, masks):
    return jnp.concatenate([values * m for m in masks], axis=1)


def per_head(left, right):
    heads = left.shape[0] // HD
    return jnp.concatenate(
        [
            dot(left[h * HD : (h + 1) * HD], right[:, h * TOK : (h + 1) * TOK], NN)
            for h in range(heads)
        ],
        axis=0,
    )


def body(
    x_in, cot_in, wqs_in, wos_in, wqv_in, wov_in, wqt_in, wot_in,
    out_ref,
    xc, wqs_ref,
    nb, k_nat, v_nat, qts, kvt, pts, gts, ogts, dqt, ats, att,
    xb, x2, xt, x3, c2, ut, u2, uv, u3, ogs, og, rsend, rs, rf,
    bias, kt_v, vt_v, qts_v, pt_v,
    whole,
    send_sem, recv_sem, local_sem,
):
    t = lax.axis_index("tm")
    v = lax.axis_index("view")
    s = lax.axis_index("space")
    core = lax.rem(t, 2)
    sibling = t + 1 - 2 * core
    y = lax.rem(v, 4)
    half = lax.rem(y, 2)
    step = 1 - 2 * core
    y_next = v - y + lax.rem(y + step + 4, 4)
    s_next = lax.rem(s + step + 4, 4)
    s_prev = lax.rem(s - step + 4, 4)

    def plus(me, k, n):
        return lax.rem(me + k + n, n)

    z_hi, z_lo = v // 4, t // 2
    even_odd = z_lo % 2
    pair_z, pair_y = 2 * z_hi + z_lo // 2, y // 2
    piece = 2 * pair_z + pair_y
    frame = 4 * half + 2 * even_odd + core
    apart = jnp.abs(half - z_lo // 2)

    def home(dz, dy):
        at_z, at_y = lax.rem(pair_z + dz, 4), lax.rem(pair_y + dy, 2)
        to_tm = 2 * (2 * (at_z % 2) + even_odd) + core
        to_view = 4 * (at_z // 2) + 2 * at_y + z_lo // 2
        return 2 * at_z + at_y, to_tm, to_view

    homes = ((2, 0), (2, 1), (1, 0), (3, 0), (1, 1), (3, 1), (0, 1), (0, 0))

    def member(m):
        flips = (1 - 2 * core) * (m & 1), (1 - 2 * even_odd) * (m >> 1 & 1), (1 - 2 * half) * (m >> 2)
        return (t + flips[0] + 2 * flips[1], v + flips[2]), frame + flips[0] + 2 * flips[1] + 4 * flips[2]

    members = (6, 7, 4, 5, 2, 3, 1)
    left = []
    count = [0]

    def ticket():
        count[0] += 1
        return count[0] - 1

    def remote(src, dst, axis, index, number, arrival):
        to = {axis: index} if isinstance(axis, str) else dict(zip(axis, index))
        return pltpu.make_async_remote_copy(
            src_ref=src,
            dst_ref=dst,
            send_sem=send_sem.at[number],
            recv_sem=recv_sem.at[arrival],
            device_id=to,
            device_id_type=MESH,
        )

    def push(src, dst, axis, index, number, arrival):
        remote(src, dst, axis, index, number, arrival).start()

    def landed(ref, arrival):
        remote(ref, ref, "tm", sibling, 0, arrival).wait_recv()

    def unless_alone(copies, here):
        pl.when(apart == 1)(copies)
        pl.when(apart == 0)(here)

    def landed_all(ref, arrival):
        unless_alone(lambda: landed(ref, arrival), lambda: landed(ref.at[1:], arrival))

    def sending(ref, eight=False):
        left.append((ref, ticket(), eight))
        return left[-1][1]

    def rows(owner, c, h, size):
        return pl.ds(pl.multiple_of(owner * LW + c * 96 + h * 48, 16), size)

    class Gather:
        def __init__(self, first, end):
            self.first, self.end = first, end
            self.others = [plus(s, -1, 4), plus(s, 1, 4), plus(s, 2, 4)]
            self.out = [sending(self.bytes_of(size)) for size in (96, 48, 144, 288)]
            self.near, self.far, self.y_near, self.y_far, self.sib = [ticket() for _ in range(5)]

        def bytes_of(self, size):
            return whole.at[self.first : self.end, 0:size, :]

        def piece(self, owner, c, h, size=48):
            return whole.at[self.first : self.end, rows(owner, c, h, size), :]

        def a(self):
            mine = self.piece(s, core, half)
            push(mine, mine, "space", plus(s, 1, 4), self.out[0], self.near)
            push(mine, mine, "space", plus(s, -1, 4), self.out[0], self.near)

        def b(self):
            landed(self.bytes_of(96), self.near)
            far = self.piece(s_prev, core, half)
            push(far, far, "space", s_next, self.out[1], self.far)
            for at in range(2):
                part = self.piece(self.others[at], core, half)
                push(part, part, "view", y_next, self.out[2], self.y_near)

        def c(self):
            landed(self.bytes_of(48), self.far)
            part = self.piece(self.others[2], core, half)
            push(part, part, "view", y_next, self.out[2], self.y_far)

        def d(self):
            landed(self.bytes_of(96), self.y_near)
            for at in range(3):
                if at == 2:
                    landed(self.bytes_of(48), self.y_far)
                part = self.piece(self.others[at], core, 0, 96)
                push(part, part, "tm", sibling, self.out[3], self.sib)

        def e(self):
            landed(self.bytes_of(288), self.sib)

    g_a, g_b, g_c = Gather(0, 4), Gather(4, 6), Gather(6, 9)
    wos, wqv, wov = whole.at[0:1], whole.at[1:4], whole.at[4:5]
    wot, wqt = whole.at[5:6], whole.at[6:9]
    own = pl.ds(pl.multiple_of(s * LW, 16), LW)

    loads = [
        pltpu.make_async_copy(src, dst, local_sem.at[at])
        for at, (src, dst) in enumerate(
            (
                (x_in, xc.at[:, 0]),
                (wqs_in, wqs_ref),
                (cot_in, xc.at[:, 1]),
                (wos_in, wos.at[:, own, :]),
                (wqv_in, wqv.at[:, own, :]),
                (wov_in, wov.at[:, own, :]),
                (wot_in, wot.at[:, own, :]),
                (wqt_in, wqt.at[:, own, :]),
            )
        )
    ]
    for copy in loads:
        copy.start()

    barrier = pltpu.get_barrier_semaphore()
    def greet(**to):
        pl.semaphore_signal(barrier, inc=1, device_id=to, device_id_type=MESH)

    for k in range(NSP):
        for j in range(NV):
            if k or j:
                greet(tm=frame, view=plus(v, j, NV), space=plus(s, k, NSP))

    @pl.when(apart == 1)
    def _():
        greet(tm=frame, view=v)

    for m in members:
        to = member(m)[0]
        greet(tm=to[0], view=to[1])
    greet(space=plus(s, 1, NSP))
    greet(space=plus(s, -1, NSP))
    greet(view=v - y + lax.rem(y - step + 4, 4))
    loads[0].wait()
    x_rows = xc[:, 0].reshape(TOK, D)
    normed, _ = rms(x_rows.astype(F32))
    nb[0] = normed.astype(BF)
    key_at = lax.broadcasted_iota(jnp.int32, (TOK, GH * TOK), 0)
    query_at = lax.broadcasted_iota(jnp.int32, (TOK, GH * TOK), 1)
    bias[...] = jnp.where(lax.rem(key_at, CH) == lax.rem(query_at, CH), 0.0, -1e30)
    lmask = head_masks(LW)
    gmask = head_masks(GW)
    pl.semaphore_wait(barrier, NSP * NV - 1 + NT_ - 1 + 3 + apart)

    halves = [slice(0, TOK // 2), slice(TOK // 2, TOK)]
    n_near, n_far = [ticket() for _ in halves], [ticket() for _ in halves]
    n_out = sending(nb.at[0:2]), sending(nb.at[0])
    for h, part in enumerate(halves):
        for k in (1, 3):
            push(nb.at[0, part], nb.at[k, part], "space", plus(s, k, NSP), n_out[0], n_near[h])
    for copy in loads[1:]:
        copy.wait()
    order = (4, 3, 5, 2, 6, 1, 7)
    x2_num, x2_out = ticket(), sending(xb, True)

    def send_tokens(dz, dy):
        place, *to = home(dz, dy)
        push(xc.at[place], xb.at[v], ("tm", "view"), to, x2_out, x2_num)

    for dz, dy in homes[:-1]:
        send_tokens(dz, dy)

    def keep_tokens():
        xb[pl.ds(v, 1)] = xc[pl.ds(piece, 1)]

    unless_alone(lambda: send_tokens(0, 0), keep_tokens)

    def project_space(k):
        tokens = nb[k]
        packed = dot(wqs_ref[...], tokens, NT)
        at = slice(k * TOK, (k + 1) * TOK)
        query = packed[:LW].astype(BF) * jnp.asarray(SCALE, BF)
        qts[:, k * LH * TOK : (k + 1) * LH * TOK] = stacked(query, lmask)
        kvt[:, at] = packed[LW:].astype(BF)
        k_nat[at, :] = jnp.transpose(packed[LW : 2 * LW]).astype(BF)
        v_nat[at, :] = jnp.transpose(packed[2 * LW :]).astype(BF)

    project_space(0)
    for h, part in enumerate(halves):
        landed(nb.at[0], n_near[h])
        push(nb.at[1 + 2 * core, part], nb.at[2, part], "space", s_next, n_out[1], n_far[h])
    g_a.a()
    project_space(1)
    project_space(3)
    for h, part in enumerate(halves):
        landed(nb.at[2, part], n_far[h])
    project_space(2)

    a_num = [ticket() for _ in range(NSP)]
    a_out = sending(ats.at[0], True), sending(ats.at[1:NSP])

    def attend_space(k):
        at = slice(k * LH * TOK, (k + 1) * LH * TOK)
        shares = softmax0(dot(k_nat[...], qts[:, at], NN)).astype(BF)
        pts[:, at] = shares
        out = jnp.transpose(per_head(kvt[LW:, :], shares)).astype(BF)
        ats[k] = out.reshape(NV, CH, LW)

        def send(dz, dy):
            place, *to = home(dz, dy)
            to.append(plus(s, -k, NSP))
            push(ats.at[k, place], att.at[s, v], ("tm", "view", "space"), to, a_out[min(k, 1)], a_num[k])

        for dz, dy in homes[:-1]:
            send(dz, dy)
        if k:
            send(0, 0)
        else:

            def keep():
                att[pl.ds(s, 1), pl.ds(v, 1)] = ats[0:1, pl.ds(piece, 1)]

            unless_alone(lambda: send(0, 0), keep)

    attend_space(2)
    g_a.b()
    g_b.a()
    attend_space(1)
    attend_space(3)
    g_a.c()
    g_b.b()
    g_c.a()
    attend_space(0)
    g_b.c()
    g_a.d()

    g_b.d()
    landed_all(xb, x2_num)
    for k in (2, 1, 3):
        landed(att.at[plus(s, k, NSP)], a_num[k])
    landed_all(att.at[s], a_num[0])
    c2_num, c2_out = ticket(), sending(c2.at[1:NT_])
    for m in members:
        to, its_frame = member(m)
        push(xb.at[its_frame, 1], c2.at[m], ("tm", "view"), to, c2_out, c2_num)
    c2[0] = xb[frame, 1]
    g_c.b()
    g_a.e()
    term = dot(att[0].reshape(TOK, LW), wos[0, :LW, :], NN)
    for h in range(1, NSP):
        term += dot(att[h].reshape(TOK, LW), wos[0, h * LW : (h + 1) * LW, :], NN)
    x2[...] = (xb[:, 0].reshape(TOK, D).astype(F32) + term).astype(BF).reshape(NV, CH, D)
    rows_view = x2[...].reshape(TOK, D)
    normed, _ = rms(rows_view.astype(F32))
    tokens = normed.astype(BF)

    def attend_small(w, g):
        lanes = slice(g * GW, (g + 1) * GW)
        query = dot(w[0, lanes, :], tokens, NT).astype(BF) * jnp.asarray(SCALE, BF)
        key_t = dot(w[1, lanes, :], tokens, NT).astype(BF)
        value_t = dot(w[2, lanes, :], tokens, NT).astype(BF)
        queries = stacked(query, gmask)
        shares = softmax0(dot(key_t, queries, TN) + bias[...]).astype(BF)
        return queries, key_t, value_t, shares

    def backward_small(w, g, queries, key_t, value_t, shares, out_grad):
        lanes = slice(g * GW, (g + 1) * GW)
        grads = stacked(out_grad, gmask)
        share_grad = dot(value_t, grads, TN)
        wide = shares.astype(F32)
        row_dot = jnp.sum(wide * share_grad, axis=0, keepdims=True)
        score_grad = (wide * (share_grad - row_dot)).astype(BF)
        query_grad = (per_head(key_t, score_grad) * SCALE).astype(BF)
        key_grad = dot(score_grad, queries, NT).astype(BF)
        value_grad = dot(shares, grads, NT).astype(BF)
        total = dot(query_grad, w[0, lanes, :], TN)
        total += dot(key_grad, w[1, lanes, :], NN)
        return total + dot(value_grad, w[2, lanes, :], NN)

    outs = []
    for g in range(GROUPS):
        queries, key_t, value_t, shares = attend_small(wqv, g)
        qts_v[g], kt_v[g], vt_v[g], pt_v[g] = queries, key_t, value_t, shares
        outs.append(per_head(value_t, shares).astype(BF))
        if g == 0:
            g_c.c()
    g_b.e()
    term = dot(jnp.concatenate(outs, axis=0), wov[0], TN)
    xt[...] = (rows_view.astype(F32) + term).astype(BF).reshape(NV, CH, D)

    x3_num, x3_out = ticket(), sending(x3.at[1:NT_])
    for m in members:
        to, its_frame = member(m)
        push(xt.at[its_frame], x3.at[m], ("tm", "view"), to, x3_out, x3_num)
    x3[0] = xt[frame]
    g_c.d()
    landed(c2.at[1:NT_], c2_num)
    upstream = c2[...].reshape(TOK, D)
    out_grads = dot(wot[0], upstream, NT).astype(BF)
    landed(x3.at[1:NT_], x3_num)
    g_c.e()
    rows_time = x3[...].reshape(TOK, D)
    normed, _ = rms(rows_time.astype(F32))
    tokens = normed.astype(BF)

    total = jnp.zeros((TOK, D), F32)
    for g in range(GROUPS):
        queries, key_t, value_t, shares = attend_small(wqt, g)
        out_grad = out_grads[g * GW : (g + 1) * GW]
        total += backward_small(wqt, g, queries, key_t, value_t, shares, out_grad)
    ut[...] = finish(upstream, rows_time, total).reshape(NT_, CH, D)

    u2_num, u2_out = ticket(), sending(ut.at[1:NT_])
    for m in members:
        push(ut.at[m], u2.at[frame], ("tm", "view"), member(m)[0], u2_out, u2_num)
    u2[pl.ds(frame, 1)] = ut[0:1]
    landed(u2.at[1:NT_], u2_num)
    upstream = u2[...].reshape(TOK, D)
    total = jnp.zeros((TOK, D), F32)
    for g in range(GROUPS):
        out_grad = dot(wov[0, g * GW : (g + 1) * GW, :], upstream, NT).astype(BF)
        total += backward_small(wqv, g, qts_v[g], kt_v[g], vt_v[g], pt_v[g], out_grad)
    upstream = finish(upstream, x2[...].reshape(TOK, D), total)
    uv[...] = upstream.reshape(NV, CH, D)

    out_grad = dot(wos[0], upstream, NT)
    for h in range(NSP):
        part = jnp.transpose(out_grad[h * LW : (h + 1) * LW]).astype(BF)
        ogs[h] = part.reshape(NV, CH, LW)
    og_num = [ticket() for _ in range(NSP)]
    og_out = sending(ogs.at[0], True), sending(ogs.at[1:NSP])
    def send_out_grad(k, j):
        to = (frame, plus(v, j, NV), plus(s, k, NSP))
        numbers = og_out[min(k, 1)], og_num[k]
        push(ogs.at[to[2], to[1]], og.at[k, piece], ("tm", "view", "space"), to, *numbers)

    def keep_out_grad():
        og[0:1, pl.ds(piece, 1)] = ogs[pl.ds(s, 1), pl.ds(v, 1)]

    for k in (2, 1, 3, 0):
        for j in order:
            send_out_grad(k, j)
        if k:
            send_out_grad(k, 0)
    unless_alone(lambda: send_out_grad(0, 0), keep_out_grad)

    def backward_space(k):
        at = slice(k * LH * TOK, (k + 1) * LH * TOK)
        out_grad = og[k].reshape(TOK, LW)
        grads = jnp.concatenate([out_grad * m for m in nmask], axis=0)
        ogts[at, :] = grads
        share_grad = dot(v_nat[...], grads, NT)
        wide = pts[:, at].astype(F32)
        row_dot = jnp.sum(wide * share_grad, axis=0, keepdims=True)
        score_grad = (wide * (share_grad - row_dot)).astype(BF)
        gts[:, at] = score_grad
        dqt[k] = (per_head(kvt[:LW, :], score_grad) * SCALE).astype(BF)

    head_at = lax.broadcasted_iota(jnp.int32, (TOK, LW), 1) // HD
    nmask = [(head_at == h).astype(F32).astype(BF) for h in range(LH)]
    u3_num, u3_out = ticket(), sending(uv, True)

    def send_upstream(j):
        to = (frame, plus(v, j, NV))
        push(uv.at[to[1]], u3.at[piece], ("tm", "view"), to, u3_out, u3_num)

    def keep_upstream():
        u3[pl.ds(piece, 1)] = uv[pl.ds(v, 1)]

    for k in (0, 1, 3, 2):
        if k:
            landed(og.at[k], og_num[k])
        else:
            landed_all(og.at[0], og_num[0])
        if k == 2:
            for j in order:
                send_upstream(j)
            unless_alone(lambda: send_upstream(0), keep_upstream)
        backward_space(k)

    def partial_sums(k):
        at = pl.ds(pl.multiple_of(k * TOK, TOK), TOK)
        key_grad = dot(gts[at, :], qts[...], NT).astype(BF)
        value_grad = dot(pts[at, :], ogts[...], NN).astype(BF)
        part = dot(dqt[k], wqs_ref[:LW, :], TN)
        part += dot(key_grad, wqs_ref[LW : 2 * LW, :], NN)
        return part + dot(value_grad, wqs_ref[2 * LW :, :], NN)

    rf_num, near_num, late_num = ticket(), ticket(), ticket()
    rs_out = sending(rsend)
    rsend[0] = partial_sums(2).astype(BF)
    push(rsend.at[0], rf, "space", s_next, rs_out, rf_num)
    rsend[1] = partial_sums(1 + 2 * core).astype(BF)
    push(rsend.at[1], rs.at[0], "space", s_prev, rs_out, near_num)
    late = partial_sums(3 - 2 * core)
    landed(rf, rf_num)
    rsend[2] = (late + rf[...].astype(F32)).astype(BF)
    push(rsend.at[2], rs.at[1], "space", s_next, rs_out, late_num)
    total = partial_sums(0)
    landed(rs.at[0], near_num)
    total += rs[0].astype(F32)
    landed(rs.at[1], late_num)
    total += rs[1].astype(F32)
    landed_all(u3, u3_num)
    out_ref[...] = finish(u3[...].reshape(TOK, D), xc[:, 0].reshape(TOK, D), total)

    def gone(ref, number):
        remote(ref, ref, "tm", sibling, number, 0).wait_send()

    for ref, number, eight in left:
        if eight:
            unless_alone(
                lambda ref=ref, number=number: gone(ref, number),
                lambda ref=ref, number=number: gone(ref.at[1:], number),
            )
        else:
            gone(ref, number)


def on_device(latents, cotangent, wqs, wos, wqv, wov, wqt, wot):
    vmem = pl.BlockSpec(memory_space=pltpu.VMEM)
    hbm = pl.BlockSpec(memory_space=pltpu.HBM)

    def buf(*shape, dtype=BF):
        return pltpu.VMEM(shape, dtype)

    wide = NSP * LH * TOK
    out = pl.pallas_call(
        body,
        out_shape=jax.ShapeDtypeStruct((TOK, D), BF),
        in_specs=[hbm] * 8,
        out_specs=vmem,
        scratch_shapes=[
            buf(NV, 2, CH, D),
            buf(3 * LW, D),
            buf(NSP, TOK, D),
            buf(NSP * TOK, LW),
            buf(NSP * TOK, LW),
            buf(LW, wide),
            buf(2 * LW, NSP * TOK),
            buf(NSP * TOK, wide),
            buf(NSP * TOK, wide),
            buf(wide, LW),
            buf(NSP, LW, TOK),
            buf(NSP, NV, CH, LW),
            buf(NSP, NV, CH, LW),
        ]
        + [buf(NV, 2, CH, D)]
        + [buf(NV, CH, D)] * 8
        + [
            buf(NSP, NV, CH, LW),
            buf(NSP, NV, CH, LW),
            buf(3, TOK, D),
            buf(2, TOK, D),
            buf(TOK, D),
            buf(TOK, GH * TOK, dtype=F32),
            buf(GROUPS, GW, TOK),
            buf(GROUPS, GW, TOK),
            buf(GROUPS, GW, GH * TOK),
            buf(GROUPS, TOK, GH * TOK),
            buf(9, D, D),
            pltpu.SemaphoreType.DMA((NSEM,)),
            pltpu.SemaphoreType.DMA((NSEM,)),
            pltpu.SemaphoreType.DMA((8,)),
        ],
        compiler_params=pltpu.CompilerParams(
            collective_id=0, has_side_effects=True, vmem_limit_bytes=60 * 1024 * 1024
        ),
        name="block_backward",
    )(
        latents.reshape(NV, CH, D),
        cotangent.reshape(NV, CH, D),
        wqs.reshape(3 * LW, D),
        wos[None],
        wqv,
        wov[None],
        wqt,
        wot[None],
    )
    return out[None, None]


def solution(mesh):
    in_specs = (
        P("view", "tm", "space", None),
        P("view", "tm", "space", None),
        P(None, "space", None),
        P("space", None),
        P(None, "space", None),
        P("space", None),
        P(None, "space", None),
        P("space", None),
    )
    return jax.shard_map(
        on_device,
        mesh=mesh,
        in_specs=in_specs,
        out_specs=P("view", "tm", "space", None),
        check_vma=False,
    )
```

```python
import jax
import jax.numpy as jnp
from jax import lax
from jax.experimental import pallas as pl
from jax.experimental.pallas import tpu as pltpu
from jax.sharding import PartitionSpec as P

MESH = pl.DeviceIdType.MESH
BF = jnp.bfloat16
F32 = jnp.float32
NN = ((1,), (0,))
NT = ((1,), (1,))
TN = ((0,), (0,))

D = 768
TOK = 128
NSP = 4
NV = 8
NT_ = 8
CH = 16
HD = 64
LH = 3
LW = LH * HD
GH = 4
GW = GH * HD
GROUPS = D // GW
SCALE = HD**-0.5
NSEM = 64


def dot(a, b, dims):
    return lax.dot_general(a, b, (dims, ((), ())), preferred_element_type=F32)


def rms(values):
    factor = lax.rsqrt(jnp.mean(values * values, axis=-1, keepdims=True) + 1e-06)
    return values * factor, factor


def finish(upstream, earlier, normed_grad):
    normed, factor = rms(earlier.astype(F32))
    inner = jnp.mean(normed_grad * normed, axis=-1, keepdims=True)
    return (upstream.astype(F32) + factor * (normed_grad - normed * inner)).astype(BF)


def softmax0(scores):
    top = jnp.max(scores, axis=0, keepdims=True)
    expo = jnp.exp(scores - top)
    return expo * (1.0 / jnp.sum(expo, axis=0, keepdims=True))


def head_masks(rows):
    head = lax.broadcasted_iota(jnp.int32, (rows, TOK), 0) // HD
    return [(head == h).astype(F32).astype(BF) for h in range(rows // HD)]


def stacked(values, masks):
    return jnp.concatenate([values * m for m in masks], axis=1)


def per_head(left, right):
    heads = left.shape[0] // HD
    return jnp.concatenate(
        [
            dot(left[h * HD : (h + 1) * HD], right[:, h * TOK : (h + 1) * TOK], NN)
            for h in range(heads)
        ],
        axis=0,
    )


def body(
    x_in, cot_in, wqs_in, wos_in, wqv_in, wov_in, wqt_in, wot_in,
    out_ref,
    xc, wqs_ref,
    nb, k_nat, v_nat, qts, kvt, pts, gts, ogts, dqt, ats, att,
    xb, x2, xt, x3, c2, ut, u2, uv, u3, ogs, og, rsend, rs, rf,
    bias, kt_v, vt_v, qts_v, pt_v,
    whole,
    send_sem, recv_sem, local_sem,
):
    t = lax.axis_index("tm")
    v = lax.axis_index("view")
    s = lax.axis_index("space")
    core = lax.rem(t, 2)
    sibling = t + 1 - 2 * core
    y = lax.rem(v, 4)
    half = lax.rem(y, 2)
    step = 1 - 2 * core
    y_next = v - y + lax.rem(y + step + 4, 4)
    s_next = lax.rem(s + step + 4, 4)
    s_prev = lax.rem(s - step + 4, 4)

    def plus(me, k, n):
        return lax.rem(me + k + n, n)

    bits = [t % 2, t // 2 % 2, t // 4]

    def paired(m):
        return t + sum((1 - 2 * bits[at]) * 2**at for at in range(3) if m >> at & 1)

    tm_order = (6, 7, 4, 5, 2, 3, 1)
    left = []
    count = [0]

    def ticket():
        count[0] += 1
        return count[0] - 1

    def remote(src, dst, axis, index, number, arrival):
        to = {axis: index} if isinstance(axis, str) else dict(zip(axis, index))
        return pltpu.make_async_remote_copy(
            src_ref=src,
            dst_ref=dst,
            send_sem=send_sem.at[number],
            recv_sem=recv_sem.at[arrival],
            device_id=to,
            device_id_type=MESH,
        )

    def push(src, dst, axis, index, number, arrival):
        remote(src, dst, axis, index, number, arrival).start()

    def landed(ref, arrival):
        remote(ref, ref, "tm", sibling, 0, arrival).wait_recv()

    def sending(ref):
        left.append((ref, ticket()))
        return left[-1][1]

    def rows(owner, c, h, size):
        return pl.ds(pl.multiple_of(owner * LW + c * 96 + h * 48, 16), size)

    class Gather:
        def __init__(self, first, end):
            self.first, self.end = first, end
            self.others = [plus(s, -1, 4), plus(s, 1, 4), plus(s, 2, 4)]
            self.out = [sending(self.bytes_of(size)) for size in (96, 48, 144, 288)]
            self.near, self.far, self.y_near, self.y_far, self.sib = [ticket() for _ in range(5)]

        def bytes_of(self, size):
            return whole.at[self.first : self.end, 0:size, :]

        def piece(self, owner, c, h, size=48):
            return whole.at[self.first : self.end, rows(owner, c, h, size), :]

        def a(self):
            mine = self.piece(s, core, half)
            push(mine, mine, "space", plus(s, 1, 4), self.out[0], self.near)
            push(mine, mine, "space", plus(s, -1, 4), self.out[0], self.near)

        def b(self):
            landed(self.bytes_of(96), self.near)
            far = self.piece(s_prev, core, half)
            push(far, far, "space", s_next, self.out[1], self.far)
            for at in range(2):
                part = self.piece(self.others[at], core, half)
                push(part, part, "view", y_next, self.out[2], self.y_near)

        def c(self):
            landed(self.bytes_of(48), self.far)
            part = self.piece(self.others[2], core, half)
            push(part, part, "view", y_next, self.out[2], self.y_far)

        def d(self):
            landed(self.bytes_of(96), self.y_near)
            for at in range(3):
                if at == 2:
                    landed(self.bytes_of(48), self.y_far)
                part = self.piece(self.others[at], core, 0, 96)
                push(part, part, "tm", sibling, self.out[3], self.sib)

        def e(self):
            landed(self.bytes_of(288), self.sib)

    g_a, g_b, g_c = Gather(0, 4), Gather(4, 6), Gather(6, 9)
    wos, wqv, wov = whole.at[0:1], whole.at[1:4], whole.at[4:5]
    wot, wqt = whole.at[5:6], whole.at[6:9]
    own = pl.ds(pl.multiple_of(s * LW, 16), LW)

    loads = [
        pltpu.make_async_copy(src, dst, local_sem.at[at])
        for at, (src, dst) in enumerate(
            (
                (x_in, xc.at[:, 0]),
                (wqs_in, wqs_ref),
                (cot_in, xc.at[:, 1]),
                (wos_in, wos.at[:, own, :]),
                (wqv_in, wqv.at[:, own, :]),
                (wov_in, wov.at[:, own, :]),
                (wot_in, wot.at[:, own, :]),
                (wqt_in, wqt.at[:, own, :]),
            )
        )
    ]
    for copy in loads:
        copy.start()

    barrier = pltpu.get_barrier_semaphore()
    for k in range(NSP):
        for j in range(NV):
            if k or j:
                pl.semaphore_signal(
                    barrier,
                    inc=1,
                    device_id={"view": plus(v, j, NV), "space": plus(s, k, NSP)},
                    device_id_type=MESH,
                )
    for k in range(1, NT_):
        pl.semaphore_signal(barrier, inc=1, device_id={"tm": plus(t, k, NT_)}, device_id_type=MESH)

    loads[0].wait()
    x_rows = xc[:, 0].reshape(TOK, D)
    normed, _ = rms(x_rows.astype(F32))
    nb[0] = normed.astype(BF)
    key_at = lax.broadcasted_iota(jnp.int32, (TOK, GH * TOK), 0)
    query_at = lax.broadcasted_iota(jnp.int32, (TOK, GH * TOK), 1)
    bias[...] = jnp.where(lax.rem(key_at, CH) == lax.rem(query_at, CH), 0.0, -1e30)
    lmask = head_masks(LW)
    gmask = head_masks(GW)
    pl.semaphore_wait(barrier, NSP * NV + NT_ - 2)

    halves = [slice(0, TOK // 2), slice(TOK // 2, TOK)]
    n_near, n_far = [ticket() for _ in halves], [ticket() for _ in halves]
    n_out = sending(nb.at[0:2]), sending(nb.at[0])
    for h, part in enumerate(halves):
        for k in (1, 3):
            push(nb.at[0, part], nb.at[k, part], "space", plus(s, k, NSP), n_out[0], n_near[h])
    for copy in loads[1:]:
        copy.wait()
    order = (4, 3, 5, 2, 6, 1, 7)
    x2_num, x2_out = ticket(), sending(xb.at[1:NV])
    for j in order:
        to = plus(v, j, NV)
        push(xc.at[to], xb.at[j], "view", to, x2_out, x2_num)
    xb[0] = xc[v]

    def project_space(k):
        tokens = nb[k]
        packed = dot(wqs_ref[...], tokens, NT)
        at = slice(k * TOK, (k + 1) * TOK)
        query = packed[:LW].astype(BF) * jnp.asarray(SCALE, BF)
        qts[:, k * LH * TOK : (k + 1) * LH * TOK] = stacked(query, lmask)
        kvt[:, at] = packed[LW:].astype(BF)
        k_nat[at, :] = jnp.transpose(packed[LW : 2 * LW]).astype(BF)
        v_nat[at, :] = jnp.transpose(packed[2 * LW :]).astype(BF)

    project_space(0)
    for h, part in enumerate(halves):
        landed(nb.at[0], n_near[h])
        push(nb.at[1 + 2 * core, part], nb.at[2, part], "space", s_next, n_out[1], n_far[h])
    g_a.a()
    project_space(1)
    project_space(3)
    for h, part in enumerate(halves):
        landed(nb.at[2, part], n_far[h])
    project_space(2)

    a_num = [ticket() for _ in range(NSP)]
    a_out = sending(ats.at[0, 1:NV]), sending(ats.at[1:NSP])

    def attend_space(k):
        at = slice(k * LH * TOK, (k + 1) * LH * TOK)
        shares = softmax0(dot(k_nat[...], qts[:, at], NN)).astype(BF)
        pts[:, at] = shares
        out = jnp.transpose(per_head(kvt[LW:, :], shares)).astype(BF)
        ats[k] = out.reshape(NV, CH, LW)

    def send_attended(k):
        for j in order + (0,):
            to = (plus(v, j, NV), plus(s, -k, NSP))
            if k or j:
                push(ats.at[k, to[0]], att.at[s, j], ("view", "space"), to, a_out[min(k, 1)], a_num[k])
            else:
                att[pl.ds(s, 1), 0:1] = ats[0:1, pl.ds(v, 1)]

    attend_space(2)
    attend_space(1)
    send_attended(2)
    send_attended(1)
    g_a.b()
    g_b.a()
    attend_space(3)
    attend_space(0)
    send_attended(3)
    send_attended(0)
    g_a.c()
    g_b.b()
    g_c.a()
    g_a.d()
    g_b.c()

    def slot_of(view):
        return lax.rem(v - view + NV, NV)

    g_b.d()
    landed(xb.at[1:NV], x2_num)
    for k in (2, 1, 3):
        landed(att.at[plus(s, k, NSP)], a_num[k])
    landed(att.at[s, 1:NV], a_num[0])
    c2_num, c2_out = ticket(), sending(c2.at[1:NT_])
    for m in tm_order:
        push(xb.at[slot_of(paired(m)), 1], c2.at[m], "tm", paired(m), c2_out, c2_num)
    c2[0] = xb[slot_of(t), 1]
    g_c.b()
    g_a.e()
    term = dot(att[0].reshape(TOK, LW), wos[0, :LW, :], NN)
    for h in range(1, NSP):
        term += dot(att[h].reshape(TOK, LW), wos[0, h * LW : (h + 1) * LW, :], NN)
    x2[...] = (xb[:, 0].reshape(TOK, D).astype(F32) + term).astype(BF).reshape(NV, CH, D)
    rows_view = x2[...].reshape(TOK, D)
    normed, _ = rms(rows_view.astype(F32))
    tokens = normed.astype(BF)

    def attend_small(w, g):
        lanes = slice(g * GW, (g + 1) * GW)
        query = dot(w[0, lanes, :], tokens, NT).astype(BF) * jnp.asarray(SCALE, BF)
        key_t = dot(w[1, lanes, :], tokens, NT).astype(BF)
        value_t = dot(w[2, lanes, :], tokens, NT).astype(BF)
        queries = stacked(query, gmask)
        shares = softmax0(dot(key_t, queries, TN) + bias[...]).astype(BF)
        return queries, key_t, value_t, shares

    def backward_small(w, g, queries, key_t, value_t, shares, out_grad):
        lanes = slice(g * GW, (g + 1) * GW)
        grads = stacked(out_grad, gmask)
        share_grad = dot(value_t, grads, TN)
        wide = shares.astype(F32)
        row_dot = jnp.sum(wide * share_grad, axis=0, keepdims=True)
        score_grad = (wide * (share_grad - row_dot)).astype(BF)
        query_grad = (per_head(key_t, score_grad) * SCALE).astype(BF)
        key_grad = dot(score_grad, queries, NT).astype(BF)
        value_grad = dot(shares, grads, NT).astype(BF)
        total = dot(query_grad, w[0, lanes, :], TN)
        total += dot(key_grad, w[1, lanes, :], NN)
        return total + dot(value_grad, w[2, lanes, :], NN)

    outs = []
    for g in range(GROUPS):
        queries, key_t, value_t, shares = attend_small(wqv, g)
        qts_v[g], kt_v[g], vt_v[g], pt_v[g] = queries, key_t, value_t, shares
        outs.append(per_head(value_t, shares).astype(BF))
    g_c.c()
    g_b.e()
    term = dot(jnp.concatenate(outs, axis=0), wov[0], TN)
    xt[...] = (rows_view.astype(F32) + term).astype(BF).reshape(NV, CH, D)

    x3_num, x3_out = ticket(), sending(x3.at[1:NT_])
    for m in tm_order:
        push(xt.at[slot_of(paired(m))], x3.at[m], "tm", paired(m), x3_out, x3_num)
    x3[0] = xt[slot_of(t)]
    g_c.d()
    landed(c2.at[1:NT_], c2_num)
    upstream = c2[...].reshape(TOK, D)
    out_grads = dot(wot[0], upstream, NT).astype(BF)
    landed(x3.at[1:NT_], x3_num)
    g_c.e()
    rows_time = x3[...].reshape(TOK, D)
    normed, _ = rms(rows_time.astype(F32))
    tokens = normed.astype(BF)

    total = jnp.zeros((TOK, D), F32)
    for g in range(GROUPS):
        queries, key_t, value_t, shares = attend_small(wqt, g)
        out_grad = out_grads[g * GW : (g + 1) * GW]
        total += backward_small(wqt, g, queries, key_t, value_t, shares, out_grad)
    ut[...] = finish(upstream, rows_time, total).reshape(NT_, CH, D)

    u2_num, u2_out = ticket(), sending(ut.at[1:NT_])
    here = slot_of(t)
    for m in tm_order:
        push(ut.at[m], u2.at[here], "tm", paired(m), u2_out, u2_num)
    u2[pl.ds(here, 1)] = ut[0:1]
    landed(u2.at[1:NT_], u2_num)
    upstream = u2[...].reshape(TOK, D)
    total = jnp.zeros((TOK, D), F32)
    for g in range(GROUPS):
        out_grad = dot(wov[0, g * GW : (g + 1) * GW, :], upstream, NT).astype(BF)
        total += backward_small(wqv, g, qts_v[g], kt_v[g], vt_v[g], pt_v[g], out_grad)
    upstream = finish(upstream, x2[...].reshape(TOK, D), total)
    uv[...] = upstream.reshape(NV, CH, D)

    out_grad = dot(wos[0], upstream, NT)
    for h in range(NSP):
        part = jnp.transpose(out_grad[h * LW : (h + 1) * LW]).astype(BF)
        ogs[h] = part.reshape(NV, CH, LW)
    og_num = [ticket() for _ in range(NSP)]
    og_out = sending(ogs.at[0, 1:NV]), sending(ogs.at[1:NSP])
    for k in (2, 1, 3, 0):
        for j in order + (0,):
            to = (plus(v, -j, NV), plus(s, k, NSP))
            if k or j:
                push(ogs.at[to[1], j], og.at[k, v], ("view", "space"), to, og_out[min(k, 1)], og_num[k])
    og[0:1, pl.ds(v, 1)] = ogs[pl.ds(s, 1), 0:1]
    def backward_space(k):
        at = slice(k * LH * TOK, (k + 1) * LH * TOK)
        out_grad = og[k].reshape(TOK, LW)
        grads = jnp.concatenate([out_grad * m for m in nmask], axis=0)
        ogts[at, :] = grads
        share_grad = dot(v_nat[...], grads, NT)
        wide = pts[:, at].astype(F32)
        row_dot = jnp.sum(wide * share_grad, axis=0, keepdims=True)
        score_grad = (wide * (share_grad - row_dot)).astype(BF)
        gts[:, at] = score_grad
        dqt[k] = (per_head(kvt[:LW, :], score_grad) * SCALE).astype(BF)

    head_at = lax.broadcasted_iota(jnp.int32, (TOK, LW), 1) // HD
    nmask = [(head_at == h).astype(F32).astype(BF) for h in range(LH)]
    u3_num, u3_out = ticket(), sending(uv.at[1:NV])
    landed(og.at[0, 1:NV], og_num[0])
    landed(og.at[1], og_num[1])
    backward_space(0)
    backward_space(1)
    landed(og.at[3], og_num[3])
    landed(og.at[2], og_num[2])
    for j in order:
        push(uv.at[j], u3.at[v], "view", plus(v, -j, NV), u3_out, u3_num)
    backward_space(3)
    backward_space(2)
    u3[pl.ds(v, 1)] = uv[0:1]

    def partial_sums(k):
        at = pl.ds(pl.multiple_of(k * TOK, TOK), TOK)
        key_grad = dot(gts[at, :], qts[...], NT).astype(BF)
        value_grad = dot(pts[at, :], ogts[...], NN).astype(BF)
        part = dot(dqt[k], wqs_ref[:LW, :], TN)
        part += dot(key_grad, wqs_ref[LW : 2 * LW, :], NN)
        return part + dot(value_grad, wqs_ref[2 * LW :, :], NN)

    rf_num, near_num, late_num = ticket(), ticket(), ticket()
    rs_out = sending(rsend)
    rsend[0] = partial_sums(2).astype(BF)
    push(rsend.at[0], rf, "space", s_next, rs_out, rf_num)
    rsend[1] = partial_sums(1 + 2 * core).astype(BF)
    push(rsend.at[1], rs.at[0], "space", s_prev, rs_out, near_num)
    late = partial_sums(3 - 2 * core)
    total = partial_sums(0)
    landed(rf, rf_num)
    rsend[2] = (late + rf[...].astype(F32)).astype(BF)
    push(rsend.at[2], rs.at[1], "space", s_next, rs_out, late_num)
    landed(rs.at[0], near_num)
    total += rs[0].astype(F32)
    landed(rs.at[1], late_num)
    total += rs[1].astype(F32)
    landed(u3.at[1:NV], u3_num)
    out_ref[...] = finish(u3[...].reshape(TOK, D), xc[:, 0].reshape(TOK, D), total)

    for ref, number in left:
        remote(ref, ref, "tm", sibling, number, 0).wait_send()


def on_device(latents, cotangent, wqs, wos, wqv, wov, wqt, wot):
    vmem = pl.BlockSpec(memory_space=pltpu.VMEM)
    hbm = pl.BlockSpec(memory_space=pltpu.HBM)

    def buf(*shape, dtype=BF):
        return pltpu.VMEM(shape, dtype)

    wide = NSP * LH * TOK
    out = pl.pallas_call(
        body,
        out_shape=jax.ShapeDtypeStruct((TOK, D), BF),
        in_specs=[hbm] * 8,
        out_specs=vmem,
        scratch_shapes=[
            buf(NV, 2, CH, D),
            buf(3 * LW, D),
            buf(NSP, TOK, D),
            buf(NSP * TOK, LW),
            buf(NSP * TOK, LW),
            buf(LW, wide),
            buf(2 * LW, NSP * TOK),
            buf(NSP * TOK, wide),
            buf(NSP * TOK, wide),
            buf(wide, LW),
            buf(NSP, LW, TOK),
            buf(NSP, NV, CH, LW),
            buf(NSP, NV, CH, LW),
        ]
        + [buf(NV, 2, CH, D)]
        + [buf(NV, CH, D)] * 8
        + [
            buf(NSP, NV, CH, LW),
            buf(NSP, NV, CH, LW),
            buf(3, TOK, D),
            buf(2, TOK, D),
            buf(TOK, D),
            buf(TOK, GH * TOK, dtype=F32),
            buf(GROUPS, GW, TOK),
            buf(GROUPS, GW, TOK),
            buf(GROUPS, GW, GH * TOK),
            buf(GROUPS, TOK, GH * TOK),
            buf(9, D, D),
            pltpu.SemaphoreType.DMA((NSEM,)),
            pltpu.SemaphoreType.DMA((NSEM,)),
            pltpu.SemaphoreType.DMA((8,)),
        ],
        compiler_params=pltpu.CompilerParams(
            collective_id=0, has_side_effects=True, vmem_limit_bytes=60 * 1024 * 1024
        ),
        name="block_backward",
    )(
        latents.reshape(NV, CH, D),
        cotangent.reshape(NV, CH, D),
        wqs.reshape(3 * LW, D),
        wos[None],
        wqv,
        wov[None],
        wqt,
        wot[None],
    )
    return out[None, None]


def solution(mesh):
    in_specs = (
        P("view", "tm", "space", None),
        P("view", "tm", "space", None),
        P(None, "space", None),
        P("space", None),
        P(None, "space", None),
        P("space", None),
        P(None, "space", None),
        P("space", None),
    )
    return jax.shard_map(
        on_device,
        mesh=mesh,
        in_specs=in_specs,
        out_specs=P("view", "tm", "space", None),
        check_vma=False,
    )
```

```python
import jax
import jax.numpy as jnp
from jax import lax
from jax.experimental import pallas as pl
from jax.experimental.pallas import tpu as pltpu
from jax.sharding import PartitionSpec as P

MESH = pl.DeviceIdType.MESH
BF = jnp.bfloat16
F32 = jnp.float32
NN = ((1,), (0,))
NT = ((1,), (1,))
TN = ((0,), (0,))

D = 768
TOK = 128
NSP = 4
NV = 8
NT_ = 8
CH = 16
HD = 64
LH = 3
LW = LH * HD
GH = 4
GW = GH * HD
GROUPS = D // GW
SCALE = HD**-0.5
NSEM = 64


def dot(a, b, dims):
    return lax.dot_general(a, b, (dims, ((), ())), preferred_element_type=F32)


def rms(values):
    factor = lax.rsqrt(jnp.mean(values * values, axis=-1, keepdims=True) + 1e-06)
    return values * factor, factor


def finish(upstream, earlier, normed_grad):
    normed, factor = rms(earlier.astype(F32))
    inner = jnp.mean(normed_grad * normed, axis=-1, keepdims=True)
    return (upstream.astype(F32) + factor * (normed_grad - normed * inner)).astype(BF)


def softmax0(scores):
    top = jnp.max(scores, axis=0, keepdims=True)
    expo = jnp.exp(scores - top)
    return expo * (1.0 / jnp.sum(expo, axis=0, keepdims=True))


def head_masks(rows):
    head = lax.broadcasted_iota(jnp.int32, (rows, TOK), 0) // HD
    return [(head == h).astype(F32).astype(BF) for h in range(rows // HD)]


def stacked(values, masks):
    return jnp.concatenate([values * m for m in masks], axis=1)


def per_head(left, right):
    heads = left.shape[0] // HD
    return jnp.concatenate(
        [
            dot(left[h * HD : (h + 1) * HD], right[:, h * TOK : (h + 1) * TOK], NN)
            for h in range(heads)
        ],
        axis=0,
    )


def body(
    x_in, cot_in, wqs_in, wos_in, wqv_in, wov_in, wqt_in, wot_in,
    out_ref,
    xc, wqs_ref,
    nb, k_nat, v_nat, qts, kvt, pts, gts, ogts, dqt, ats, att,
    xb, x2, xt, x3, c2, ut, u2, uv, u3, ogs, og, rsend, rs, rf,
    bias, kt_v, vt_v, qts_v, pt_v,
    whole,
    send_sem, recv_sem, local_sem,
):
    t = lax.axis_index("tm")
    v = lax.axis_index("view")
    s = lax.axis_index("space")
    core = lax.rem(t, 2)
    sibling = t + 1 - 2 * core
    y = lax.rem(v, 4)
    half = lax.rem(y, 2)
    step = 1 - 2 * core
    y_next = v - y + lax.rem(y + step + 4, 4)
    s_next = lax.rem(s + step + 4, 4)
    s_prev = lax.rem(s - step + 4, 4)

    def plus(me, k, n):
        return lax.rem(me + k + n, n)

    bits = [t % 2, t // 2 % 2, t // 4]

    def paired(m):
        return t + sum((1 - 2 * bits[at]) * 2**at for at in range(3) if m >> at & 1)

    tm_order = (6, 7, 4, 5, 2, 3, 1)
    left = []
    count = [0]

    def ticket():
        count[0] += 1
        return count[0] - 1

    def remote(src, dst, axis, index, number, arrival):
        to = {axis: index} if isinstance(axis, str) else dict(zip(axis, index))
        return pltpu.make_async_remote_copy(
            src_ref=src,
            dst_ref=dst,
            send_sem=send_sem.at[number],
            recv_sem=recv_sem.at[arrival],
            device_id=to,
            device_id_type=MESH,
        )

    def push(src, dst, axis, index, number, arrival):
        remote(src, dst, axis, index, number, arrival).start()

    def landed(ref, arrival):
        remote(ref, ref, "tm", sibling, 0, arrival).wait_recv()

    def sending(ref):
        left.append((ref, ticket()))
        return left[-1][1]

    def rows(owner, c, h, size):
        return pl.ds(pl.multiple_of(owner * LW + c * 96 + h * 48, 16), size)

    class Gather:
        def __init__(self, first, end):
            self.first, self.end = first, end
            self.others = [plus(s, -1, 4), plus(s, 1, 4), plus(s, 2, 4)]
            self.out = [sending(self.bytes_of(size)) for size in (96, 48, 144, 288)]
            self.near, self.far, self.y_near, self.y_far, self.sib = [ticket() for _ in range(5)]

        def bytes_of(self, size):
            return whole.at[self.first : self.end, 0:size, :]

        def piece(self, owner, c, h, size=48):
            return whole.at[self.first : self.end, rows(owner, c, h, size), :]

        def a(self):
            mine = self.piece(s, core, half)
            push(mine, mine, "space", plus(s, 1, 4), self.out[0], self.near)
            push(mine, mine, "space", plus(s, -1, 4), self.out[0], self.near)

        def b(self):
            landed(self.bytes_of(96), self.near)
            far = self.piece(s_prev, core, half)
            push(far, far, "space", s_next, self.out[1], self.far)
            for at in range(2):
                part = self.piece(self.others[at], core, half)
                push(part, part, "view", y_next, self.out[2], self.y_near)

        def c(self):
            landed(self.bytes_of(48), self.far)
            part = self.piece(self.others[2], core, half)
            push(part, part, "view", y_next, self.out[2], self.y_far)

        def d(self):
            landed(self.bytes_of(96), self.y_near)
            for at in range(3):
                if at == 2:
                    landed(self.bytes_of(48), self.y_far)
                part = self.piece(self.others[at], core, 0, 96)
                push(part, part, "tm", sibling, self.out[3], self.sib)

        def e(self):
            landed(self.bytes_of(288), self.sib)

    g_a, g_b, g_c = Gather(0, 4), Gather(4, 6), Gather(6, 9)
    wos, wqv, wov = whole.at[0:1], whole.at[1:4], whole.at[4:5]
    wot, wqt = whole.at[5:6], whole.at[6:9]
    own = pl.ds(pl.multiple_of(s * LW, 16), LW)

    loads = [
        pltpu.make_async_copy(src, dst, local_sem.at[at])
        for at, (src, dst) in enumerate(
            (
                (x_in, xc.at[:, 0]),
                (wqs_in, wqs_ref),
                (cot_in, xc.at[:, 1]),
                (wos_in, wos.at[:, own, :]),
                (wqv_in, wqv.at[:, own, :]),
                (wov_in, wov.at[:, own, :]),
                (wot_in, wot.at[:, own, :]),
                (wqt_in, wqt.at[:, own, :]),
            )
        )
    ]
    for copy in loads:
        copy.start()

    barrier = pltpu.get_barrier_semaphore()
    for k in range(NSP):
        for j in range(NV):
            if k or j:
                pl.semaphore_signal(
                    barrier,
                    inc=1,
                    device_id={"view": plus(v, j, NV), "space": plus(s, k, NSP)},
                    device_id_type=MESH,
                )
    for k in range(1, NT_):
        pl.semaphore_signal(barrier, inc=1, device_id={"tm": plus(t, k, NT_)}, device_id_type=MESH)

    loads[0].wait()
    x_rows = xc[:, 0].reshape(TOK, D)
    normed, _ = rms(x_rows.astype(F32))
    nb[0] = normed.astype(BF)
    key_at = lax.broadcasted_iota(jnp.int32, (TOK, GH * TOK), 0)
    query_at = lax.broadcasted_iota(jnp.int32, (TOK, GH * TOK), 1)
    bias[...] = jnp.where(lax.rem(key_at, CH) == lax.rem(query_at, CH), 0.0, -1e30)
    lmask = head_masks(LW)
    gmask = head_masks(GW)
    pl.semaphore_wait(barrier, NSP * NV + NT_ - 2)

    halves = [slice(0, TOK // 2), slice(TOK // 2, TOK)]
    n_near, n_far = [ticket() for _ in halves], [ticket() for _ in halves]
    n_out = sending(nb.at[0:2]), sending(nb.at[0])
    for h, part in enumerate(halves):
        for k in (1, 3):
            push(nb.at[0, part], nb.at[k, part], "space", plus(s, k, NSP), n_out[0], n_near[h])
    for copy in loads[1:]:
        copy.wait()
    order = (4, 3, 5, 2, 6, 1, 7)
    x2_num, x2_out = ticket(), sending(xb.at[1:NV])
    for j in order:
        to = plus(v, j, NV)
        push(xc.at[to], xb.at[j], "view", to, x2_out, x2_num)
    xb[0] = xc[v]

    def project_space(k):
        tokens = nb[k]
        packed = dot(wqs_ref[...], tokens, NT)
        at = slice(k * TOK, (k + 1) * TOK)
        query = packed[:LW].astype(BF) * jnp.asarray(SCALE, BF)
        qts[:, k * LH * TOK : (k + 1) * LH * TOK] = stacked(query, lmask)
        kvt[:, at] = packed[LW:].astype(BF)
        k_nat[at, :] = jnp.transpose(packed[LW : 2 * LW]).astype(BF)
        v_nat[at, :] = jnp.transpose(packed[2 * LW :]).astype(BF)

    project_space(0)
    for h, part in enumerate(halves):
        landed(nb.at[0], n_near[h])
        push(nb.at[1 + 2 * core, part], nb.at[2, part], "space", s_next, n_out[1], n_far[h])
    g_a.a()
    project_space(1)
    project_space(3)
    for h, part in enumerate(halves):
        landed(nb.at[2, part], n_far[h])
    project_space(2)

    a_num = [ticket() for _ in range(NSP)]
    a_out = sending(ats.at[0, 1:NV]), sending(ats.at[1:NSP])

    def attend_space(k):
        at = slice(k * LH * TOK, (k + 1) * LH * TOK)
        shares = softmax0(dot(k_nat[...], qts[:, at], NN)).astype(BF)
        pts[:, at] = shares
        out = jnp.transpose(per_head(kvt[LW:, :], shares)).astype(BF)
        ats[k] = out.reshape(NV, CH, LW)

    def send_attended(k):
        for j in order + (0,):
            to = (plus(v, j, NV), plus(s, -k, NSP))
            if k or j:
                push(ats.at[k, to[0]], att.at[s, j], ("view", "space"), to, a_out[min(k, 1)], a_num[k])
            else:
                att[pl.ds(s, 1), 0:1] = ats[0:1, pl.ds(v, 1)]

    attend_space(2)
    attend_space(1)
    send_attended(2)
    send_attended(1)
    g_a.b()
    g_b.a()
    attend_space(3)
    attend_space(0)
    send_attended(3)
    send_attended(0)
    g_a.c()
    g_b.b()
    g_c.a()
    g_a.d()
    g_b.c()

    def slot_of(view):
        return lax.rem(v - view + NV, NV)

    g_b.d()
    landed(xb.at[1:NV], x2_num)
    g_c.b()
    for k in (2, 1, 3):
        landed(att.at[plus(s, k, NSP)], a_num[k])
    landed(att.at[s, 1:NV], a_num[0])
    c2_num, c2_out = ticket(), sending(c2.at[1:NT_])
    for m in tm_order:
        push(xb.at[slot_of(paired(m)), 1], c2.at[m], "tm", paired(m), c2_out, c2_num)
    c2[0] = xb[slot_of(t), 1]
    g_a.e()
    term = dot(att[0].reshape(TOK, LW), wos[0, :LW, :], NN)
    for h in range(1, NSP):
        term += dot(att[h].reshape(TOK, LW), wos[0, h * LW : (h + 1) * LW, :], NN)
    x2[...] = (xb[:, 0].reshape(TOK, D).astype(F32) + term).astype(BF).reshape(NV, CH, D)
    rows_view = x2[...].reshape(TOK, D)
    normed, _ = rms(rows_view.astype(F32))
    tokens = normed.astype(BF)

    def attend_small(w, g):
        lanes = slice(g * GW, (g + 1) * GW)
        query = dot(w[0, lanes, :], tokens, NT).astype(BF) * jnp.asarray(SCALE, BF)
        key_t = dot(w[1, lanes, :], tokens, NT).astype(BF)
        value_t = dot(w[2, lanes, :], tokens, NT).astype(BF)
        queries = stacked(query, gmask)
        shares = softmax0(dot(key_t, queries, TN) + bias[...]).astype(BF)
        return queries, key_t, value_t, shares

    def backward_small(w, g, queries, key_t, value_t, shares, out_grad):
        lanes = slice(g * GW, (g + 1) * GW)
        grads = stacked(out_grad, gmask)
        share_grad = dot(value_t, grads, TN)
        wide = shares.astype(F32)
        row_dot = jnp.sum(wide * share_grad, axis=0, keepdims=True)
        score_grad = (wide * (share_grad - row_dot)).astype(BF)
        query_grad = (per_head(key_t, score_grad) * SCALE).astype(BF)
        key_grad = dot(score_grad, queries, NT).astype(BF)
        value_grad = dot(shares, grads, NT).astype(BF)
        total = dot(query_grad, w[0, lanes, :], TN)
        total += dot(key_grad, w[1, lanes, :], NN)
        return total + dot(value_grad, w[2, lanes, :], NN)

    g_c.c()
    outs = []
    for g in range(GROUPS):
        queries, key_t, value_t, shares = attend_small(wqv, g)
        qts_v[g], kt_v[g], vt_v[g], pt_v[g] = queries, key_t, value_t, shares
        outs.append(per_head(value_t, shares).astype(BF))
    g_c.d()
    g_b.e()
    term = dot(jnp.concatenate(outs, axis=0), wov[0], TN)
    xt[...] = (rows_view.astype(F32) + term).astype(BF).reshape(NV, CH, D)

    x3_num, x3_out = ticket(), sending(x3.at[1:NT_])
    for m in tm_order:
        push(xt.at[slot_of(paired(m))], x3.at[m], "tm", paired(m), x3_out, x3_num)
    x3[0] = xt[slot_of(t)]
    landed(c2.at[1:NT_], c2_num)
    upstream = c2[...].reshape(TOK, D)
    out_grads = dot(wot[0], upstream, NT).astype(BF)
    landed(x3.at[1:NT_], x3_num)
    g_c.e()
    rows_time = x3[...].reshape(TOK, D)
    normed, _ = rms(rows_time.astype(F32))
    tokens = normed.astype(BF)

    total = jnp.zeros((TOK, D), F32)
    for g in range(GROUPS):
        queries, key_t, value_t, shares = attend_small(wqt, g)
        out_grad = out_grads[g * GW : (g + 1) * GW]
        total += backward_small(wqt, g, queries, key_t, value_t, shares, out_grad)
    ut[...] = finish(upstream, rows_time, total).reshape(NT_, CH, D)

    u2_num, u2_out = ticket(), sending(ut.at[1:NT_])
    here = slot_of(t)
    for m in tm_order:
        push(ut.at[m], u2.at[here], "tm", paired(m), u2_out, u2_num)
    u2[pl.ds(here, 1)] = ut[0:1]
    landed(u2.at[1:NT_], u2_num)
    upstream = u2[...].reshape(TOK, D)
    total = jnp.zeros((TOK, D), F32)
    for g in range(GROUPS):
        out_grad = dot(wov[0, g * GW : (g + 1) * GW, :], upstream, NT).astype(BF)
        total += backward_small(wqv, g, qts_v[g], kt_v[g], vt_v[g], pt_v[g], out_grad)
    upstream = finish(upstream, x2[...].reshape(TOK, D), total)
    uv[...] = upstream.reshape(NV, CH, D)

    out_grad = dot(wos[0], upstream, NT)
    for h in range(NSP):
        part = jnp.transpose(out_grad[h * LW : (h + 1) * LW]).astype(BF)
        ogs[h] = part.reshape(NV, CH, LW)
    og_num = [ticket() for _ in range(NSP)]
    og_out = sending(ogs.at[0, 1:NV]), sending(ogs.at[1:NSP])
    for k in (2, 1, 3, 0):
        for j in order + (0,):
            to = (plus(v, -j, NV), plus(s, k, NSP))
            if k or j:
                push(ogs.at[to[1], j], og.at[k, v], ("view", "space"), to, og_out[min(k, 1)], og_num[k])
    og[0:1, pl.ds(v, 1)] = ogs[pl.ds(s, 1), 0:1]
    def backward_space(k):
        at = slice(k * LH * TOK, (k + 1) * LH * TOK)
        out_grad = og[k].reshape(TOK, LW)
        grads = jnp.concatenate([out_grad * m for m in nmask], axis=0)
        ogts[at, :] = grads
        share_grad = dot(v_nat[...], grads, NT)
        wide = pts[:, at].astype(F32)
        row_dot = jnp.sum(wide * share_grad, axis=0, keepdims=True)
        score_grad = (wide * (share_grad - row_dot)).astype(BF)
        gts[:, at] = score_grad
        dqt[k] = (per_head(kvt[:LW, :], score_grad) * SCALE).astype(BF)

    head_at = lax.broadcasted_iota(jnp.int32, (TOK, LW), 1) // HD
    nmask = [(head_at == h).astype(F32).astype(BF) for h in range(LH)]
    u3_num, u3_out = ticket(), sending(uv.at[1:NV])
    landed(og.at[0, 1:NV], og_num[0])
    landed(og.at[1], og_num[1])
    backward_space(0)
    backward_space(1)
    landed(og.at[3], og_num[3])
    landed(og.at[2], og_num[2])
    for j in order:
        push(uv.at[j], u3.at[v], "view", plus(v, -j, NV), u3_out, u3_num)
    backward_space(3)
    backward_space(2)
    u3[pl.ds(v, 1)] = uv[0:1]

    def partial_sums(k):
        at = pl.ds(pl.multiple_of(k * TOK, TOK), TOK)
        key_grad = dot(gts[at, :], qts[...], NT).astype(BF)
        value_grad = dot(pts[at, :], ogts[...], NN).astype(BF)
        part = dot(dqt[k], wqs_ref[:LW, :], TN)
        part += dot(key_grad, wqs_ref[LW : 2 * LW, :], NN)
        return part + dot(value_grad, wqs_ref[2 * LW :, :], NN)

    rf_num, near_num, late_num = ticket(), ticket(), ticket()
    rs_out = sending(rsend)
    rsend[0] = partial_sums(2).astype(BF)
    push(rsend.at[0], rf, "space", s_next, rs_out, rf_num)
    rsend[1] = partial_sums(1 + 2 * core).astype(BF)
    push(rsend.at[1], rs.at[0], "space", s_prev, rs_out, near_num)
    late = partial_sums(3 - 2 * core)
    total = partial_sums(0)
    landed(rf, rf_num)
    rsend[2] = (late + rf[...].astype(F32)).astype(BF)
    push(rsend.at[2], rs.at[1], "space", s_next, rs_out, late_num)
    landed(rs.at[0], near_num)
    total += rs[0].astype(F32)
    landed(rs.at[1], late_num)
    total += rs[1].astype(F32)
    landed(u3.at[1:NV], u3_num)
    out_ref[...] = finish(u3[...].reshape(TOK, D), xc[:, 0].reshape(TOK, D), total)

    for ref, number in left:
        remote(ref, ref, "tm", sibling, number, 0).wait_send()


def on_device(latents, cotangent, wqs, wos, wqv, wov, wqt, wot):
    vmem = pl.BlockSpec(memory_space=pltpu.VMEM)
    hbm = pl.BlockSpec(memory_space=pltpu.HBM)

    def buf(*shape, dtype=BF):
        return pltpu.VMEM(shape, dtype)

    wide = NSP * LH * TOK
    out = pl.pallas_call(
        body,
        out_shape=jax.ShapeDtypeStruct((TOK, D), BF),
        in_specs=[hbm] * 8,
        out_specs=vmem,
        scratch_shapes=[
            buf(NV, 2, CH, D),
            buf(3 * LW, D),
            buf(NSP, TOK, D),
            buf(NSP * TOK, LW),
            buf(NSP * TOK, LW),
            buf(LW, wide),
            buf(2 * LW, NSP * TOK),
            buf(NSP * TOK, wide),
            buf(NSP * TOK, wide),
            buf(wide, LW),
            buf(NSP, LW, TOK),
            buf(NSP, NV, CH, LW),
            buf(NSP, NV, CH, LW),
        ]
        + [buf(NV, 2, CH, D)]
        + [buf(NV, CH, D)] * 8
        + [
            buf(NSP, NV, CH, LW),
            buf(NSP, NV, CH, LW),
            buf(3, TOK, D),
            buf(2, TOK, D),
            buf(TOK, D),
            buf(TOK, GH * TOK, dtype=F32),
            buf(GROUPS, GW, TOK),
            buf(GROUPS, GW, TOK),
            buf(GROUPS, GW, GH * TOK),
            buf(GROUPS, TOK, GH * TOK),
            buf(9, D, D),
            pltpu.SemaphoreType.DMA((NSEM,)),
            pltpu.SemaphoreType.DMA((NSEM,)),
            pltpu.SemaphoreType.DMA((8,)),
        ],
        compiler_params=pltpu.CompilerParams(
            collective_id=0, has_side_effects=True, vmem_limit_bytes=60 * 1024 * 1024
        ),
        name="block_backward",
    )(
        latents.reshape(NV, CH, D),
        cotangent.reshape(NV, CH, D),
        wqs.reshape(3 * LW, D),
        wos[None],
        wqv,
        wov[None],
        wqt,
        wot[None],
    )
    return out[None, None]


def solution(mesh):
    in_specs = (
        P("view", "tm", "space", None),
        P("view", "tm", "space", None),
        P(None, "space", None),
        P("space", None),
        P(None, "space", None),
        P("space", None),
        P(None, "space", None),
        P("space", None),
    )
    return jax.shard_map(
        on_device,
        mesh=mesh,
        in_specs=in_specs,
        out_specs=P("view", "tm", "space", None),
        check_vma=False,
    )
```

```python
import jax
import jax.numpy as jnp
from jax import lax
from jax.experimental import pallas as pl
from jax.experimental.pallas import tpu as pltpu
from jax.sharding import PartitionSpec as P

MESH = pl.DeviceIdType.MESH
BF = jnp.bfloat16
F32 = jnp.float32
NN = ((1,), (0,))
NT = ((1,), (1,))
TN = ((0,), (0,))

D = 768
TOK = 128
NSP = 4
NV = 8
NT_ = 8
CH = 16
HD = 64
LH = 3
LW = LH * HD
GH = 4
GW = GH * HD
GROUPS = D // GW
SCALE = HD**-0.5
NSEM = 128


def dot(a, b, dims):
    return lax.dot_general(a, b, (dims, ((), ())), preferred_element_type=F32)


def rms(values):
    factor = lax.rsqrt(jnp.mean(values * values, axis=-1, keepdims=True) + 1e-06)
    return values * factor, factor


def finish(upstream, earlier, normed_grad):
    normed, factor = rms(earlier.astype(F32))
    inner = jnp.mean(normed_grad * normed, axis=-1, keepdims=True)
    return (upstream.astype(F32) + factor * (normed_grad - normed * inner)).astype(BF)


def softmax0(scores):
    top = jnp.max(scores, axis=0, keepdims=True)
    expo = jnp.exp(scores - top)
    return expo * (1.0 / jnp.sum(expo, axis=0, keepdims=True))


def head_masks(rows):
    head = lax.broadcasted_iota(jnp.int32, (rows, TOK), 0) // HD
    return [(head == h).astype(F32).astype(BF) for h in range(rows // HD)]


def stacked(values, masks):
    return jnp.concatenate([values * m for m in masks], axis=1)


def per_head(left, right):
    heads = left.shape[0] // HD
    return jnp.concatenate(
        [
            dot(left[h * HD : (h + 1) * HD], right[:, h * TOK : (h + 1) * TOK], NN)
            for h in range(heads)
        ],
        axis=0,
    )


def body(
    x_in, cot_in, wqs_in, wos_in, wqv_in, wov_in, wqt_in, wot_in,
    out_ref,
    xc, wqs_ref,
    nb, k_nat, v_nat, qts, kvt, pts, gts, ogts, dqt, ats, att,
    xb, x2, xt, x3, c2, ut, u2, uv, u3, ogs, og, rsend, rs, rf,
    bias, kt_v, vt_v, qts_v, pt_v,
    whole,
    send_sem, recv_sem, local_sem,
):
    t = lax.axis_index("tm")
    v = lax.axis_index("view")
    s = lax.axis_index("space")
    core = lax.rem(t, 2)
    sibling = t + 1 - 2 * core
    y = lax.rem(v, 4)
    half = lax.rem(y, 2)
    step = 1 - 2 * core
    y_next = v - y + lax.rem(y + step + 4, 4)
    s_next = lax.rem(s + step + 4, 4)
    s_prev = lax.rem(s - step + 4, 4)

    def plus(me, k, n):
        return lax.rem(me + k + n, n)

    bits = [t % 2, t // 2 % 2, t // 4]

    def paired(m):
        return t + sum((1 - 2 * bits[at]) * 2**at for at in range(3) if m >> at & 1)

    tm_order = (6, 7, 4, 5, 2, 3, 1)
    left = []
    count = [0]

    def ticket():
        count[0] += 1
        return count[0] - 1

    def remote(src, dst, axis, index, number, arrival):
        to = {axis: index} if isinstance(axis, str) else dict(zip(axis, index))
        return pltpu.make_async_remote_copy(
            src_ref=src,
            dst_ref=dst,
            send_sem=send_sem.at[number],
            recv_sem=recv_sem.at[arrival],
            device_id=to,
            device_id_type=MESH,
        )

    def push(src, dst, axis, index, number, arrival):
        remote(src, dst, axis, index, number, arrival).start()

    def landed(ref, arrival):
        remote(ref, ref, "tm", sibling, 0, arrival).wait_recv()

    def sending(ref):
        left.append((ref, ticket()))
        return left[-1][1]

    def rows(owner, c, h, size):
        return pl.ds(pl.multiple_of(owner * LW + c * 96 + h * 48, 16), size)

    class Gather:
        def __init__(self, first, end):
            self.first, self.end = first, end
            self.others = [plus(s, -1, 4), plus(s, 1, 4), plus(s, 2, 4)]
            self.out = [sending(self.bytes_of(size)) for size in (96, 48, 144, 288)]
            self.near, self.far, self.y_near, self.y_far, self.sib = [ticket() for _ in range(5)]

        def bytes_of(self, size):
            return whole.at[self.first : self.end, 0:size, :]

        def piece(self, owner, c, h, size=48):
            return whole.at[self.first : self.end, rows(owner, c, h, size), :]

        def a(self):
            mine = self.piece(s, core, half)
            push(mine, mine, "space", plus(s, 1, 4), self.out[0], self.near)
            push(mine, mine, "space", plus(s, -1, 4), self.out[0], self.near)

        def b(self):
            landed(self.bytes_of(96), self.near)
            far = self.piece(s_prev, core, half)
            push(far, far, "space", s_next, self.out[1], self.far)
            for at in range(2):
                part = self.piece(self.others[at], core, half)
                push(part, part, "view", y_next, self.out[2], self.y_near)

        def c(self):
            landed(self.bytes_of(48), self.far)
            part = self.piece(self.others[2], core, half)
            push(part, part, "view", y_next, self.out[2], self.y_far)

        def d(self):
            landed(self.bytes_of(96), self.y_near)
            for at in range(3):
                if at == 2:
                    landed(self.bytes_of(48), self.y_far)
                part = self.piece(self.others[at], core, 0, 96)
                push(part, part, "tm", sibling, self.out[3], self.sib)

        def e(self):
            landed(self.bytes_of(288), self.sib)

    g_a1, g_a2, g_b, g_c = Gather(0, 2), Gather(2, 4), Gather(4, 6), Gather(6, 9)
    wqv, wos, wov = whole.at[0:3], whole.at[3:4], whole.at[4:5]
    wot, wqt = whole.at[5:6], whole.at[6:9]
    own = pl.ds(pl.multiple_of(s * LW, 16), LW)

    loads = [
        pltpu.make_async_copy(src, dst, local_sem.at[at])
        for at, (src, dst) in enumerate(
            (
                (x_in, xc.at[:, 0]),
                (wqs_in, wqs_ref),
                (cot_in, xc.at[:, 1]),
                (wos_in, wos.at[:, own, :]),
                (wqv_in, wqv.at[:, own, :]),
                (wov_in, wov.at[:, own, :]),
                (wot_in, wot.at[:, own, :]),
                (wqt_in, wqt.at[:, own, :]),
            )
        )
    ]
    for copy in loads:
        copy.start()

    barrier = pltpu.get_barrier_semaphore()
    for k in range(NSP):
        for j in range(NV):
            if k or j:
                pl.semaphore_signal(
                    barrier,
                    inc=1,
                    device_id={"view": plus(v, j, NV), "space": plus(s, k, NSP)},
                    device_id_type=MESH,
                )
    for k in range(1, NT_):
        pl.semaphore_signal(barrier, inc=1, device_id={"tm": plus(t, k, NT_)}, device_id_type=MESH)

    loads[0].wait()
    x_rows = xc[:, 0].reshape(TOK, D)
    normed, _ = rms(x_rows.astype(F32))
    nb[0] = normed.astype(BF)
    key_at = lax.broadcasted_iota(jnp.int32, (TOK, GH * TOK), 0)
    query_at = lax.broadcasted_iota(jnp.int32, (TOK, GH * TOK), 1)
    bias[...] = jnp.where(lax.rem(key_at, CH) == lax.rem(query_at, CH), 0.0, -1e30)
    lmask = head_masks(LW)
    gmask = head_masks(GW)
    pl.semaphore_wait(barrier, NSP * NV + NT_ - 2)

    halves = [slice(0, TOK // 2), slice(TOK // 2, TOK)]
    n_near, n_far = [ticket() for _ in halves], [ticket() for _ in halves]
    n_out = sending(nb.at[0:2]), sending(nb.at[0])
    for h, part in enumerate(halves):
        for k in (1, 3):
            push(nb.at[0, part], nb.at[k, part], "space", plus(s, k, NSP), n_out[0], n_near[h])
    for copy in loads[1:]:
        copy.wait()
    g_a1.a()
    order = (4, 3, 5, 2, 6, 1, 7)
    x2_num, x2_out = ticket(), sending(xb.at[1:NV])
    for j in order:
        to = plus(v, j, NV)
        push(xc.at[to], xb.at[j], "view", to, x2_out, x2_num)
    xb[0] = xc[v]

    def project_space(k):
        tokens = nb[k]
        packed = dot(wqs_ref[...], tokens, NT)
        at = slice(k * TOK, (k + 1) * TOK)
        query = packed[:LW].astype(BF) * jnp.asarray(SCALE, BF)
        qts[:, k * LH * TOK : (k + 1) * LH * TOK] = stacked(query, lmask)
        kvt[:, at] = packed[LW:].astype(BF)
        k_nat[at, :] = jnp.transpose(packed[LW : 2 * LW]).astype(BF)
        v_nat[at, :] = jnp.transpose(packed[2 * LW :]).astype(BF)

    project_space(0)
    for h, part in enumerate(halves):
        landed(nb.at[0], n_near[h])
        push(nb.at[1 + 2 * core, part], nb.at[2, part], "space", s_next, n_out[1], n_far[h])
    g_a2.a()
    project_space(1)
    project_space(3)
    g_a1.b()
    for h, part in enumerate(halves):
        landed(nb.at[2, part], n_far[h])
    project_space(2)

    a_num = [ticket() for _ in range(NSP)]
    a_out = sending(ats.at[0, 1:NV]), sending(ats.at[1:NSP])

    def attend_space(k):
        at = slice(k * LH * TOK, (k + 1) * LH * TOK)
        shares = softmax0(dot(k_nat[...], qts[:, at], NN)).astype(BF)
        pts[:, at] = shares
        out = jnp.transpose(per_head(kvt[LW:, :], shares)).astype(BF)
        ats[k] = out.reshape(NV, CH, LW)

    def send_attended(k):
        for j in order + (0,):
            to = (plus(v, j, NV), plus(s, -k, NSP))
            if k or j:
                push(ats.at[k, to[0]], att.at[s, j], ("view", "space"), to, a_out[min(k, 1)], a_num[k])
            else:
                att[pl.ds(s, 1), 0:1] = ats[0:1, pl.ds(v, 1)]

    attend_space(2)
    attend_space(1)
    send_attended(2)
    send_attended(1)
    g_a2.b()
    g_a1.c()
    g_b.a()
    attend_space(3)
    attend_space(0)
    send_attended(3)
    send_attended(0)
    g_a2.c()
    g_a1.d()
    g_b.b()
    g_c.a()
    g_a2.d()
    g_b.c()

    def slot_of(view):
        return lax.rem(v - view + NV, NV)

    landed(xb.at[1:NV], x2_num)
    for k in (2, 1, 3):
        landed(att.at[plus(s, k, NSP)], a_num[k])
    landed(att.at[s, 1:NV], a_num[0])
    c2_num, c2_out = ticket(), sending(c2.at[1:NT_])
    for m in tm_order:
        push(xb.at[slot_of(paired(m)), 1], c2.at[m], "tm", paired(m), c2_out, c2_num)
    c2[0] = xb[slot_of(t), 1]
    g_b.d()
    g_c.b()
    g_a1.e()
    g_a2.e()
    term = dot(att[0].reshape(TOK, LW), wos[0, :LW, :], NN)
    for h in range(1, NSP):
        term += dot(att[h].reshape(TOK, LW), wos[0, h * LW : (h + 1) * LW, :], NN)
    x2[...] = (xb[:, 0].reshape(TOK, D).astype(F32) + term).astype(BF).reshape(NV, CH, D)
    rows_view = x2[...].reshape(TOK, D)
    normed, _ = rms(rows_view.astype(F32))
    tokens = normed.astype(BF)

    def attend_small(w, g):
        lanes = slice(g * GW, (g + 1) * GW)
        query = dot(w[0, lanes, :], tokens, NT).astype(BF) * jnp.asarray(SCALE, BF)
        key_t = dot(w[1, lanes, :], tokens, NT).astype(BF)
        value_t = dot(w[2, lanes, :], tokens, NT).astype(BF)
        queries = stacked(query, gmask)
        shares = softmax0(dot(key_t, queries, TN) + bias[...]).astype(BF)
        return queries, key_t, value_t, shares

    def backward_small(w, g, queries, key_t, value_t, shares, out_grad):
        lanes = slice(g * GW, (g + 1) * GW)
        grads = stacked(out_grad, gmask)
        share_grad = dot(value_t, grads, TN)
        wide = shares.astype(F32)
        row_dot = jnp.sum(wide * share_grad, axis=0, keepdims=True)
        score_grad = (wide * (share_grad - row_dot)).astype(BF)
        query_grad = (per_head(key_t, score_grad) * SCALE).astype(BF)
        key_grad = dot(score_grad, queries, NT).astype(BF)
        value_grad = dot(shares, grads, NT).astype(BF)
        total = dot(query_grad, w[0, lanes, :], TN)
        total += dot(key_grad, w[1, lanes, :], NN)
        return total + dot(value_grad, w[2, lanes, :], NN)

    outs = []
    for g in range(GROUPS):
        queries, key_t, value_t, shares = attend_small(wqv, g)
        qts_v[g], kt_v[g], vt_v[g], pt_v[g] = queries, key_t, value_t, shares
        outs.append(per_head(value_t, shares).astype(BF))
    g_c.c()
    g_b.e()
    term = dot(jnp.concatenate(outs, axis=0), wov[0], TN)
    xt[...] = (rows_view.astype(F32) + term).astype(BF).reshape(NV, CH, D)

    x3_num, x3_out = ticket(), sending(x3.at[1:NT_])
    for m in tm_order:
        push(xt.at[slot_of(paired(m))], x3.at[m], "tm", paired(m), x3_out, x3_num)
    x3[0] = xt[slot_of(t)]
    g_c.d()
    landed(c2.at[1:NT_], c2_num)
    upstream = c2[...].reshape(TOK, D)
    out_grads = dot(wot[0], upstream, NT).astype(BF)
    landed(x3.at[1:NT_], x3_num)
    g_c.e()
    rows_time = x3[...].reshape(TOK, D)
    normed, _ = rms(rows_time.astype(F32))
    tokens = normed.astype(BF)

    total = jnp.zeros((TOK, D), F32)
    for g in range(GROUPS):
        queries, key_t, value_t, shares = attend_small(wqt, g)
        out_grad = out_grads[g * GW : (g + 1) * GW]
        total += backward_small(wqt, g, queries, key_t, value_t, shares, out_grad)
    ut[...] = finish(upstream, rows_time, total).reshape(NT_, CH, D)

    u2_num, u2_out = ticket(), sending(ut.at[1:NT_])
    here = slot_of(t)
    for m in tm_order:
        push(ut.at[m], u2.at[here], "tm", paired(m), u2_out, u2_num)
    u2[pl.ds(here, 1)] = ut[0:1]
    landed(u2.at[1:NT_], u2_num)
    upstream = u2[...].reshape(TOK, D)
    total = jnp.zeros((TOK, D), F32)
    for g in range(GROUPS):
        out_grad = dot(wov[0, g * GW : (g + 1) * GW, :], upstream, NT).astype(BF)
        total += backward_small(wqv, g, qts_v[g], kt_v[g], vt_v[g], pt_v[g], out_grad)
    upstream = finish(upstream, x2[...].reshape(TOK, D), total)
    uv[...] = upstream.reshape(NV, CH, D)

    out_grad = dot(wos[0], upstream, NT)
    for h in range(NSP):
        part = jnp.transpose(out_grad[h * LW : (h + 1) * LW]).astype(BF)
        ogs[h] = part.reshape(NV, CH, LW)
    og_num = [ticket() for _ in range(NSP)]
    og_out = sending(ogs.at[0, 1:NV]), sending(ogs.at[1:NSP])
    for k in (2, 1, 3, 0):
        for j in order + (0,):
            to = (plus(v, -j, NV), plus(s, k, NSP))
            if k or j:
                push(ogs.at[to[1], j], og.at[k, v], ("view", "space"), to, og_out[min(k, 1)], og_num[k])
    og[0:1, pl.ds(v, 1)] = ogs[pl.ds(s, 1), 0:1]
    def backward_space(k):
        at = slice(k * LH * TOK, (k + 1) * LH * TOK)
        out_grad = og[k].reshape(TOK, LW)
        grads = jnp.concatenate([out_grad * m for m in nmask], axis=0)
        ogts[at, :] = grads
        share_grad = dot(v_nat[...], grads, NT)
        wide = pts[:, at].astype(F32)
        row_dot = jnp.sum(wide * share_grad, axis=0, keepdims=True)
        score_grad = (wide * (share_grad - row_dot)).astype(BF)
        gts[:, at] = score_grad
        dqt[k] = (per_head(kvt[:LW, :], score_grad) * SCALE).astype(BF)

    head_at = lax.broadcasted_iota(jnp.int32, (TOK, LW), 1) // HD
    nmask = [(head_at == h).astype(F32).astype(BF) for h in range(LH)]
    u3_num, u3_out = ticket(), sending(uv.at[1:NV])
    landed(og.at[0, 1:NV], og_num[0])
    landed(og.at[1], og_num[1])
    backward_space(0)
    backward_space(1)
    landed(og.at[3], og_num[3])
    landed(og.at[2], og_num[2])
    for j in order:
        push(uv.at[j], u3.at[v], "view", plus(v, -j, NV), u3_out, u3_num)
    backward_space(3)
    backward_space(2)
    u3[pl.ds(v, 1)] = uv[0:1]

    def partial_sums(k):
        at = pl.ds(pl.multiple_of(k * TOK, TOK), TOK)
        key_grad = dot(gts[at, :], qts[...], NT).astype(BF)
        value_grad = dot(pts[at, :], ogts[...], NN).astype(BF)
        part = dot(dqt[k], wqs_ref[:LW, :], TN)
        part += dot(key_grad, wqs_ref[LW : 2 * LW, :], NN)
        return part + dot(value_grad, wqs_ref[2 * LW :, :], NN)

    rf_num, near_num, late_num = ticket(), ticket(), ticket()
    rs_out = sending(rsend)
    rsend[0] = partial_sums(2).astype(BF)
    push(rsend.at[0], rf, "space", s_next, rs_out, rf_num)
    rsend[1] = partial_sums(1 + 2 * core).astype(BF)
    push(rsend.at[1], rs.at[0], "space", s_prev, rs_out, near_num)
    late = partial_sums(3 - 2 * core)
    total = partial_sums(0)
    landed(rf, rf_num)
    rsend[2] = (late + rf[...].astype(F32)).astype(BF)
    push(rsend.at[2], rs.at[1], "space", s_next, rs_out, late_num)
    landed(rs.at[0], near_num)
    total += rs[0].astype(F32)
    landed(rs.at[1], late_num)
    total += rs[1].astype(F32)
    landed(u3.at[1:NV], u3_num)
    out_ref[...] = finish(u3[...].reshape(TOK, D), xc[:, 0].reshape(TOK, D), total)

    for ref, number in left:
        remote(ref, ref, "tm", sibling, number, 0).wait_send()


def on_device(latents, cotangent, wqs, wos, wqv, wov, wqt, wot):
    vmem = pl.BlockSpec(memory_space=pltpu.VMEM)
    hbm = pl.BlockSpec(memory_space=pltpu.HBM)

    def buf(*shape, dtype=BF):
        return pltpu.VMEM(shape, dtype)

    wide = NSP * LH * TOK
    out = pl.pallas_call(
        body,
        out_shape=jax.ShapeDtypeStruct((TOK, D), BF),
        in_specs=[hbm] * 8,
        out_specs=vmem,
        scratch_shapes=[
            buf(NV, 2, CH, D),
            buf(3 * LW, D),
            buf(NSP, TOK, D),
            buf(NSP * TOK, LW),
            buf(NSP * TOK, LW),
            buf(LW, wide),
            buf(2 * LW, NSP * TOK),
            buf(NSP * TOK, wide),
            buf(NSP * TOK, wide),
            buf(wide, LW),
            buf(NSP, LW, TOK),
            buf(NSP, NV, CH, LW),
            buf(NSP, NV, CH, LW),
        ]
        + [buf(NV, 2, CH, D)]
        + [buf(NV, CH, D)] * 8
        + [
            buf(NSP, NV, CH, LW),
            buf(NSP, NV, CH, LW),
            buf(3, TOK, D),
            buf(2, TOK, D),
            buf(TOK, D),
            buf(TOK, GH * TOK, dtype=F32),
            buf(GROUPS, GW, TOK),
            buf(GROUPS, GW, TOK),
            buf(GROUPS, GW, GH * TOK),
            buf(GROUPS, TOK, GH * TOK),
            buf(9, D, D),
            pltpu.SemaphoreType.DMA((NSEM,)),
            pltpu.SemaphoreType.DMA((NSEM,)),
            pltpu.SemaphoreType.DMA((8,)),
        ],
        compiler_params=pltpu.CompilerParams(
            collective_id=0, has_side_effects=True, vmem_limit_bytes=60 * 1024 * 1024
        ),
        name="block_backward",
    )(
        latents.reshape(NV, CH, D),
        cotangent.reshape(NV, CH, D),
        wqs.reshape(3 * LW, D),
        wos[None],
        wqv,
        wov[None],
        wqt,
        wot[None],
    )
    return out[None, None]


def solution(mesh):
    in_specs = (
        P("view", "tm", "space", None),
        P("view", "tm", "space", None),
        P(None, "space", None),
        P("space", None),
        P(None, "space", None),
        P("space", None),
        P(None, "space", None),
        P("space", None),
    )
    return jax.shard_map(
        on_device,
        mesh=mesh,
        in_specs=in_specs,
        out_specs=P("view", "tm", "space", None),
        check_vma=False,
    )
```

```python
import jax
import jax.numpy as jnp
from jax import lax
from jax.experimental import pallas as pl
from jax.experimental.pallas import tpu as pltpu
from jax.sharding import PartitionSpec as P

MESH = pl.DeviceIdType.MESH
BF = jnp.bfloat16
F32 = jnp.float32
NN = ((1,), (0,))
NT = ((1,), (1,))
TN = ((0,), (0,))

D = 768
TOK = 128
NSP = 4
NV = 8
NT_ = 8
CH = 16
HD = 64
LH = 3
LW = LH * HD
GH = 4
GW = GH * HD
GROUPS = D // GW
SCALE = HD**-0.5
NSEM = 64


def dot(a, b, dims):
    return lax.dot_general(a, b, (dims, ((), ())), preferred_element_type=F32)


def rms(values):
    factor = lax.rsqrt(jnp.mean(values * values, axis=-1, keepdims=True) + 1e-06)
    return values * factor, factor


def finish(upstream, normed, factor, normed_grad):
    inner = jnp.mean(normed_grad * normed, axis=-1, keepdims=True)
    return (upstream.astype(F32) + factor * (normed_grad - normed * inner)).astype(BF)


def softmax0(scores):
    top = jnp.max(scores, axis=0, keepdims=True)
    expo = jnp.exp(scores - top)
    return expo * (1.0 / jnp.sum(expo, axis=0, keepdims=True))


def head_masks(rows):
    head = lax.broadcasted_iota(jnp.int32, (rows, TOK), 0) // HD
    return [(head == h).astype(F32).astype(BF) for h in range(rows // HD)]


def stacked(values, masks):
    return jnp.concatenate([values * m for m in masks], axis=1)


def per_head(left, right):
    heads = left.shape[0] // HD
    return jnp.concatenate(
        [
            dot(left[h * HD : (h + 1) * HD], right[:, h * TOK : (h + 1) * TOK], NN)
            for h in range(heads)
        ],
        axis=0,
    )


def body(
    x_in, cot_in, wqs_in, wos_in, wqv_in, wov_in, wqt_in, wot_in,
    out_ref,
    xc, wqs_ref,
    nb, k_nat, v_nat, qts, kvt, pts, gts, ogts, dqt, ats, att,
    xb, x2, xt, x3, c2, ut, u2, uv, u3, ogs, og, rsend, rs, rf,
    bias, kt_v, vt_v, v_v, qts_v, pt_v,
    whole,
    send_sem, recv_sem, local_sem,
):
    t = lax.axis_index("tm")
    v = lax.axis_index("view")
    s = lax.axis_index("space")
    core = lax.rem(t, 2)
    sibling = t + 1 - 2 * core
    y = lax.rem(v, 4)
    half = lax.rem(y, 2)
    step = 1 - 2 * core
    y_next = v - y + lax.rem(y + step + 4, 4)
    s_next = lax.rem(s + step + 4, 4)
    s_prev = lax.rem(s - step + 4, 4)

    def plus(me, k, n):
        return lax.rem(me + k + n, n)

    bits = [t % 2, t // 2 % 2, t // 4]

    def paired(m):
        return t + sum((1 - 2 * bits[at]) * 2**at for at in range(3) if m >> at & 1)

    tm_order = (6, 7, 4, 5, 2, 3, 1)
    left = []
    count = [0]

    def ticket():
        count[0] += 1
        return count[0] - 1

    def remote(src, dst, axis, index, number, arrival):
        to = {axis: index} if isinstance(axis, str) else dict(zip(axis, index))
        return pltpu.make_async_remote_copy(
            src_ref=src,
            dst_ref=dst,
            send_sem=send_sem.at[number],
            recv_sem=recv_sem.at[arrival],
            device_id=to,
            device_id_type=MESH,
        )

    def push(src, dst, axis, index, number, arrival):
        remote(src, dst, axis, index, number, arrival).start()

    def landed(ref, arrival):
        remote(ref, ref, "tm", sibling, 0, arrival).wait_recv()

    def sending(ref):
        left.append((ref, ticket()))
        return left[-1][1]

    def rows(owner, c, h, size):
        return pl.ds(pl.multiple_of(owner * LW + c * 96 + h * 48, 16), size)

    class Gather:
        def __init__(self, first, end):
            self.first, self.end = first, end
            self.others = [plus(s, -1, 4), plus(s, 1, 4), plus(s, 2, 4)]
            self.out = [sending(self.bytes_of(size)) for size in (96, 48, 144, 288)]
            self.near, self.far, self.y_near, self.y_far, self.sib = [ticket() for _ in range(5)]

        def bytes_of(self, size):
            return whole.at[self.first : self.end, 0:size, :]

        def piece(self, owner, c, h, size=48):
            return whole.at[self.first : self.end, rows(owner, c, h, size), :]

        def a(self):
            mine = self.piece(s, core, half)
            push(mine, mine, "space", plus(s, 1, 4), self.out[0], self.near)
            push(mine, mine, "space", plus(s, -1, 4), self.out[0], self.near)

        def b(self):
            landed(self.bytes_of(96), self.near)
            far = self.piece(s_prev, core, half)
            push(far, far, "space", s_next, self.out[1], self.far)
            for at in range(2):
                part = self.piece(self.others[at], core, half)
                push(part, part, "view", y_next, self.out[2], self.y_near)

        def c(self):
            landed(self.bytes_of(48), self.far)
            part = self.piece(self.others[2], core, half)
            push(part, part, "view", y_next, self.out[2], self.y_far)

        def d(self):
            landed(self.bytes_of(96), self.y_near)
            for at in range(3):
                if at == 2:
                    landed(self.bytes_of(48), self.y_far)
                part = self.piece(self.others[at], core, 0, 96)
                push(part, part, "tm", sibling, self.out[3], self.sib)

        def e(self):
            landed(self.bytes_of(288), self.sib)

    g_a, g_b, g_c = Gather(0, 4), Gather(4, 6), Gather(6, 9)
    wos, wqv, wov = whole.at[0:1], whole.at[1:4], whole.at[4:5]
    wot, wqt = whole.at[5:6], whole.at[6:9]
    own = pl.ds(pl.multiple_of(s * LW, 16), LW)

    loads = [
        pltpu.make_async_copy(src, dst, local_sem.at[at])
        for at, (src, dst) in enumerate(
            (
                (x_in, xc.at[:, 0]),
                (wqs_in, wqs_ref),
                (cot_in, xc.at[:, 1]),
                (wos_in, wos.at[:, own, :]),
                (wqv_in, wqv.at[:, own, :]),
                (wov_in, wov.at[:, own, :]),
                (wot_in, wot.at[:, own, :]),
                (wqt_in, wqt.at[:, own, :]),
            )
        )
    ]
    for copy in loads:
        copy.start()

    barrier = pltpu.get_barrier_semaphore()
    for k in range(NSP):
        for j in range(NV):
            if k or j:
                pl.semaphore_signal(
                    barrier,
                    inc=1,
                    device_id={"view": plus(v, j, NV), "space": plus(s, k, NSP)},
                    device_id_type=MESH,
                )
    for k in range(1, NT_):
        pl.semaphore_signal(barrier, inc=1, device_id={"tm": plus(t, k, NT_)}, device_id_type=MESH)

    loads[0].wait()
    x_rows = xc[:, 0].reshape(TOK, D)
    normed, _ = rms(x_rows.astype(F32))
    nb[0] = normed.astype(BF)
    key_at = lax.broadcasted_iota(jnp.int32, (TOK, GH * TOK), 0)
    query_at = lax.broadcasted_iota(jnp.int32, (TOK, GH * TOK), 1)
    bias[...] = jnp.where(lax.rem(key_at, CH) == lax.rem(query_at, CH), 0.0, -1e30)
    lmask = head_masks(LW)
    gmask = head_masks(GW)
    pl.semaphore_wait(barrier, NSP * NV + NT_ - 2)

    halves = [slice(0, TOK // 2), slice(TOK // 2, TOK)]
    n_near, n_far = [ticket() for _ in halves], [ticket() for _ in halves]
    n_out = sending(nb.at[0:2]), sending(nb.at[0])
    for h, part in enumerate(halves):
        for k in (1, 3):
            push(nb.at[0, part], nb.at[k, part], "space", plus(s, k, NSP), n_out[0], n_near[h])
    for copy in loads[1:]:
        copy.wait()
    order = (4, 3, 5, 2, 6, 1, 7)
    x2_num, x2_out = ticket(), sending(xb.at[1:NV])
    for j in order:
        to = plus(v, j, NV)
        push(xc.at[to], xb.at[j], "view", to, x2_out, x2_num)
    xb[0] = xc[v]

    def project_space(k):
        tokens = nb[k]
        packed = dot(wqs_ref[...], tokens, NT)
        at = slice(k * TOK, (k + 1) * TOK)
        query = packed[:LW].astype(BF) * jnp.asarray(SCALE, BF)
        qts[:, k * LH * TOK : (k + 1) * LH * TOK] = stacked(query, lmask)
        kvt[:, at] = packed[LW:].astype(BF)
        k_nat[at, :] = jnp.transpose(packed[LW : 2 * LW]).astype(BF)
        v_nat[at, :] = jnp.transpose(packed[2 * LW :]).astype(BF)

    project_space(0)
    for h, part in enumerate(halves):
        landed(nb.at[0], n_near[h])
        push(nb.at[1 + 2 * core, part], nb.at[2, part], "space", s_next, n_out[1], n_far[h])
    g_a.a()
    project_space(1)
    project_space(3)
    for h, part in enumerate(halves):
        landed(nb.at[2, part], n_far[h])
    project_space(2)

    a_num = [ticket() for _ in range(NSP)]
    a_out = sending(ats.at[0, 1:NV]), sending(ats.at[1:NSP])

    def attend_space(k):
        at = slice(k * LH * TOK, (k + 1) * LH * TOK)
        shares = softmax0(dot(k_nat[...], qts[:, at], NN)).astype(BF)
        pts[:, at] = shares
        out = jnp.transpose(per_head(kvt[LW:, :], shares)).astype(BF)
        ats[k] = out.reshape(NV, CH, LW)

    def send_attended(k):
        for j in order + (0,):
            to = (plus(v, j, NV), plus(s, -k, NSP))
            if k or j:
                push(ats.at[k, to[0]], att.at[s, j], ("view", "space"), to, a_out[min(k, 1)], a_num[k])
            else:
                att[pl.ds(s, 1), 0:1] = ats[0:1, pl.ds(v, 1)]

    attend_space(2)
    attend_space(1)
    send_attended(2)
    send_attended(1)
    g_a.b()
    g_b.a()
    attend_space(3)
    attend_space(0)
    send_attended(3)
    send_attended(0)
    g_a.c()
    g_b.b()
    g_c.a()
    g_a.d()
    g_b.c()

    def slot_of(view):
        return lax.rem(v - view + NV, NV)

    g_b.d()
    landed(xb.at[1:NV], x2_num)
    for k in (2, 1, 3):
        landed(att.at[plus(s, k, NSP)], a_num[k])
    landed(att.at[s, 1:NV], a_num[0])
    c2_num, c2_out = ticket(), sending(c2.at[1:NT_])
    for m in tm_order:
        push(xb.at[slot_of(paired(m)), 1], c2.at[m], "tm", paired(m), c2_out, c2_num)
    c2[0] = xb[slot_of(t), 1]
    g_c.b()
    g_a.e()
    term = dot(att[0].reshape(TOK, LW), wos[0, :LW, :], NN)
    for h in range(1, NSP):
        term += dot(att[h].reshape(TOK, LW), wos[0, h * LW : (h + 1) * LW, :], NN)
    x2[...] = (xb[:, 0].reshape(TOK, D).astype(F32) + term).astype(BF).reshape(NV, CH, D)
    rows_view = x2[...].reshape(TOK, D)
    normed, _ = rms(rows_view.astype(F32))
    tokens = normed.astype(BF)

    def attend_small(w, g):
        lanes = slice(g * GW, (g + 1) * GW)
        query = dot(w[0, lanes, :], tokens, NT).astype(BF) * jnp.asarray(SCALE, BF)
        key_t = dot(w[1, lanes, :], tokens, NT).astype(BF)
        value_t = dot(w[2, lanes, :], tokens, NT).astype(BF)
        queries = stacked(query, gmask)
        shares = softmax0(dot(key_t, queries, TN) + bias[...]).astype(BF)
        return queries, key_t, value_t, shares

    def backward_small(queries, key_t, value, shares, grads):
        share_grad = dot(value, grads, NN)
        wide = shares.astype(F32)
        row_dot = jnp.sum(wide * share_grad, axis=0, keepdims=True)
        score_grad = (wide * (share_grad - row_dot)).astype(BF)
        query_grad = (per_head(key_t, score_grad) * SCALE).astype(BF)
        key_grad = dot(score_grad, queries, NT).astype(BF)
        value_grad = dot(shares, grads, NT).astype(BF)
        return jnp.transpose(query_grad), key_grad, value_grad

    def normed_grad_of(parts, w):
        columns = [part[at] for at in range(3) for part in parts]
        return dot(jnp.concatenate(columns, axis=1), w[...].reshape(3 * D, D), NN)

    outs = []
    for g in range(GROUPS):
        queries, key_t, value_t, shares = attend_small(wqv, g)
        qts_v[g], kt_v[g], vt_v[g], pt_v[g] = queries, key_t, value_t, shares
        outs.append(per_head(value_t, shares).astype(BF))
    g_c.c()
    g_b.e()
    term = dot(jnp.concatenate(outs, axis=0), wov[0], TN)
    xt[...] = (rows_view.astype(F32) + term).astype(BF).reshape(NV, CH, D)

    x3_num, x3_out = ticket(), sending(x3.at[1:NT_])
    for m in tm_order:
        push(xt.at[slot_of(paired(m))], x3.at[m], "tm", paired(m), x3_out, x3_num)
    x3[0] = xt[slot_of(t)]
    g_c.d()
    landed(c2.at[1:NT_], c2_num)
    upstream = c2[...].reshape(TOK, D)
    out_grads = dot(wot[0], upstream, NT).astype(BF)
    grads_t = [stacked(out_grads[g * GW : (g + 1) * GW], gmask) for g in range(GROUPS)]
    for g in range(GROUPS):
        v_v[g] = jnp.transpose(vt_v[g])
    landed(x3.at[1:NT_], x3_num)
    g_c.e()
    rows_time = x3[...].reshape(TOK, D)
    normed, factor = rms(rows_time.astype(F32))
    tokens = normed.astype(BF)

    parts = []
    for g in range(GROUPS):
        queries, key_t, value_t, shares = attend_small(wqt, g)
        parts.append(backward_small(queries, key_t, jnp.transpose(value_t), shares, grads_t[g]))
    total = normed_grad_of(parts, wqt)
    ut[...] = finish(upstream, normed, factor, total).reshape(NT_, CH, D)

    u2_num, u2_out = ticket(), sending(ut.at[1:NT_])
    here = slot_of(t)
    for m in tm_order:
        push(ut.at[m], u2.at[here], "tm", paired(m), u2_out, u2_num)
    u2[pl.ds(here, 1)] = ut[0:1]
    normed, factor = rms(x2[...].reshape(TOK, D).astype(F32))
    landed(u2.at[1:NT_], u2_num)
    upstream = u2[...].reshape(TOK, D)
    parts = []
    for g in range(GROUPS):
        out_grad = dot(wov[0, g * GW : (g + 1) * GW, :], upstream, NT).astype(BF)
        saved = qts_v[g], kt_v[g], v_v[g], pt_v[g]
        parts.append(backward_small(*saved, stacked(out_grad, gmask)))
    upstream = finish(upstream, normed, factor, normed_grad_of(parts, wqv))
    uv[...] = upstream.reshape(NV, CH, D)

    out_grad = dot(wos[0], upstream, NT)
    for h in range(NSP):
        part = jnp.transpose(out_grad[h * LW : (h + 1) * LW]).astype(BF)
        ogs[h] = part.reshape(NV, CH, LW)
    og_num = [ticket() for _ in range(NSP)]
    og_out = sending(ogs.at[0, 1:NV]), sending(ogs.at[1:NSP])
    for k in (2, 1, 3, 0):
        for j in order + (0,):
            to = (plus(v, -j, NV), plus(s, k, NSP))
            if k or j:
                push(ogs.at[to[1], j], og.at[k, v], ("view", "space"), to, og_out[min(k, 1)], og_num[k])
    og[0:1, pl.ds(v, 1)] = ogs[pl.ds(s, 1), 0:1]
    def backward_space(k):
        at = slice(k * LH * TOK, (k + 1) * LH * TOK)
        out_grad = og[k].reshape(TOK, LW)
        grads = jnp.concatenate([out_grad * m for m in nmask], axis=0)
        ogts[at, :] = grads
        share_grad = dot(v_nat[...], grads, NT)
        wide = pts[:, at].astype(F32)
        row_dot = jnp.sum(wide * share_grad, axis=0, keepdims=True)
        score_grad = (wide * (share_grad - row_dot)).astype(BF)
        gts[:, at] = score_grad
        dqt[k] = (per_head(kvt[:LW, :], score_grad) * SCALE).astype(BF)

    head_at = lax.broadcasted_iota(jnp.int32, (TOK, LW), 1) // HD
    nmask = [(head_at == h).astype(F32).astype(BF) for h in range(LH)]
    u3_num, u3_out = ticket(), sending(uv.at[1:NV])
    landed(og.at[0, 1:NV], og_num[0])
    landed(og.at[1], og_num[1])
    backward_space(0)
    backward_space(1)
    landed(og.at[3], og_num[3])
    landed(og.at[2], og_num[2])
    for j in order:
        push(uv.at[j], u3.at[v], "view", plus(v, -j, NV), u3_out, u3_num)
    backward_space(3)
    backward_space(2)
    u3[pl.ds(v, 1)] = uv[0:1]

    def partial_sums(k):
        at = pl.ds(pl.multiple_of(k * TOK, TOK), TOK)
        key_grad = dot(gts[at, :], qts[...], NT).astype(BF)
        value_grad = dot(pts[at, :], ogts[...], NN).astype(BF)
        part = dot(dqt[k], wqs_ref[:LW, :], TN)
        part += dot(key_grad, wqs_ref[LW : 2 * LW, :], NN)
        return part + dot(value_grad, wqs_ref[2 * LW :, :], NN)

    rf_num, near_num, late_num = ticket(), ticket(), ticket()
    rs_out = sending(rsend)
    rsend[0] = partial_sums(2).astype(BF)
    push(rsend.at[0], rf, "space", s_next, rs_out, rf_num)
    rsend[1] = partial_sums(1 + 2 * core).astype(BF)
    push(rsend.at[1], rs.at[0], "space", s_prev, rs_out, near_num)
    late = partial_sums(3 - 2 * core)
    total = partial_sums(0)
    landed(rf, rf_num)
    rsend[2] = (late + rf[...].astype(F32)).astype(BF)
    push(rsend.at[2], rs.at[1], "space", s_next, rs_out, late_num)
    normed, factor = rms(xc[:, 0].reshape(TOK, D).astype(F32))
    landed(rs.at[0], near_num)
    total += rs[0].astype(F32)
    landed(rs.at[1], late_num)
    total += rs[1].astype(F32)
    landed(u3.at[1:NV], u3_num)
    out_ref[...] = finish(u3[...].reshape(TOK, D), normed, factor, total)

    for ref, number in left:
        remote(ref, ref, "tm", sibling, number, 0).wait_send()


def on_device(latents, cotangent, wqs, wos, wqv, wov, wqt, wot):
    vmem = pl.BlockSpec(memory_space=pltpu.VMEM)
    hbm = pl.BlockSpec(memory_space=pltpu.HBM)

    def buf(*shape, dtype=BF):
        return pltpu.VMEM(shape, dtype)

    wide = NSP * LH * TOK
    out = pl.pallas_call(
        body,
        out_shape=jax.ShapeDtypeStruct((TOK, D), BF),
        in_specs=[hbm] * 8,
        out_specs=vmem,
        scratch_shapes=[
            buf(NV, 2, CH, D),
            buf(3 * LW, D),
            buf(NSP, TOK, D),
            buf(NSP * TOK, LW),
            buf(NSP * TOK, LW),
            buf(LW, wide),
            buf(2 * LW, NSP * TOK),
            buf(NSP * TOK, wide),
            buf(NSP * TOK, wide),
            buf(wide, LW),
            buf(NSP, LW, TOK),
            buf(NSP, NV, CH, LW),
            buf(NSP, NV, CH, LW),
        ]
        + [buf(NV, 2, CH, D)]
        + [buf(NV, CH, D)] * 8
        + [
            buf(NSP, NV, CH, LW),
            buf(NSP, NV, CH, LW),
            buf(3, TOK, D),
            buf(2, TOK, D),
            buf(TOK, D),
            buf(TOK, GH * TOK, dtype=F32),
            buf(GROUPS, GW, TOK),
            buf(GROUPS, GW, TOK),
            buf(GROUPS, TOK, GW),
            buf(GROUPS, GW, GH * TOK),
            buf(GROUPS, TOK, GH * TOK),
            buf(9, D, D),
            pltpu.SemaphoreType.DMA((NSEM,)),
            pltpu.SemaphoreType.DMA((NSEM,)),
            pltpu.SemaphoreType.DMA((8,)),
        ],
        compiler_params=pltpu.CompilerParams(
            collective_id=0, has_side_effects=True, vmem_limit_bytes=60 * 1024 * 1024
        ),
        name="block_backward",
    )(
        latents.reshape(NV, CH, D),
        cotangent.reshape(NV, CH, D),
        wqs.reshape(3 * LW, D),
        wos[None],
        wqv,
        wov[None],
        wqt,
        wot[None],
    )
    return out[None, None]


def solution(mesh):
    in_specs = (
        P("view", "tm", "space", None),
        P("view", "tm", "space", None),
        P(None, "space", None),
        P("space", None),
        P(None, "space", None),
        P("space", None),
        P(None, "space", None),
        P("space", None),
    )
    return jax.shard_map(
        on_device,
        mesh=mesh,
        in_specs=in_specs,
        out_specs=P("view", "tm", "space", None),
        check_vma=False,
    )
```

```python
import jax
import jax.numpy as jnp
from jax import lax
from jax.experimental import pallas as pl
from jax.experimental.pallas import tpu as pltpu
from jax.sharding import PartitionSpec as P

MESH = pl.DeviceIdType.MESH
BF = jnp.bfloat16
F32 = jnp.float32
NN = ((1,), (0,))
NT = ((1,), (1,))
TN = ((0,), (0,))

D = 768
TOK = 128
NSP = 4
NV = 8
NT_ = 8
CH = 16
HD = 64
LH = 3
LW = LH * HD
GH = 4
GW = GH * HD
GROUPS = D // GW
SCALE = HD**-0.5
NSEM = 64
VMEM = 859 * 65536


def dot(a, b, dims):
    return lax.dot_general(a, b, (dims, ((), ())), preferred_element_type=F32)


def rms(values):
    factor = lax.rsqrt(jnp.mean(values * values, axis=-1, keepdims=True) + 1e-06)
    return values * factor, factor


def finish(upstream, normed, factor, normed_grad):
    inner = jnp.mean(normed_grad * normed, axis=-1, keepdims=True)
    return (upstream.astype(F32) + factor * (normed_grad - normed * inner)).astype(BF)


def softmax0(scores):
    top = jnp.max(scores, axis=0, keepdims=True)
    expo = jnp.exp(scores - top)
    return expo * (1.0 / jnp.sum(expo, axis=0, keepdims=True))


def head_masks(rows):
    head = lax.broadcasted_iota(jnp.int32, (rows, TOK), 0) // HD
    return [(head == h).astype(F32).astype(BF) for h in range(rows // HD)]


def stacked(values, masks):
    return jnp.concatenate([values * m for m in masks], axis=1)


def per_head(left, right):
    heads = left.shape[0] // HD
    return jnp.concatenate(
        [
            dot(left[h * HD : (h + 1) * HD], right[:, h * TOK : (h + 1) * TOK], NN)
            for h in range(heads)
        ],
        axis=0,
    )


def body(
    x_in, cot_in, wqs_in, wos_in, wqv_in, wov_in, wqt_in, wot_in,
    out_ref,
    xc, wqs_ref,
    nb, k_nat, v_nat, qts, kvt, pts, gts, ogts, dqt, ats, att,
    xb, x2, xt, x3, c2, ut, u2, uv, u3, ogs, og, rsend, rs, rf,
    bias, kt_v, vt_v, v_v, qts_v, pt_v,
    whole,
    send_sem, recv_sem, local_sem,
):
    t = lax.axis_index("tm")
    v = lax.axis_index("view")
    s = lax.axis_index("space")
    core = lax.rem(t, 2)
    sibling = t + 1 - 2 * core
    y = lax.rem(v, 4)
    half = lax.rem(y, 2)
    step = 1 - 2 * core
    y_next = v - y + lax.rem(y + step + 4, 4)
    s_next = lax.rem(s + step + 4, 4)
    s_prev = lax.rem(s - step + 4, 4)

    def plus(me, k, n):
        return lax.rem(me + k + n, n)

    bits = [t % 2, t // 2 % 2, t // 4]

    def paired(m):
        return t + sum((1 - 2 * bits[at]) * 2**at for at in range(3) if m >> at & 1)

    tm_order = (6, 7, 4, 5, 2, 3, 1)
    left = []
    count = [0]

    def ticket():
        count[0] += 1
        return count[0] - 1

    def remote(src, dst, axis, index, number, arrival):
        to = {axis: index} if isinstance(axis, str) else dict(zip(axis, index))
        return pltpu.make_async_remote_copy(
            src_ref=src,
            dst_ref=dst,
            send_sem=send_sem.at[number],
            recv_sem=recv_sem.at[arrival],
            device_id=to,
            device_id_type=MESH,
        )

    def push(src, dst, axis, index, number, arrival):
        remote(src, dst, axis, index, number, arrival).start()

    def landed(ref, arrival):
        remote(ref, ref, "tm", sibling, 0, arrival).wait_recv()

    def gone(ref, number):
        remote(ref, ref, "tm", sibling, number, 0).wait_send()

    def sending(ref):
        left.append((ref, ticket()))
        return left[-1][1]

    def rows(owner, c, h, size):
        return pl.ds(pl.multiple_of(owner * LW + c * 96 + h * 48, 16), size)

    class Gather:
        def __init__(self, first, end):
            self.first, self.end = first, end
            self.others = [plus(s, -1, 4), plus(s, 1, 4), plus(s, 2, 4)]
            self.out = [sending(self.bytes_of(size)) for size in (96, 48, 144, 288)]
            self.near, self.far, self.y_near, self.y_far, self.sib = [ticket() for _ in range(5)]

        def bytes_of(self, size):
            return whole.at[self.first : self.end, 0:size, :]

        def piece(self, owner, c, h, size=48):
            return whole.at[self.first : self.end, rows(owner, c, h, size), :]

        def a(self):
            mine = self.piece(s, core, half)
            push(mine, mine, "space", plus(s, 1, 4), self.out[0], self.near)
            push(mine, mine, "space", plus(s, -1, 4), self.out[0], self.near)

        def b(self):
            landed(self.bytes_of(96), self.near)
            far = self.piece(s_prev, core, half)
            push(far, far, "space", s_next, self.out[1], self.far)
            for at in range(2):
                part = self.piece(self.others[at], core, half)
                push(part, part, "view", y_next, self.out[2], self.y_near)

        def c(self):
            landed(self.bytes_of(48), self.far)
            part = self.piece(self.others[2], core, half)
            push(part, part, "view", y_next, self.out[2], self.y_far)

        def d(self):
            landed(self.bytes_of(96), self.y_near)
            for at in range(3):
                if at == 2:
                    landed(self.bytes_of(48), self.y_far)
                part = self.piece(self.others[at], core, 0, 96)
                push(part, part, "tm", sibling, self.out[3], self.sib)

        def e(self):
            landed(self.bytes_of(288), self.sib)

    g_a, g_b, g_c = Gather(0, 4), Gather(4, 6), Gather(6, 9)
    wos, wqv, wov = whole.at[0:1], whole.at[1:4], whole.at[4:5]
    wot, wqt = whole.at[5:6], whole.at[6:9]
    own = pl.ds(pl.multiple_of(s * LW, 16), LW)

    loads = [
        pltpu.make_async_copy(src, dst, local_sem.at[at])
        for at, (src, dst) in enumerate(
            (
                (x_in, xc.at[:, 0]),
                (wqs_in, wqs_ref),
                (cot_in, xc.at[:, 1]),
                (wos_in, wos.at[:, own, :]),
                (wqv_in, wqv.at[:, own, :]),
                (wov_in, wov.at[:, own, :]),
                (wot_in, wot.at[:, own, :]),
                (wqt_in, wqt.at[:, own, :]),
            )
        )
    ]
    for copy in loads:
        copy.start()

    barrier = pltpu.get_barrier_semaphore()
    for k in range(NSP):
        for j in range(NV):
            if k or j:
                pl.semaphore_signal(
                    barrier,
                    inc=1,
                    device_id={"view": plus(v, j, NV), "space": plus(s, k, NSP)},
                    device_id_type=MESH,
                )
    for k in range(1, NT_):
        pl.semaphore_signal(barrier, inc=1, device_id={"tm": plus(t, k, NT_)}, device_id_type=MESH)

    loads[0].wait()
    x_rows = xc[:, 0].reshape(TOK, D)
    normed, _ = rms(x_rows.astype(F32))
    nb[0] = normed.astype(BF)
    key_at = lax.broadcasted_iota(jnp.int32, (TOK, GH * TOK), 0)
    query_at = lax.broadcasted_iota(jnp.int32, (TOK, GH * TOK), 1)
    bias[...] = jnp.where(lax.rem(key_at, CH) == lax.rem(query_at, CH), 0.0, -1e30)
    lmask = head_masks(LW)
    gmask = head_masks(GW)
    pl.semaphore_wait(barrier, NSP * NV + NT_ - 2)

    halves = [slice(0, TOK // 2), slice(TOK // 2, TOK)]
    n_near, n_far = [ticket() for _ in halves], [ticket() for _ in halves]
    n_out = sending(nb.at[0:2]), sending(nb.at[0])
    for h, part in enumerate(halves):
        for k in (1, 3):
            push(nb.at[0, part], nb.at[k, part], "space", plus(s, k, NSP), n_out[0], n_near[h])
    for copy in loads[1:]:
        copy.wait()
    order = (4, 3, 5, 2, 6, 1, 7)
    x2_num, x2_out = ticket(), sending(xb.at[1:NV])
    for j in order:
        to = plus(v, j, NV)
        push(xc.at[to], xb.at[j], "view", to, x2_out, x2_num)
    xb[0] = xc[v]

    def project_space(k):
        tokens = nb[k]
        packed = dot(wqs_ref[...], tokens, NT)
        at = slice(k * TOK, (k + 1) * TOK)
        query = packed[:LW].astype(BF) * jnp.asarray(SCALE, BF)
        qts[:, k * LH * TOK : (k + 1) * LH * TOK] = stacked(query, lmask)
        kvt[:, at] = packed[LW:].astype(BF)
        k_nat[at, :] = jnp.transpose(packed[LW : 2 * LW]).astype(BF)
        v_nat[at, :] = jnp.transpose(packed[2 * LW :]).astype(BF)

    project_space(0)
    for h, part in enumerate(halves):
        landed(nb.at[0], n_near[h])
        push(nb.at[1 + 2 * core, part], nb.at[2, part], "space", s_next, n_out[1], n_far[h])
    g_a.a()
    project_space(1)
    project_space(3)
    for h, part in enumerate(halves):
        landed(nb.at[2, part], n_far[h])
    project_space(2)

    a_num = [ticket() for _ in range(NSP)]
    a_out = sending(ats.at[0, 1:NV]), sending(ats.at[1:NSP])

    def attend_space(k):
        at = slice(k * LH * TOK, (k + 1) * LH * TOK)
        shares = softmax0(dot(k_nat[...], qts[:, at], NN)).astype(BF)
        pts[:, at] = shares
        out = jnp.transpose(per_head(kvt[LW:, :], shares)).astype(BF)
        ats[k] = out.reshape(NV, CH, LW)

    def send_attended(k):
        for j in order + (0,):
            to = (plus(v, j, NV), plus(s, -k, NSP))
            if k or j:
                push(ats.at[k, to[0]], att.at[s, j], ("view", "space"), to, a_out[min(k, 1)], a_num[k])
            else:
                att[pl.ds(s, 1), 0:1] = ats[0:1, pl.ds(v, 1)]

    attend_space(2)
    attend_space(1)
    send_attended(2)
    send_attended(1)
    g_a.b()
    g_b.a()
    attend_space(3)
    attend_space(0)
    send_attended(3)
    send_attended(0)
    g_a.c()
    g_b.b()
    g_c.a()
    g_a.d()
    g_b.c()

    def slot_of(view):
        return lax.rem(v - view + NV, NV)

    g_b.d()
    landed(xb.at[1:NV], x2_num)
    for k in (2, 1, 3):
        landed(att.at[plus(s, k, NSP)], a_num[k])
    landed(att.at[s, 1:NV], a_num[0])
    c2_num, c2_out = ticket(), sending(c2.at[1:NT_])
    for m in tm_order:
        push(xb.at[slot_of(paired(m)), 1], c2.at[m], "tm", paired(m), c2_out, c2_num)
    c2[0] = xb[slot_of(t), 1]
    g_c.b()
    g_a.e()
    term = dot(att[0].reshape(TOK, LW), wos[0, :LW, :], NN)
    for h in range(1, NSP):
        term += dot(att[h].reshape(TOK, LW), wos[0, h * LW : (h + 1) * LW, :], NN)
    x2[...] = (xb[:, 0].reshape(TOK, D).astype(F32) + term).astype(BF).reshape(NV, CH, D)
    rows_view = x2[...].reshape(TOK, D)
    normed, _ = rms(rows_view.astype(F32))
    tokens = normed.astype(BF)

    def attend_small(w, g):
        lanes = slice(g * GW, (g + 1) * GW)
        query = dot(w[0, lanes, :], tokens, NT).astype(BF) * jnp.asarray(SCALE, BF)
        key_t = dot(w[1, lanes, :], tokens, NT).astype(BF)
        value_t = dot(w[2, lanes, :], tokens, NT).astype(BF)
        queries = stacked(query, gmask)
        shares = softmax0(dot(key_t, queries, TN) + bias[...]).astype(BF)
        return queries, key_t, value_t, shares

    def backward_small(queries, key_t, value, shares, grads):
        share_grad = dot(value, grads, NN)
        wide = shares.astype(F32)
        row_dot = jnp.sum(wide * share_grad, axis=0, keepdims=True)
        score_grad = (wide * (share_grad - row_dot)).astype(BF)
        query_grad = (per_head(key_t, score_grad) * SCALE).astype(BF)
        key_grad = dot(score_grad, queries, NT).astype(BF)
        value_grad = dot(shares, grads, NT).astype(BF)
        return jnp.transpose(query_grad), key_grad, value_grad

    def normed_grad_of(parts, w):
        columns = [part[at] for at in range(3) for part in parts]
        return dot(jnp.concatenate(columns, axis=1), w[...].reshape(3 * D, D), NN)

    outs = []
    for g in range(GROUPS):
        queries, key_t, value_t, shares = attend_small(wqv, g)
        qts_v[g], kt_v[g], vt_v[g], pt_v[g] = queries, key_t, value_t, shares
        outs.append(per_head(value_t, shares).astype(BF))
    g_c.c()
    g_b.e()
    term = dot(jnp.concatenate(outs, axis=0), wov[0], TN)
    xt[...] = (rows_view.astype(F32) + term).astype(BF).reshape(NV, CH, D)

    x3_num, x3_out = ticket(), sending(x3.at[1:NT_])
    for m in tm_order:
        push(xt.at[slot_of(paired(m))], x3.at[m], "tm", paired(m), x3_out, x3_num)
    x3[0] = xt[slot_of(t)]
    g_c.d()
    landed(c2.at[1:NT_], c2_num)
    upstream = c2[...].reshape(TOK, D)
    out_grads = dot(wot[0], upstream, NT).astype(BF)
    grads_t = [stacked(out_grads[g * GW : (g + 1) * GW], gmask) for g in range(GROUPS)]
    for g in range(GROUPS):
        v_v[g] = jnp.transpose(vt_v[g])
    landed(x3.at[1:NT_], x3_num)
    g_c.e()
    rows_time = x3[...].reshape(TOK, D)
    normed, factor = rms(rows_time.astype(F32))
    tokens = normed.astype(BF)

    parts = []
    for g in range(GROUPS):
        queries, key_t, value_t, shares = attend_small(wqt, g)
        parts.append(backward_small(queries, key_t, jnp.transpose(value_t), shares, grads_t[g]))
    total = normed_grad_of(parts, wqt)
    ut[...] = finish(upstream, normed, factor, total).reshape(NT_, CH, D)

    u2_num, u2_out = ticket(), sending(ut.at[1:NT_])
    here = slot_of(t)
    for m in tm_order:
        push(ut.at[m], u2.at[here], "tm", paired(m), u2_out, u2_num)
    u2[pl.ds(here, 1)] = ut[0:1]
    normed, factor = rms(x2[...].reshape(TOK, D).astype(F32))
    for ref, number in left[:-1]:
        gone(ref, number)
    del left[:-1]
    landed(u2.at[1:NT_], u2_num)
    upstream = u2[...].reshape(TOK, D)
    parts = []
    for g in range(GROUPS):
        out_grad = dot(wov[0, g * GW : (g + 1) * GW, :], upstream, NT).astype(BF)
        saved = qts_v[g], kt_v[g], v_v[g], pt_v[g]
        parts.append(backward_small(*saved, stacked(out_grad, gmask)))
    upstream = finish(upstream, normed, factor, normed_grad_of(parts, wqv))
    uv[...] = upstream.reshape(NV, CH, D)

    out_grad = dot(wos[0], upstream, NT)
    for h in range(NSP):
        part = jnp.transpose(out_grad[h * LW : (h + 1) * LW]).astype(BF)
        ogs[h] = part.reshape(NV, CH, LW)
    og_num = [ticket() for _ in range(NSP)]
    og_out = sending(ogs.at[0, 1:NV]), sending(ogs.at[1:NSP])
    for k in (2, 1, 3, 0):
        for j in order + (0,):
            to = (plus(v, -j, NV), plus(s, k, NSP))
            if k or j:
                push(ogs.at[to[1], j], og.at[k, v], ("view", "space"), to, og_out[min(k, 1)], og_num[k])
    og[0:1, pl.ds(v, 1)] = ogs[pl.ds(s, 1), 0:1]
    def backward_space(k):
        at = slice(k * LH * TOK, (k + 1) * LH * TOK)
        out_grad = og[k].reshape(TOK, LW)
        grads = jnp.concatenate([out_grad * m for m in nmask], axis=0)
        ogts[at, :] = grads
        share_grad = dot(v_nat[...], grads, NT)
        wide = pts[:, at].astype(F32)
        row_dot = jnp.sum(wide * share_grad, axis=0, keepdims=True)
        score_grad = (wide * (share_grad - row_dot)).astype(BF)
        gts[:, at] = score_grad
        dqt[k] = (per_head(kvt[:LW, :], score_grad) * SCALE).astype(BF)

    head_at = lax.broadcasted_iota(jnp.int32, (TOK, LW), 1) // HD
    nmask = [(head_at == h).astype(F32).astype(BF) for h in range(LH)]
    u3_num, u3_out = ticket(), sending(uv.at[1:NV])
    landed(og.at[0, 1:NV], og_num[0])
    landed(og.at[1], og_num[1])
    backward_space(0)
    backward_space(1)
    landed(og.at[3], og_num[3])
    landed(og.at[2], og_num[2])
    for j in order:
        push(uv.at[j], u3.at[v], "view", plus(v, -j, NV), u3_out, u3_num)
    backward_space(3)
    backward_space(2)
    u3[pl.ds(v, 1)] = uv[0:1]

    def partial_sums(k):
        at = pl.ds(pl.multiple_of(k * TOK, TOK), TOK)
        key_grad = dot(gts[at, :], qts[...], NT).astype(BF)
        value_grad = dot(pts[at, :], ogts[...], NN).astype(BF)
        part = dot(dqt[k], wqs_ref[:LW, :], TN)
        part += dot(key_grad, wqs_ref[LW : 2 * LW, :], NN)
        return part + dot(value_grad, wqs_ref[2 * LW :, :], NN)

    rf_num, late_num = [ticket() for _ in halves], [ticket() for _ in halves]
    near_num = ticket()
    rs_out = sending(rsend)
    rsend[0] = partial_sums(2).astype(BF)
    for h, part in enumerate(halves):
        push(rsend.at[0, part], rf.at[part], "space", s_next, rs_out, rf_num[h])
    rsend[1] = partial_sums(1 + 2 * core).astype(BF)
    push(rsend.at[1], rs.at[0], "space", s_prev, rs_out, near_num)
    late = partial_sums(3 - 2 * core)
    total = partial_sums(0)
    normed, factor = rms(xc[:, 0].reshape(TOK, D).astype(F32))
    for h, part in enumerate(halves):
        landed(rf.at[part], rf_num[h])
        rsend[2, part] = (late[part] + rf[part].astype(F32)).astype(BF)
        push(rsend.at[2, part], rs.at[1, part], "space", s_next, rs_out, late_num[h])
    landed(rs.at[0], near_num)
    total += rs[0].astype(F32)
    for h, part in enumerate(halves):
        landed(rs.at[1, part], late_num[h])
    total += rs[1].astype(F32)
    landed(u3.at[1:NV], u3_num)
    out_ref[...] = finish(u3[...].reshape(TOK, D), normed, factor, total)

    for ref, number in left:
        gone(ref, number)


def on_device(latents, cotangent, wqs, wos, wqv, wov, wqt, wot):
    vmem = pl.BlockSpec(memory_space=pltpu.VMEM)
    hbm = pl.BlockSpec(memory_space=pltpu.HBM)

    def buf(*shape, dtype=BF):
        return pltpu.VMEM(shape, dtype)

    wide = NSP * LH * TOK
    out = pl.pallas_call(
        body,
        out_shape=jax.ShapeDtypeStruct((TOK, D), BF),
        in_specs=[hbm] * 8,
        out_specs=vmem,
        scratch_shapes=[
            buf(NV, 2, CH, D),
            buf(3 * LW, D),
            buf(NSP, TOK, D),
            buf(NSP * TOK, LW),
            buf(NSP * TOK, LW),
            buf(LW, wide),
            buf(2 * LW, NSP * TOK),
            buf(NSP * TOK, wide),
            buf(NSP * TOK, wide),
            buf(wide, LW),
            buf(NSP, LW, TOK),
            buf(NSP, NV, CH, LW),
            buf(NSP, NV, CH, LW),
        ]
        + [buf(NV, 2, CH, D)]
        + [buf(NV, CH, D)] * 8
        + [
            buf(NSP, NV, CH, LW),
            buf(NSP, NV, CH, LW),
            buf(3, TOK, D),
            buf(2, TOK, D),
            buf(TOK, D),
            buf(TOK, GH * TOK, dtype=F32),
            buf(GROUPS, GW, TOK),
            buf(GROUPS, GW, TOK),
            buf(GROUPS, TOK, GW),
            buf(GROUPS, GW, GH * TOK),
            buf(GROUPS, TOK, GH * TOK),
            buf(9, D, D),
            pltpu.SemaphoreType.DMA((NSEM,)),
            pltpu.SemaphoreType.DMA((NSEM,)),
            pltpu.SemaphoreType.DMA((8,)),
        ],
        compiler_params=pltpu.CompilerParams(
            collective_id=0, has_side_effects=True, vmem_limit_bytes=VMEM
        ),
        name="block_backward",
    )(
        latents.reshape(NV, CH, D),
        cotangent.reshape(NV, CH, D),
        wqs.reshape(3 * LW, D),
        wos[None],
        wqv,
        wov[None],
        wqt,
        wot[None],
    )
    return out[None, None]


def solution(mesh):
    in_specs = (
        P("view", "tm", "space", None),
        P("view", "tm", "space", None),
        P(None, "space", None),
        P("space", None),
        P(None, "space", None),
        P("space", None),
        P(None, "space", None),
        P("space", None),
    )
    return jax.shard_map(
        on_device,
        mesh=mesh,
        in_specs=in_specs,
        out_specs=P("view", "tm", "space", None),
        check_vma=False,
    )
```

```python
import jax
import jax.numpy as jnp
from jax import lax
from jax.experimental import pallas as pl
from jax.experimental.pallas import tpu as pltpu
from jax.sharding import PartitionSpec as P

MESH = pl.DeviceIdType.MESH
BF = jnp.bfloat16
F32 = jnp.float32
NN = ((1,), (0,))
NT = ((1,), (1,))
TN = ((0,), (0,))

D = 768
TOK = 128
NSP = 4
NV = 8
NT_ = 8
CH = 16
HD = 64
LH = 3
LW = LH * HD
GH = 4
GW = GH * HD
GROUPS = D // GW
SCALE = HD**-0.5
NSEM = 64
VMEM = 859 * 65536


def dot(a, b, dims):
    return lax.dot_general(a, b, (dims, ((), ())), preferred_element_type=F32)


def rms(values):
    factor = lax.rsqrt(jnp.mean(values * values, axis=-1, keepdims=True) + 1e-06)
    return values * factor, factor


def finish(upstream, normed, factor, normed_grad):
    inner = jnp.mean(normed_grad * normed, axis=-1, keepdims=True)
    return (upstream.astype(F32) + factor * (normed_grad - normed * inner)).astype(BF)


def softmax0(scores):
    top = jnp.max(scores, axis=0, keepdims=True)
    expo = jnp.exp(scores - top)
    return expo * (1.0 / jnp.sum(expo, axis=0, keepdims=True))


def head_masks(rows):
    head = lax.broadcasted_iota(jnp.int32, (rows, TOK), 0) // HD
    return [(head == h).astype(F32).astype(BF) for h in range(rows // HD)]


def stacked(values, masks):
    return jnp.concatenate([values * m for m in masks], axis=1)


def per_head(left, right):
    heads = left.shape[0] // HD
    return jnp.concatenate(
        [
            dot(left[h * HD : (h + 1) * HD], right[:, h * TOK : (h + 1) * TOK], NN)
            for h in range(heads)
        ],
        axis=0,
    )


def body(
    x_in, cot_in, wqs_in, wos_in, wqv_in, wov_in, wqt_in, wot_in,
    out_ref,
    xc, wqs_ref,
    nb, k_nat, v_nat, qts, kvt, pts, gts, ogts, dqt, ats, att,
    xb, x2, xt, x3, c2, ut, u2, uv, u3, ogs, og, rsend, rs, rf,
    bias, kt_v, vt_v, v_v, qts_v, pt_v,
    whole,
    send_sem, recv_sem, local_sem,
):
    t = lax.axis_index("tm")
    v = lax.axis_index("view")
    s = lax.axis_index("space")
    core = lax.rem(t, 2)
    sibling = t + 1 - 2 * core
    y = lax.rem(v, 4)
    half = lax.rem(y, 2)
    step = 1 - 2 * core
    y_next = v - y + lax.rem(y + step + 4, 4)
    s_next = lax.rem(s + step + 4, 4)
    s_prev = lax.rem(s - step + 4, 4)

    def plus(me, k, n):
        return lax.rem(me + k + n, n)

    bits = [t % 2, t // 2 % 2, t // 4]

    def paired(m):
        return t + sum((1 - 2 * bits[at]) * 2**at for at in range(3) if m >> at & 1)

    tm_order = (6, 7, 4, 5, 2, 3, 1)
    left = []
    count = [0]

    def ticket():
        count[0] += 1
        return count[0] - 1

    def remote(src, dst, axis, index, number, arrival):
        to = {axis: index} if isinstance(axis, str) else dict(zip(axis, index))
        return pltpu.make_async_remote_copy(
            src_ref=src,
            dst_ref=dst,
            send_sem=send_sem.at[number],
            recv_sem=recv_sem.at[arrival],
            device_id=to,
            device_id_type=MESH,
        )

    def push(src, dst, axis, index, number, arrival):
        remote(src, dst, axis, index, number, arrival).start()

    def landed(ref, arrival):
        remote(ref, ref, "tm", sibling, 0, arrival).wait_recv()

    def gone(ref, number):
        remote(ref, ref, "tm", sibling, number, 0).wait_send()

    def sending(ref):
        left.append((ref, ticket()))
        return left[-1][1]

    def rows(owner, c, h, size):
        return pl.ds(pl.multiple_of(owner * LW + c * 96 + h * 48, 16), size)

    class Gather:
        def __init__(self, first, end):
            self.first, self.end = first, end
            self.others = [plus(s, -1, 4), plus(s, 1, 4), plus(s, 2, 4)]
            self.out = [sending(self.bytes_of(size)) for size in (96, 48, 144, 288)]
            self.near, self.far, self.y_near, self.y_far, self.sib = [ticket() for _ in range(5)]

        def bytes_of(self, size):
            return whole.at[self.first : self.end, 0:size, :]

        def piece(self, owner, c, h, size=48):
            return whole.at[self.first : self.end, rows(owner, c, h, size), :]

        def a(self):
            mine = self.piece(s, core, half)
            push(mine, mine, "space", plus(s, 1, 4), self.out[0], self.near)
            push(mine, mine, "space", plus(s, -1, 4), self.out[0], self.near)

        def b(self):
            landed(self.bytes_of(96), self.near)
            far = self.piece(s_prev, core, half)
            push(far, far, "space", s_next, self.out[1], self.far)
            for at in range(2):
                part = self.piece(self.others[at], core, half)
                push(part, part, "view", y_next, self.out[2], self.y_near)

        def c(self):
            landed(self.bytes_of(48), self.far)
            part = self.piece(self.others[2], core, half)
            push(part, part, "view", y_next, self.out[2], self.y_far)

        def d(self):
            landed(self.bytes_of(96), self.y_near)
            for at in range(3):
                if at == 2:
                    landed(self.bytes_of(48), self.y_far)
                part = self.piece(self.others[at], core, 0, 96)
                push(part, part, "tm", sibling, self.out[3], self.sib)

        def e(self):
            landed(self.bytes_of(288), self.sib)

    g_a, g_b, g_c = Gather(0, 4), Gather(4, 6), Gather(6, 9)
    wos, wqv, wov = whole.at[0:1], whole.at[1:4], whole.at[4:5]
    wot, wqt = whole.at[5:6], whole.at[6:9]
    own = pl.ds(pl.multiple_of(s * LW, 16), LW)

    loads = [
        pltpu.make_async_copy(src, dst, local_sem.at[at])
        for at, (src, dst) in enumerate(
            (
                (x_in, xc.at[:, 0]),
                (wqs_in, wqs_ref),
                (cot_in, xc.at[:, 1]),
                (wos_in, wos.at[:, own, :]),
                (wqv_in, wqv.at[:, own, :]),
                (wov_in, wov.at[:, own, :]),
                (wot_in, wot.at[:, own, :]),
                (wqt_in, wqt.at[:, own, :]),
            )
        )
    ]
    for copy in loads:
        copy.start()

    barrier = pltpu.get_barrier_semaphore()
    for k in range(NSP):
        for j in range(NV):
            if k or j:
                pl.semaphore_signal(
                    barrier,
                    inc=1,
                    device_id={"view": plus(v, j, NV), "space": plus(s, k, NSP)},
                    device_id_type=MESH,
                )
    for k in range(1, NT_):
        pl.semaphore_signal(barrier, inc=1, device_id={"tm": plus(t, k, NT_)}, device_id_type=MESH)

    loads[0].wait()
    x_rows = xc[:, 0].reshape(TOK, D)
    normed, _ = rms(x_rows.astype(F32))
    nb[0] = normed.astype(BF)
    key_at = lax.broadcasted_iota(jnp.int32, (TOK, GH * TOK), 0)
    query_at = lax.broadcasted_iota(jnp.int32, (TOK, GH * TOK), 1)
    bias[...] = jnp.where(lax.rem(key_at, CH) == lax.rem(query_at, CH), 0.0, -1e30)
    lmask = head_masks(LW)
    gmask = head_masks(GW)
    pl.semaphore_wait(barrier, NSP * NV + NT_ - 2)

    halves = [slice(0, TOK // 2), slice(TOK // 2, TOK)]
    n_near, n_far = [ticket() for _ in halves], [ticket() for _ in halves]
    n_out = sending(nb.at[0:2]), sending(nb.at[0])
    for h, part in enumerate(halves):
        for k in (1, 3):
            push(nb.at[0, part], nb.at[k, part], "space", plus(s, k, NSP), n_out[0], n_near[h])
    for copy in loads[1:]:
        copy.wait()
    order = (4, 3, 5, 2, 6, 1, 7)
    x2_num, x2_out = ticket(), sending(xb.at[1:NV])
    for j in order:
        to = plus(v, j, NV)
        push(xc.at[to], xb.at[j], "view", to, x2_out, x2_num)
    xb[0] = xc[v]

    def project_space(k):
        tokens = nb[k]
        packed = dot(wqs_ref[...], tokens, NT)
        at = slice(k * TOK, (k + 1) * TOK)
        query = packed[:LW].astype(BF) * jnp.asarray(SCALE, BF)
        qts[:, k * LH * TOK : (k + 1) * LH * TOK] = stacked(query, lmask)
        kvt[:, at] = packed[LW:].astype(BF)
        k_nat[at, :] = jnp.transpose(packed[LW : 2 * LW]).astype(BF)
        v_nat[at, :] = jnp.transpose(packed[2 * LW :]).astype(BF)

    project_space(0)
    for h, part in enumerate(halves):
        landed(nb.at[0], n_near[h])
        push(nb.at[1 + 2 * core, part], nb.at[2, part], "space", s_next, n_out[1], n_far[h])
    g_a.a()
    project_space(1)
    project_space(3)
    for h, part in enumerate(halves):
        landed(nb.at[2, part], n_far[h])
    project_space(2)

    a_num = [ticket() for _ in range(NSP)]
    a_out = sending(ats.at[0, 1:NV]), sending(ats.at[1:NSP])

    def attend_space(k):
        at = slice(k * LH * TOK, (k + 1) * LH * TOK)
        shares = softmax0(dot(k_nat[...], qts[:, at], NN)).astype(BF)
        pts[:, at] = shares
        out = jnp.transpose(per_head(kvt[LW:, :], shares)).astype(BF)
        ats[k] = out.reshape(NV, CH, LW)

    def send_attended(k):
        for j in order + (0,):
            to = (plus(v, j, NV), plus(s, -k, NSP))
            if k or j:
                push(ats.at[k, to[0]], att.at[s, j], ("view", "space"), to, a_out[min(k, 1)], a_num[k])
            else:
                att[pl.ds(s, 1), 0:1] = ats[0:1, pl.ds(v, 1)]

    attend_space(2)
    attend_space(1)
    send_attended(2)
    send_attended(1)
    g_a.b()
    g_b.a()
    attend_space(3)
    attend_space(0)
    send_attended(3)
    send_attended(0)
    g_a.c()
    g_b.b()
    g_c.a()
    g_a.d()
    g_b.c()

    def slot_of(view):
        return lax.rem(v - view + NV, NV)

    g_b.d()
    landed(xb.at[1:NV], x2_num)
    for k in (2, 1, 3):
        landed(att.at[plus(s, k, NSP)], a_num[k])
    landed(att.at[s, 1:NV], a_num[0])
    c2_num, c2_out = ticket(), sending(c2.at[1:NT_])
    for m in tm_order:
        push(xb.at[slot_of(paired(m)), 1], c2.at[m], "tm", paired(m), c2_out, c2_num)
    c2[0] = xb[slot_of(t), 1]
    g_c.b()
    g_a.e()
    term = dot(att[0].reshape(TOK, LW), wos[0, :LW, :], NN)
    for h in range(1, NSP):
        term += dot(att[h].reshape(TOK, LW), wos[0, h * LW : (h + 1) * LW, :], NN)
    x2[...] = (xb[:, 0].reshape(TOK, D).astype(F32) + term).astype(BF).reshape(NV, CH, D)
    rows_view = x2[...].reshape(TOK, D)
    normed, _ = rms(rows_view.astype(F32))
    tokens = normed.astype(BF)

    def attend_small(w, g):
        lanes = slice(g * GW, (g + 1) * GW)
        query = dot(w[0, lanes, :], tokens, NT).astype(BF) * jnp.asarray(SCALE, BF)
        key_t = dot(w[1, lanes, :], tokens, NT).astype(BF)
        value_t = dot(w[2, lanes, :], tokens, NT).astype(BF)
        queries = stacked(query, gmask)
        shares = softmax0(dot(key_t, queries, TN) + bias[...]).astype(BF)
        return queries, key_t, value_t, shares

    def backward_small(queries, key_t, value, shares, grads):
        share_grad = dot(value, grads, NN)
        wide = shares.astype(F32)
        row_dot = jnp.sum(wide * share_grad, axis=0, keepdims=True)
        score_grad = (wide * (share_grad - row_dot)).astype(BF)
        query_grad = (per_head(key_t, score_grad) * SCALE).astype(BF)
        key_grad = dot(score_grad, queries, NT).astype(BF)
        value_grad = dot(shares, grads, NT).astype(BF)
        return jnp.transpose(query_grad), key_grad, value_grad

    def normed_grad_of(parts, w):
        columns = [part[at] for at in range(3) for part in parts]
        return dot(jnp.concatenate(columns, axis=1), w[...].reshape(3 * D, D), NN)

    outs = []
    for g in range(GROUPS):
        queries, key_t, value_t, shares = attend_small(wqv, g)
        qts_v[g], kt_v[g], vt_v[g], pt_v[g] = queries, key_t, value_t, shares
        outs.append(per_head(value_t, shares).astype(BF))
        if g == 1:
            g_c.c()
    g_b.e()
    term = dot(jnp.concatenate(outs, axis=0), wov[0], TN)
    xt[...] = (rows_view.astype(F32) + term).astype(BF).reshape(NV, CH, D)

    x3_num, x3_out = ticket(), sending(x3.at[1:NT_])
    for m in tm_order:
        push(xt.at[slot_of(paired(m))], x3.at[m], "tm", paired(m), x3_out, x3_num)
    x3[0] = xt[slot_of(t)]
    landed(c2.at[1:NT_], c2_num)
    upstream = c2[...].reshape(TOK, D)
    out_grads = dot(wot[0], upstream, NT).astype(BF)
    grads_t = [stacked(out_grads[g * GW : (g + 1) * GW], gmask) for g in range(GROUPS)]
    for g in range(GROUPS):
        v_v[g] = jnp.transpose(vt_v[g])
    g_c.d()
    landed(x3.at[1:NT_], x3_num)
    g_c.e()
    rows_time = x3[...].reshape(TOK, D)
    normed, factor = rms(rows_time.astype(F32))
    tokens = normed.astype(BF)

    parts = []
    for g in range(GROUPS):
        queries, key_t, value_t, shares = attend_small(wqt, g)
        parts.append(backward_small(queries, key_t, jnp.transpose(value_t), shares, grads_t[g]))
    total = normed_grad_of(parts, wqt)
    ut[...] = finish(upstream, normed, factor, total).reshape(NT_, CH, D)

    u2_num, u2_out = ticket(), sending(ut.at[1:NT_])
    here = slot_of(t)
    for m in tm_order:
        push(ut.at[m], u2.at[here], "tm", paired(m), u2_out, u2_num)
    u2[pl.ds(here, 1)] = ut[0:1]
    normed, factor = rms(x2[...].reshape(TOK, D).astype(F32))
    for ref, number in left[:-1]:
        gone(ref, number)
    del left[:-1]
    landed(u2.at[1:NT_], u2_num)
    upstream = u2[...].reshape(TOK, D)
    parts = []
    for g in range(GROUPS):
        out_grad = dot(wov[0, g * GW : (g + 1) * GW, :], upstream, NT).astype(BF)
        saved = qts_v[g], kt_v[g], v_v[g], pt_v[g]
        parts.append(backward_small(*saved, stacked(out_grad, gmask)))
    upstream = finish(upstream, normed, factor, normed_grad_of(parts, wqv))
    uv[...] = upstream.reshape(NV, CH, D)

    out_grad = dot(wos[0], upstream, NT)
    for h in range(NSP):
        part = jnp.transpose(out_grad[h * LW : (h + 1) * LW]).astype(BF)
        ogs[h] = part.reshape(NV, CH, LW)
    og_num = [ticket() for _ in range(NSP)]
    og_out = sending(ogs.at[0, 1:NV]), sending(ogs.at[1:NSP])
    for k in (2, 1, 3, 0):
        for j in order + (0,):
            to = (plus(v, -j, NV), plus(s, k, NSP))
            if k or j:
                push(ogs.at[to[1], j], og.at[k, v], ("view", "space"), to, og_out[min(k, 1)], og_num[k])
    og[0:1, pl.ds(v, 1)] = ogs[pl.ds(s, 1), 0:1]
    def backward_space(k):
        at = slice(k * LH * TOK, (k + 1) * LH * TOK)
        out_grad = og[k].reshape(TOK, LW)
        grads = jnp.concatenate([out_grad * m for m in nmask], axis=0)
        ogts[at, :] = grads
        share_grad = dot(v_nat[...], grads, NT)
        wide = pts[:, at].astype(F32)
        row_dot = jnp.sum(wide * share_grad, axis=0, keepdims=True)
        score_grad = (wide * (share_grad - row_dot)).astype(BF)
        gts[:, at] = score_grad
        dqt[k] = (per_head(kvt[:LW, :], score_grad) * SCALE).astype(BF)

    head_at = lax.broadcasted_iota(jnp.int32, (TOK, LW), 1) // HD
    nmask = [(head_at == h).astype(F32).astype(BF) for h in range(LH)]
    u3_num, u3_out = ticket(), sending(uv.at[1:NV])
    landed(og.at[0, 1:NV], og_num[0])
    landed(og.at[1], og_num[1])
    backward_space(0)
    backward_space(1)
    landed(og.at[3], og_num[3])
    landed(og.at[2], og_num[2])
    for j in order:
        push(uv.at[j], u3.at[v], "view", plus(v, -j, NV), u3_out, u3_num)
    backward_space(3)
    backward_space(2)
    u3[pl.ds(v, 1)] = uv[0:1]

    def partial_sums(k):
        at = pl.ds(pl.multiple_of(k * TOK, TOK), TOK)
        key_grad = dot(gts[at, :], qts[...], NT).astype(BF)
        value_grad = dot(pts[at, :], ogts[...], NN).astype(BF)
        part = dot(dqt[k], wqs_ref[:LW, :], TN)
        part += dot(key_grad, wqs_ref[LW : 2 * LW, :], NN)
        return part + dot(value_grad, wqs_ref[2 * LW :, :], NN)

    rf_num, late_num = [ticket() for _ in halves], [ticket() for _ in halves]
    near_num = ticket()
    rs_out = sending(rsend)
    rsend[0] = partial_sums(2).astype(BF)
    for h, part in enumerate(halves):
        push(rsend.at[0, part], rf.at[part], "space", s_next, rs_out, rf_num[h])
    rsend[1] = partial_sums(1 + 2 * core).astype(BF)
    push(rsend.at[1], rs.at[0], "space", s_prev, rs_out, near_num)
    late = partial_sums(3 - 2 * core)
    total = partial_sums(0)
    normed, factor = rms(xc[:, 0].reshape(TOK, D).astype(F32))
    for h, part in enumerate(halves):
        landed(rf.at[part], rf_num[h])
        rsend[2, part] = (late[part] + rf[part].astype(F32)).astype(BF)
        push(rsend.at[2, part], rs.at[1, part], "space", s_next, rs_out, late_num[h])
    landed(rs.at[0], near_num)
    total += rs[0].astype(F32)
    for h, part in enumerate(halves):
        landed(rs.at[1, part], late_num[h])
    total += rs[1].astype(F32)
    landed(u3.at[1:NV], u3_num)
    out_ref[...] = finish(u3[...].reshape(TOK, D), normed, factor, total)

    for ref, number in left:
        gone(ref, number)


def on_device(latents, cotangent, wqs, wos, wqv, wov, wqt, wot):
    vmem = pl.BlockSpec(memory_space=pltpu.VMEM)
    hbm = pl.BlockSpec(memory_space=pltpu.HBM)

    def buf(*shape, dtype=BF):
        return pltpu.VMEM(shape, dtype)

    wide = NSP * LH * TOK
    out = pl.pallas_call(
        body,
        out_shape=jax.ShapeDtypeStruct((TOK, D), BF),
        in_specs=[hbm] * 8,
        out_specs=vmem,
        scratch_shapes=[
            buf(NV, 2, CH, D),
            buf(3 * LW, D),
            buf(NSP, TOK, D),
            buf(NSP * TOK, LW),
            buf(NSP * TOK, LW),
            buf(LW, wide),
            buf(2 * LW, NSP * TOK),
            buf(NSP * TOK, wide),
            buf(NSP * TOK, wide),
            buf(wide, LW),
            buf(NSP, LW, TOK),
            buf(NSP, NV, CH, LW),
            buf(NSP, NV, CH, LW),
        ]
        + [buf(NV, 2, CH, D)]
        + [buf(NV, CH, D)] * 8
        + [
            buf(NSP, NV, CH, LW),
            buf(NSP, NV, CH, LW),
            buf(3, TOK, D),
            buf(2, TOK, D),
            buf(TOK, D),
            buf(TOK, GH * TOK, dtype=F32),
            buf(GROUPS, GW, TOK),
            buf(GROUPS, GW, TOK),
            buf(GROUPS, TOK, GW),
            buf(GROUPS, GW, GH * TOK),
            buf(GROUPS, TOK, GH * TOK),
            buf(9, D, D),
            pltpu.SemaphoreType.DMA((NSEM,)),
            pltpu.SemaphoreType.DMA((NSEM,)),
            pltpu.SemaphoreType.DMA((8,)),
        ],
        compiler_params=pltpu.CompilerParams(
            collective_id=0, has_side_effects=True, vmem_limit_bytes=VMEM
        ),
        name="block_backward",
    )(
        latents.reshape(NV, CH, D),
        cotangent.reshape(NV, CH, D),
        wqs.reshape(3 * LW, D),
        wos[None],
        wqv,
        wov[None],
        wqt,
        wot[None],
    )
    return out[None, None]


def solution(mesh):
    in_specs = (
        P("view", "tm", "space", None),
        P("view", "tm", "space", None),
        P(None, "space", None),
        P("space", None),
        P(None, "space", None),
        P("space", None),
        P(None, "space", None),
        P("space", None),
    )
    return jax.shard_map(
        on_device,
        mesh=mesh,
        in_specs=in_specs,
        out_specs=P("view", "tm", "space", None),
        check_vma=False,
    )
```

```python
import jax
import jax.numpy as jnp
from jax import lax
from jax.experimental import pallas as pl
from jax.experimental.pallas import tpu as pltpu
from jax.sharding import PartitionSpec as P

MESH = pl.DeviceIdType.MESH
BF = jnp.bfloat16
F32 = jnp.float32
NN = ((1,), (0,))
NT = ((1,), (1,))
TN = ((0,), (0,))

D = 768
TOK = 128
NSP = 4
NV = 8
NT_ = 8
CH = 16
HD = 64
LH = 3
LW = LH * HD
GH = 4
GW = GH * HD
GROUPS = D // GW
SCALE = HD**-0.5
NSEM = 64
VMEM = 859 * 65536


def dot(a, b, dims):
    return lax.dot_general(a, b, (dims, ((), ())), preferred_element_type=F32)


def rms(values):
    factor = lax.rsqrt(jnp.mean(values * values, axis=-1, keepdims=True) + 1e-06)
    return values * factor, factor


def finish(upstream, normed, factor, normed_grad):
    inner = jnp.mean(normed_grad * normed, axis=-1, keepdims=True)
    return (upstream.astype(F32) + factor * (normed_grad - normed * inner)).astype(BF)


def softmax0(scores):
    top = jnp.max(scores, axis=0, keepdims=True)
    expo = jnp.exp(scores - top)
    return expo * (1.0 / jnp.sum(expo, axis=0, keepdims=True))


def head_masks(rows):
    head = lax.broadcasted_iota(jnp.int32, (rows, TOK), 0) // HD
    return [(head == h).astype(F32).astype(BF) for h in range(rows // HD)]


def stacked(values, masks):
    return jnp.concatenate([values * m for m in masks], axis=1)


def per_head(left, right):
    heads = left.shape[0] // HD
    return jnp.concatenate(
        [
            dot(left[h * HD : (h + 1) * HD], right[:, h * TOK : (h + 1) * TOK], NN)
            for h in range(heads)
        ],
        axis=0,
    )


def body(
    x_in, cot_in, wqs_in, wos_in, wqv_in, wov_in, wqt_in, wot_in,
    out_ref,
    xc, wqs_ref,
    nb, k_nat, v_nat, qts, kvt, pts, gts, ogts, dqt, ats, att,
    xb, x2, xt, x3, c2, ut, u2, uv, u3, ogs, og, rsend, rs, rf,
    bias, kt_v, vt_v, v_v, qts_v, pt_v,
    whole,
    send_sem, recv_sem, local_sem,
):
    t = lax.axis_index("tm")
    v = lax.axis_index("view")
    s = lax.axis_index("space")
    core = lax.rem(t, 2)
    sibling = t + 1 - 2 * core
    y = lax.rem(v, 4)
    half = lax.rem(y, 2)
    step = 1 - 2 * core
    y_next = v - y + lax.rem(y + step + 4, 4)
    s_next = lax.rem(s + step + 4, 4)
    s_prev = lax.rem(s - step + 4, 4)

    def plus(me, k, n):
        return lax.rem(me + k + n, n)

    bits = [t % 2, t // 2 % 2, t // 4]

    def paired(m):
        return t + sum((1 - 2 * bits[at]) * 2**at for at in range(3) if m >> at & 1)

    tm_order = (6, 7, 4, 5, 2, 3, 1)
    left = []
    count = [0]

    def ticket():
        count[0] += 1
        return count[0] - 1

    def remote(src, dst, axis, index, number, arrival):
        to = {axis: index} if isinstance(axis, str) else dict(zip(axis, index))
        return pltpu.make_async_remote_copy(
            src_ref=src,
            dst_ref=dst,
            send_sem=send_sem.at[number],
            recv_sem=recv_sem.at[arrival],
            device_id=to,
            device_id_type=MESH,
        )

    def push(src, dst, axis, index, number, arrival):
        remote(src, dst, axis, index, number, arrival).start()

    def landed(ref, arrival):
        remote(ref, ref, "tm", sibling, 0, arrival).wait_recv()

    def gone(ref, number):
        remote(ref, ref, "tm", sibling, number, 0).wait_send()

    def sending(ref):
        left.append((ref, ticket()))
        return left[-1][1]

    def rows(owner, c, h, size):
        return pl.ds(pl.multiple_of(owner * LW + c * 96 + h * 48, 16), size)

    class Gather:
        def __init__(self, first, end):
            self.first, self.end = first, end
            self.others = [plus(s, -1, 4), plus(s, 1, 4), plus(s, 2, 4)]
            self.out = [sending(self.bytes_of(size)) for size in (96, 48, 144, 288)]
            self.near, self.far, self.y_near, self.y_far, self.sib = [ticket() for _ in range(5)]

        def bytes_of(self, size):
            return whole.at[self.first : self.end, 0:size, :]

        def piece(self, owner, c, h, size=48):
            return whole.at[self.first : self.end, rows(owner, c, h, size), :]

        def a(self):
            mine = self.piece(s, core, half)
            push(mine, mine, "space", plus(s, 1, 4), self.out[0], self.near)
            push(mine, mine, "space", plus(s, -1, 4), self.out[0], self.near)

        def b(self):
            landed(self.bytes_of(96), self.near)
            far = self.piece(s_prev, core, half)
            push(far, far, "space", s_next, self.out[1], self.far)
            for at in range(2):
                part = self.piece(self.others[at], core, half)
                push(part, part, "view", y_next, self.out[2], self.y_near)

        def c(self):
            landed(self.bytes_of(48), self.far)
            part = self.piece(self.others[2], core, half)
            push(part, part, "view", y_next, self.out[2], self.y_far)

        def d(self):
            landed(self.bytes_of(96), self.y_near)
            for at in range(3):
                if at == 2:
                    landed(self.bytes_of(48), self.y_far)
                part = self.piece(self.others[at], core, 0, 96)
                push(part, part, "tm", sibling, self.out[3], self.sib)

        def e(self):
            landed(self.bytes_of(288), self.sib)

    g_a, g_b, g_c = Gather(0, 4), Gather(4, 6), Gather(6, 9)
    wos, wqv, wov = whole.at[0:1], whole.at[1:4], whole.at[4:5]
    wot, wqt = whole.at[5:6], whole.at[6:9]
    own = pl.ds(pl.multiple_of(s * LW, 16), LW)

    loads = [
        pltpu.make_async_copy(src, dst, local_sem.at[at])
        for at, (src, dst) in enumerate(
            (
                (x_in, xc.at[:, 0]),
                (wqs_in, wqs_ref),
                (cot_in, xc.at[:, 1]),
                (wos_in, wos.at[:, own, :]),
                (wqv_in, wqv.at[:, own, :]),
                (wov_in, wov.at[:, own, :]),
                (wot_in, wot.at[:, own, :]),
                (wqt_in, wqt.at[:, own, :]),
            )
        )
    ]
    for copy in loads:
        copy.start()

    barrier = pltpu.get_barrier_semaphore()
    for k in range(NSP):
        for j in range(NV):
            if k or j:
                pl.semaphore_signal(
                    barrier,
                    inc=1,
                    device_id={"view": plus(v, j, NV), "space": plus(s, k, NSP)},
                    device_id_type=MESH,
                )
    for k in range(1, NT_):
        pl.semaphore_signal(barrier, inc=1, device_id={"tm": plus(t, k, NT_)}, device_id_type=MESH)

    loads[0].wait()
    x_rows = xc[:, 0].reshape(TOK, D)
    normed, _ = rms(x_rows.astype(F32))
    nb[0] = normed.astype(BF)
    key_at = lax.broadcasted_iota(jnp.int32, (TOK, GH * TOK), 0)
    query_at = lax.broadcasted_iota(jnp.int32, (TOK, GH * TOK), 1)
    bias[...] = jnp.where(lax.rem(key_at, CH) == lax.rem(query_at, CH), 0.0, -1e30)
    lmask = head_masks(LW)
    gmask = head_masks(GW)
    pl.semaphore_wait(barrier, NSP * NV + NT_ - 2)

    halves = [slice(0, TOK // 2), slice(TOK // 2, TOK)]
    n_near, n_far = [ticket() for _ in halves], [ticket() for _ in halves]
    n_out = sending(nb.at[0:2]), sending(nb.at[0])
    for h, part in enumerate(halves):
        for k in (1, 3):
            push(nb.at[0, part], nb.at[k, part], "space", plus(s, k, NSP), n_out[0], n_near[h])
    for copy in loads[1:]:
        copy.wait()
    order = (4, 3, 5, 2, 6, 1, 7)
    x2_num, x2_out = ticket(), sending(xb.at[1:NV])
    for j in order:
        to = plus(v, j, NV)
        push(xc.at[to], xb.at[j], "view", to, x2_out, x2_num)
    xb[0] = xc[v]

    def project_space(k):
        tokens = nb[k]
        packed = dot(wqs_ref[...], tokens, NT)
        at = slice(k * TOK, (k + 1) * TOK)
        query = packed[:LW].astype(BF) * jnp.asarray(SCALE, BF)
        qts[:, k * LH * TOK : (k + 1) * LH * TOK] = stacked(query, lmask)
        kvt[:, at] = packed[LW:].astype(BF)
        k_nat[at, :] = jnp.transpose(packed[LW : 2 * LW]).astype(BF)
        v_nat[at, :] = jnp.transpose(packed[2 * LW :]).astype(BF)

    project_space(0)
    for h, part in enumerate(halves):
        landed(nb.at[0], n_near[h])
        push(nb.at[1 + 2 * core, part], nb.at[2, part], "space", s_next, n_out[1], n_far[h])
    g_a.a()
    project_space(1)
    project_space(3)
    for h, part in enumerate(halves):
        landed(nb.at[2, part], n_far[h])
    project_space(2)

    a_num = [ticket() for _ in range(NSP)]
    a_out = sending(ats.at[0, 1:NV]), sending(ats.at[1:NSP])

    def attend_space(k):
        at = slice(k * LH * TOK, (k + 1) * LH * TOK)
        shares = softmax0(dot(k_nat[...], qts[:, at], NN)).astype(BF)
        pts[:, at] = shares
        out = jnp.transpose(per_head(kvt[LW:, :], shares)).astype(BF)
        ats[k] = out.reshape(NV, CH, LW)

    def send_attended(k):
        for j in order + (0,):
            to = (plus(v, j, NV), plus(s, -k, NSP))
            if k or j:
                push(ats.at[k, to[0]], att.at[s, j], ("view", "space"), to, a_out[min(k, 1)], a_num[k])
            else:
                att[pl.ds(s, 1), 0:1] = ats[0:1, pl.ds(v, 1)]

    attend_space(2)
    attend_space(1)
    send_attended(2)
    send_attended(1)
    g_a.b()
    g_b.a()
    attend_space(3)
    attend_space(0)
    send_attended(3)
    send_attended(0)
    g_a.c()
    g_b.b()
    g_c.a()
    g_a.d()
    g_b.c()

    def slot_of(view):
        return lax.rem(v - view + NV, NV)

    g_b.d()
    landed(xb.at[1:NV], x2_num)
    for k in (2, 1, 3):
        landed(att.at[plus(s, k, NSP)], a_num[k])
    landed(att.at[s, 1:NV], a_num[0])
    c2_num, c2_out = ticket(), sending(c2.at[1:NT_])
    for m in tm_order:
        push(xb.at[slot_of(paired(m)), 1], c2.at[m], "tm", paired(m), c2_out, c2_num)
    c2[0] = xb[slot_of(t), 1]
    g_c.b()
    g_a.e()
    term = dot(att[0].reshape(TOK, LW), wos[0, :LW, :], NN)
    for h in range(1, NSP):
        term += dot(att[h].reshape(TOK, LW), wos[0, h * LW : (h + 1) * LW, :], NN)
    x2[...] = (xb[:, 0].reshape(TOK, D).astype(F32) + term).astype(BF).reshape(NV, CH, D)
    rows_view = x2[...].reshape(TOK, D)
    normed, _ = rms(rows_view.astype(F32))
    tokens = normed.astype(BF)

    def attend_small(w, g):
        lanes = slice(g * GW, (g + 1) * GW)
        query = dot(w[0, lanes, :], tokens, NT).astype(BF) * jnp.asarray(SCALE, BF)
        key_t = dot(w[1, lanes, :], tokens, NT).astype(BF)
        value_t = dot(w[2, lanes, :], tokens, NT).astype(BF)
        queries = stacked(query, gmask)
        shares = softmax0(dot(key_t, queries, TN) + bias[...]).astype(BF)
        return queries, key_t, value_t, shares

    def backward_small(queries, key_t, value, shares, grads):
        share_grad = dot(value, grads, NN)
        wide = shares.astype(F32)
        row_dot = jnp.sum(wide * share_grad, axis=0, keepdims=True)
        score_grad = (wide * (share_grad - row_dot)).astype(BF)
        query_grad = (per_head(key_t, score_grad) * SCALE).astype(BF)
        key_grad = dot(score_grad, queries, NT).astype(BF)
        value_grad = dot(shares, grads, NT).astype(BF)
        return jnp.transpose(query_grad), key_grad, value_grad

    def normed_grad_of(parts, w):
        columns = [part[at] for at in range(3) for part in parts]
        return dot(jnp.concatenate(columns, axis=1), w[...].reshape(3 * D, D), NN)

    outs = []
    for g in range(GROUPS):
        queries, key_t, value_t, shares = attend_small(wqv, g)
        qts_v[g], kt_v[g], vt_v[g], pt_v[g] = queries, key_t, value_t, shares
        outs.append(per_head(value_t, shares).astype(BF))
    g_b.e()
    term = dot(jnp.concatenate(outs, axis=0), wov[0], TN)
    xt[...] = (rows_view.astype(F32) + term).astype(BF).reshape(NV, CH, D)

    x3_num, x3_out = ticket(), sending(x3.at[1:NT_])
    for m in tm_order:
        push(xt.at[slot_of(paired(m))], x3.at[m], "tm", paired(m), x3_out, x3_num)
    x3[0] = xt[slot_of(t)]
    g_c.c()
    landed(c2.at[1:NT_], c2_num)
    upstream = c2[...].reshape(TOK, D)
    out_grads = dot(wot[0], upstream, NT).astype(BF)
    grads_t = [stacked(out_grads[g * GW : (g + 1) * GW], gmask) for g in range(GROUPS)]
    for g in range(GROUPS):
        v_v[g] = jnp.transpose(vt_v[g])
    g_c.d()
    landed(x3.at[1:NT_], x3_num)
    g_c.e()
    rows_time = x3[...].reshape(TOK, D)
    normed, factor = rms(rows_time.astype(F32))
    tokens = normed.astype(BF)

    parts = []
    for g in range(GROUPS):
        queries, key_t, value_t, shares = attend_small(wqt, g)
        parts.append(backward_small(queries, key_t, jnp.transpose(value_t), shares, grads_t[g]))
    total = normed_grad_of(parts, wqt)
    ut[...] = finish(upstream, normed, factor, total).reshape(NT_, CH, D)

    u2_num, u2_out = ticket(), sending(ut.at[1:NT_])
    here = slot_of(t)
    for m in tm_order:
        push(ut.at[m], u2.at[here], "tm", paired(m), u2_out, u2_num)
    u2[pl.ds(here, 1)] = ut[0:1]
    normed, factor = rms(x2[...].reshape(TOK, D).astype(F32))
    for ref, number in left[:-1]:
        gone(ref, number)
    del left[:-1]
    landed(u2.at[1:NT_], u2_num)
    upstream = u2[...].reshape(TOK, D)
    parts = []
    for g in range(GROUPS):
        out_grad = dot(wov[0, g * GW : (g + 1) * GW, :], upstream, NT).astype(BF)
        saved = qts_v[g], kt_v[g], v_v[g], pt_v[g]
        parts.append(backward_small(*saved, stacked(out_grad, gmask)))
    upstream = finish(upstream, normed, factor, normed_grad_of(parts, wqv))
    uv[...] = upstream.reshape(NV, CH, D)

    out_grad = dot(wos[0], upstream, NT)
    for h in range(NSP):
        part = jnp.transpose(out_grad[h * LW : (h + 1) * LW]).astype(BF)
        ogs[h] = part.reshape(NV, CH, LW)
    og_num = [ticket() for _ in range(NSP)]
    og_out = sending(ogs.at[0, 1:NV]), sending(ogs.at[1:NSP])
    for k in (2, 1, 3, 0):
        for j in order + (0,):
            to = (plus(v, -j, NV), plus(s, k, NSP))
            if k or j:
                push(ogs.at[to[1], j], og.at[k, v], ("view", "space"), to, og_out[min(k, 1)], og_num[k])
    og[0:1, pl.ds(v, 1)] = ogs[pl.ds(s, 1), 0:1]
    def backward_space(k):
        at = slice(k * LH * TOK, (k + 1) * LH * TOK)
        out_grad = og[k].reshape(TOK, LW)
        grads = jnp.concatenate([out_grad * m for m in nmask], axis=0)
        ogts[at, :] = grads
        share_grad = dot(v_nat[...], grads, NT)
        wide = pts[:, at].astype(F32)
        row_dot = jnp.sum(wide * share_grad, axis=0, keepdims=True)
        score_grad = (wide * (share_grad - row_dot)).astype(BF)
        gts[:, at] = score_grad
        dqt[k] = (per_head(kvt[:LW, :], score_grad) * SCALE).astype(BF)

    head_at = lax.broadcasted_iota(jnp.int32, (TOK, LW), 1) // HD
    nmask = [(head_at == h).astype(F32).astype(BF) for h in range(LH)]
    u3_num, u3_out = ticket(), sending(uv.at[1:NV])
    landed(og.at[0, 1:NV], og_num[0])
    landed(og.at[1], og_num[1])
    backward_space(0)
    backward_space(1)
    landed(og.at[3], og_num[3])
    landed(og.at[2], og_num[2])
    for j in order:
        push(uv.at[j], u3.at[v], "view", plus(v, -j, NV), u3_out, u3_num)
    backward_space(3)
    backward_space(2)
    u3[pl.ds(v, 1)] = uv[0:1]

    def partial_sums(k):
        at = pl.ds(pl.multiple_of(k * TOK, TOK), TOK)
        key_grad = dot(gts[at, :], qts[...], NT).astype(BF)
        value_grad = dot(pts[at, :], ogts[...], NN).astype(BF)
        part = dot(dqt[k], wqs_ref[:LW, :], TN)
        part += dot(key_grad, wqs_ref[LW : 2 * LW, :], NN)
        return part + dot(value_grad, wqs_ref[2 * LW :, :], NN)

    rf_num, late_num = [ticket() for _ in halves], [ticket() for _ in halves]
    near_num = ticket()
    rs_out = sending(rsend)
    rsend[0] = partial_sums(2).astype(BF)
    for h, part in enumerate(halves):
        push(rsend.at[0, part], rf.at[part], "space", s_next, rs_out, rf_num[h])
    rsend[1] = partial_sums(1 + 2 * core).astype(BF)
    push(rsend.at[1], rs.at[0], "space", s_prev, rs_out, near_num)
    late = partial_sums(3 - 2 * core)
    total = partial_sums(0)
    normed, factor = rms(xc[:, 0].reshape(TOK, D).astype(F32))
    for h, part in enumerate(halves):
        landed(rf.at[part], rf_num[h])
        rsend[2, part] = (late[part] + rf[part].astype(F32)).astype(BF)
        push(rsend.at[2, part], rs.at[1, part], "space", s_next, rs_out, late_num[h])
    landed(rs.at[0], near_num)
    total += rs[0].astype(F32)
    for h, part in enumerate(halves):
        landed(rs.at[1, part], late_num[h])
    total += rs[1].astype(F32)
    landed(u3.at[1:NV], u3_num)
    out_ref[...] = finish(u3[...].reshape(TOK, D), normed, factor, total)

    for ref, number in left:
        gone(ref, number)


def on_device(latents, cotangent, wqs, wos, wqv, wov, wqt, wot):
    vmem = pl.BlockSpec(memory_space=pltpu.VMEM)
    hbm = pl.BlockSpec(memory_space=pltpu.HBM)

    def buf(*shape, dtype=BF):
        return pltpu.VMEM(shape, dtype)

    wide = NSP * LH * TOK
    out = pl.pallas_call(
        body,
        out_shape=jax.ShapeDtypeStruct((TOK, D), BF),
        in_specs=[hbm] * 8,
        out_specs=vmem,
        scratch_shapes=[
            buf(NV, 2, CH, D),
            buf(3 * LW, D),
            buf(NSP, TOK, D),
            buf(NSP * TOK, LW),
            buf(NSP * TOK, LW),
            buf(LW, wide),
            buf(2 * LW, NSP * TOK),
            buf(NSP * TOK, wide),
            buf(NSP * TOK, wide),
            buf(wide, LW),
            buf(NSP, LW, TOK),
            buf(NSP, NV, CH, LW),
            buf(NSP, NV, CH, LW),
        ]
        + [buf(NV, 2, CH, D)]
        + [buf(NV, CH, D)] * 8
        + [
            buf(NSP, NV, CH, LW),
            buf(NSP, NV, CH, LW),
            buf(3, TOK, D),
            buf(2, TOK, D),
            buf(TOK, D),
            buf(TOK, GH * TOK, dtype=F32),
            buf(GROUPS, GW, TOK),
            buf(GROUPS, GW, TOK),
            buf(GROUPS, TOK, GW),
            buf(GROUPS, GW, GH * TOK),
            buf(GROUPS, TOK, GH * TOK),
            buf(9, D, D),
            pltpu.SemaphoreType.DMA((NSEM,)),
            pltpu.SemaphoreType.DMA((NSEM,)),
            pltpu.SemaphoreType.DMA((8,)),
        ],
        compiler_params=pltpu.CompilerParams(
            collective_id=0, has_side_effects=True, vmem_limit_bytes=VMEM
        ),
        name="block_backward",
    )(
        latents.reshape(NV, CH, D),
        cotangent.reshape(NV, CH, D),
        wqs.reshape(3 * LW, D),
        wos[None],
        wqv,
        wov[None],
        wqt,
        wot[None],
    )
    return out[None, None]


def solution(mesh):
    in_specs = (
        P("view", "tm", "space", None),
        P("view", "tm", "space", None),
        P(None, "space", None),
        P("space", None),
        P(None, "space", None),
        P("space", None),
        P(None, "space", None),
        P("space", None),
    )
    return jax.shard_map(
        on_device,
        mesh=mesh,
        in_specs=in_specs,
        out_specs=P("view", "tm", "space", None),
        check_vma=False,
    )
```

```python
import jax
import jax.numpy as jnp
from jax import lax
from jax.experimental import pallas as pl
from jax.experimental.pallas import tpu as pltpu
from jax.sharding import PartitionSpec as P

MESH = pl.DeviceIdType.MESH
BF = jnp.bfloat16
F32 = jnp.float32
NN = ((1,), (0,))
NT = ((1,), (1,))
TN = ((0,), (0,))

D = 768
TOK = 128
NSP = 4
NV = 8
NT_ = 8
CH = 16
HD = 64
LH = 3
LW = LH * HD
GH = 4
GW = GH * HD
GROUPS = D // GW
SCALE = HD**-0.5
NSEM = 64
VMEM = 859 * 65536


def dot(a, b, dims):
    return lax.dot_general(a, b, (dims, ((), ())), preferred_element_type=F32)


def rms(values):
    factor = lax.rsqrt(jnp.mean(values * values, axis=-1, keepdims=True) + 1e-06)
    return values * factor, factor


def finish(upstream, normed, factor, normed_grad):
    inner = jnp.mean(normed_grad * normed, axis=-1, keepdims=True)
    return (upstream.astype(F32) + factor * (normed_grad - normed * inner)).astype(BF)


def softmax0(scores):
    top = jnp.max(scores, axis=0, keepdims=True)
    expo = jnp.exp(scores - top)
    return expo * (1.0 / jnp.sum(expo, axis=0, keepdims=True))


def head_masks(rows):
    head = lax.broadcasted_iota(jnp.int32, (rows, TOK), 0) // HD
    return [(head == h).astype(F32).astype(BF) for h in range(rows // HD)]


def stacked(values, masks):
    return jnp.concatenate([values * m for m in masks], axis=1)


def per_head(left, right):
    heads = left.shape[0] // HD
    return jnp.concatenate(
        [
            dot(left[h * HD : (h + 1) * HD], right[:, h * TOK : (h + 1) * TOK], NN)
            for h in range(heads)
        ],
        axis=0,
    )


def body(
    x_in, cot_in, wqs_in, wos_in, wqv_in, wov_in, wqt_in, wot_in,
    out_ref,
    xc, wqs_ref,
    nb, k_nat, v_nat, qts, kvt, pts, gts, ogts, dqt, ats, att,
    xb, x2, xt, x3, c2, ut, u2, uv, u3, ogs, og, rsend, rs, rf,
    bias, kt_v, vt_v, v_v, qts_v, pt_v,
    whole,
    send_sem, recv_sem, local_sem,
):
    t = lax.axis_index("tm")
    v = lax.axis_index("view")
    s = lax.axis_index("space")
    core = lax.rem(t, 2)
    sibling = t + 1 - 2 * core
    y = lax.rem(v, 4)
    half = lax.rem(y, 2)
    step = 1 - 2 * core
    y_next = v - y + lax.rem(y + step + 4, 4)
    s_next = lax.rem(s + step + 4, 4)
    s_prev = lax.rem(s - step + 4, 4)

    def plus(me, k, n):
        return lax.rem(me + k + n, n)

    bits = [t % 2, t // 2 % 2, t // 4]

    def paired(m):
        return t + sum((1 - 2 * bits[at]) * 2**at for at in range(3) if m >> at & 1)

    tm_order = (6, 7, 4, 5, 2, 3, 1)
    left = []
    count = [0]

    def ticket():
        count[0] += 1
        return count[0] - 1

    def remote(src, dst, axis, index, number, arrival):
        to = {axis: index} if isinstance(axis, str) else dict(zip(axis, index))
        return pltpu.make_async_remote_copy(
            src_ref=src,
            dst_ref=dst,
            send_sem=send_sem.at[number],
            recv_sem=recv_sem.at[arrival],
            device_id=to,
            device_id_type=MESH,
        )

    def push(src, dst, axis, index, number, arrival):
        remote(src, dst, axis, index, number, arrival).start()

    def landed(ref, arrival):
        remote(ref, ref, "tm", sibling, 0, arrival).wait_recv()

    def gone(ref, number):
        remote(ref, ref, "tm", sibling, number, 0).wait_send()

    def sending(ref):
        left.append((ref, ticket()))
        return left[-1][1]

    def rows(owner, c, h, size):
        return pl.ds(pl.multiple_of(owner * LW + c * 96 + h * 48, 16), size)

    class Gather:
        def __init__(self, first, end):
            self.first, self.end = first, end
            self.others = [plus(s, -1, 4), plus(s, 1, 4), plus(s, 2, 4)]
            self.out = [sending(self.bytes_of(size)) for size in (96, 48, 144, 288)]
            self.near, self.far, self.y_near, self.y_far, self.sib = [ticket() for _ in range(5)]

        def bytes_of(self, size):
            return whole.at[self.first : self.end, 0:size, :]

        def piece(self, owner, c, h, size=48):
            return whole.at[self.first : self.end, rows(owner, c, h, size), :]

        def a(self):
            mine = self.piece(s, core, half)
            push(mine, mine, "space", plus(s, 1, 4), self.out[0], self.near)
            push(mine, mine, "space", plus(s, -1, 4), self.out[0], self.near)

        def b(self):
            landed(self.bytes_of(96), self.near)
            far = self.piece(s_prev, core, half)
            push(far, far, "space", s_next, self.out[1], self.far)
            for at in range(2):
                part = self.piece(self.others[at], core, half)
                push(part, part, "view", y_next, self.out[2], self.y_near)

        def c(self):
            landed(self.bytes_of(48), self.far)
            part = self.piece(self.others[2], core, half)
            push(part, part, "view", y_next, self.out[2], self.y_far)

        def d(self):
            landed(self.bytes_of(96), self.y_near)
            for at in range(3):
                if at == 2:
                    landed(self.bytes_of(48), self.y_far)
                part = self.piece(self.others[at], core, 0, 96)
                push(part, part, "tm", sibling, self.out[3], self.sib)

        def e(self):
            landed(self.bytes_of(288), self.sib)

    g_a, g_b, g_c = Gather(0, 4), Gather(4, 6), Gather(6, 9)
    wos, wqv, wov = whole.at[0:1], whole.at[1:4], whole.at[4:5]
    wot, wqt = whole.at[5:6], whole.at[6:9]
    own = pl.ds(pl.multiple_of(s * LW, 16), LW)

    loads = [
        pltpu.make_async_copy(src, dst, local_sem.at[at])
        for at, (src, dst) in enumerate(
            (
                (x_in, xc.at[:, 0]),
                (wqs_in, wqs_ref),
                (cot_in, xc.at[:, 1]),
                (wos_in, wos.at[:, own, :]),
                (wqv_in, wqv.at[:, own, :]),
                (wov_in, wov.at[:, own, :]),
                (wot_in, wot.at[:, own, :]),
                (wqt_in, wqt.at[:, own, :]),
            )
        )
    ]
    for copy in loads:
        copy.start()

    barrier = pltpu.get_barrier_semaphore()
    for k in range(NSP):
        for j in range(NV):
            if k or j:
                pl.semaphore_signal(
                    barrier,
                    inc=1,
                    device_id={"view": plus(v, j, NV), "space": plus(s, k, NSP)},
                    device_id_type=MESH,
                )
    for k in range(1, NT_):
        pl.semaphore_signal(barrier, inc=1, device_id={"tm": plus(t, k, NT_)}, device_id_type=MESH)

    loads[0].wait()
    x_rows = xc[:, 0].reshape(TOK, D)
    normed, _ = rms(x_rows.astype(F32))
    nb[0] = normed.astype(BF)
    key_at = lax.broadcasted_iota(jnp.int32, (TOK, GH * TOK), 0)
    query_at = lax.broadcasted_iota(jnp.int32, (TOK, GH * TOK), 1)
    bias[...] = jnp.where(lax.rem(key_at, CH) == lax.rem(query_at, CH), 0.0, -1e30)
    lmask = head_masks(LW)
    gmask = head_masks(GW)
    pl.semaphore_wait(barrier, NSP * NV + NT_ - 2)

    halves = [slice(0, TOK // 2), slice(TOK // 2, TOK)]
    n_near, n_far = [ticket() for _ in halves], [ticket() for _ in halves]
    n_out = sending(nb.at[0:2]), sending(nb.at[0])
    for h, part in enumerate(halves):
        for k in (1, 3):
            push(nb.at[0, part], nb.at[k, part], "space", plus(s, k, NSP), n_out[0], n_near[h])
    for copy in loads[1:]:
        copy.wait()
    order = (4, 3, 5, 2, 6, 1, 7)
    x2_num, x2_out = ticket(), sending(xb.at[1:NV])
    for j in order:
        to = plus(v, j, NV)
        push(xc.at[to], xb.at[j], "view", to, x2_out, x2_num)
    xb[0] = xc[v]

    def project_space(k):
        tokens = nb[k]
        packed = dot(wqs_ref[...], tokens, NT)
        at = slice(k * TOK, (k + 1) * TOK)
        query = packed[:LW].astype(BF) * jnp.asarray(SCALE, BF)
        qts[:, k * LH * TOK : (k + 1) * LH * TOK] = stacked(query, lmask)
        kvt[:, at] = packed[LW:].astype(BF)
        k_nat[at, :] = jnp.transpose(packed[LW : 2 * LW]).astype(BF)
        v_nat[at, :] = jnp.transpose(packed[2 * LW :]).astype(BF)

    project_space(0)
    for h, part in enumerate(halves):
        landed(nb.at[0], n_near[h])
        push(nb.at[1 + 2 * core, part], nb.at[2, part], "space", s_next, n_out[1], n_far[h])
    g_a.a()
    project_space(1)
    project_space(3)
    for h, part in enumerate(halves):
        landed(nb.at[2, part], n_far[h])
    project_space(2)

    a_num = [ticket() for _ in range(NSP)]
    a_out = sending(ats.at[0, 1:NV]), sending(ats.at[1:NSP])

    def attend_space(k):
        at = slice(k * LH * TOK, (k + 1) * LH * TOK)
        shares = softmax0(dot(k_nat[...], qts[:, at], NN)).astype(BF)
        pts[:, at] = shares
        out = jnp.transpose(per_head(kvt[LW:, :], shares)).astype(BF)
        ats[k] = out.reshape(NV, CH, LW)

    def send_attended(k):
        for j in order + (0,):
            to = (plus(v, j, NV), plus(s, -k, NSP))
            if k or j:
                push(ats.at[k, to[0]], att.at[s, j], ("view", "space"), to, a_out[min(k, 1)], a_num[k])
            else:
                att[pl.ds(s, 1), 0:1] = ats[0:1, pl.ds(v, 1)]

    attend_space(2)
    attend_space(1)
    send_attended(2)
    send_attended(1)
    g_a.b()
    g_b.a()
    attend_space(3)
    attend_space(0)
    send_attended(3)
    send_attended(0)
    g_a.c()
    g_b.b()
    g_c.a()
    g_a.d()
    g_b.c()

    def slot_of(view):
        return lax.rem(v - view + NV, NV)

    g_b.d()
    landed(xb.at[1:NV], x2_num)
    for k in (2, 1, 3):
        landed(att.at[plus(s, k, NSP)], a_num[k])
    landed(att.at[s, 1:NV], a_num[0])
    c2_num, c2_out = ticket(), sending(c2.at[1:NT_])
    for m in tm_order:
        push(xb.at[slot_of(paired(m)), 1], c2.at[m], "tm", paired(m), c2_out, c2_num)
    c2[0] = xb[slot_of(t), 1]
    g_c.b()
    g_a.e()
    term = dot(att[0].reshape(TOK, LW), wos[0, :LW, :], NN)
    for h in range(1, NSP):
        term += dot(att[h].reshape(TOK, LW), wos[0, h * LW : (h + 1) * LW, :], NN)
    x2[...] = (xb[:, 0].reshape(TOK, D).astype(F32) + term).astype(BF).reshape(NV, CH, D)
    rows_view = x2[...].reshape(TOK, D)
    normed, _ = rms(rows_view.astype(F32))
    tokens = normed.astype(BF)

    def attend_small(w, g):
        lanes = slice(g * GW, (g + 1) * GW)
        query = dot(w[0, lanes, :], tokens, NT).astype(BF) * jnp.asarray(SCALE, BF)
        key_t = dot(w[1, lanes, :], tokens, NT).astype(BF)
        value_t = dot(w[2, lanes, :], tokens, NT).astype(BF)
        queries = stacked(query, gmask)
        shares = softmax0(dot(key_t, queries, TN) + bias[...]).astype(BF)
        return queries, key_t, value_t, shares

    def backward_small(queries, key_t, value, shares, grads):
        share_grad = dot(value, grads, NN)
        wide = shares.astype(F32)
        row_dot = jnp.sum(wide * share_grad, axis=0, keepdims=True)
        score_grad = (wide * (share_grad - row_dot)).astype(BF)
        query_grad = (per_head(key_t, score_grad) * SCALE).astype(BF)
        key_grad = dot(score_grad, queries, NT).astype(BF)
        value_grad = dot(shares, grads, NT).astype(BF)
        return jnp.transpose(query_grad), key_grad, value_grad

    def normed_grad_of(parts, w):
        columns = [part[at] for at in range(3) for part in parts]
        return dot(jnp.concatenate(columns, axis=1), w[...].reshape(3 * D, D), NN)

    outs = []
    for g in range(GROUPS):
        queries, key_t, value_t, shares = attend_small(wqv, g)
        qts_v[g], kt_v[g], vt_v[g], pt_v[g] = queries, key_t, value_t, shares
        outs.append(per_head(value_t, shares).astype(BF))
    g_c.c()
    g_b.e()
    term = dot(jnp.concatenate(outs, axis=0), wov[0], TN)
    xt[...] = (rows_view.astype(F32) + term).astype(BF).reshape(NV, CH, D)

    x3_num, x3_out = ticket(), sending(x3.at[1:NT_])
    for m in tm_order:
        push(xt.at[slot_of(paired(m))], x3.at[m], "tm", paired(m), x3_out, x3_num)
    x3[0] = xt[slot_of(t)]
    landed(c2.at[1:NT_], c2_num)
    upstream = c2[...].reshape(TOK, D)
    out_grads = dot(wot[0], upstream, NT).astype(BF)
    grads_t = [stacked(out_grads[g * GW : (g + 1) * GW], gmask) for g in range(GROUPS)]
    for g in range(GROUPS):
        v_v[g] = jnp.transpose(vt_v[g])
    g_c.d()
    landed(x3.at[1:NT_], x3_num)
    g_c.e()
    rows_time = x3[...].reshape(TOK, D)
    normed, factor = rms(rows_time.astype(F32))
    tokens = normed.astype(BF)

    parts = []
    for g in range(GROUPS):
        queries, key_t, value_t, shares = attend_small(wqt, g)
        parts.append(backward_small(queries, key_t, jnp.transpose(value_t), shares, grads_t[g]))
    total = normed_grad_of(parts, wqt)
    ut[...] = finish(upstream, normed, factor, total).reshape(NT_, CH, D)

    u2_num, u2_out = ticket(), sending(ut.at[1:NT_])
    here = slot_of(t)
    for m in tm_order:
        push(ut.at[m], u2.at[here], "tm", paired(m), u2_out, u2_num)
    u2[pl.ds(here, 1)] = ut[0:1]
    normed, factor = rms(x2[...].reshape(TOK, D).astype(F32))
    for ref, number in left[:-1]:
        gone(ref, number)
    del left[:-1]
    landed(u2.at[1:NT_], u2_num)
    upstream = u2[...].reshape(TOK, D)
    parts = []
    for g in range(GROUPS):
        out_grad = dot(wov[0, g * GW : (g + 1) * GW, :], upstream, NT).astype(BF)
        saved = qts_v[g], kt_v[g], v_v[g], pt_v[g]
        parts.append(backward_small(*saved, stacked(out_grad, gmask)))
    upstream = finish(upstream, normed, factor, normed_grad_of(parts, wqv))
    uv[...] = upstream.reshape(NV, CH, D)

    out_grad = dot(wos[0], upstream, NT)
    for h in range(NSP):
        part = jnp.transpose(out_grad[h * LW : (h + 1) * LW]).astype(BF)
        ogs[h] = part.reshape(NV, CH, LW)
    og_num = [ticket() for _ in range(NSP)]
    og_out = sending(ogs.at[0, 1:NV]), sending(ogs.at[1:NSP])
    for k in (2, 1, 3, 0):
        for j in order + (0,):
            to = (plus(v, -j, NV), plus(s, k, NSP))
            if k or j:
                push(ogs.at[to[1], j], og.at[k, v], ("view", "space"), to, og_out[min(k, 1)], og_num[k])
    og[0:1, pl.ds(v, 1)] = ogs[pl.ds(s, 1), 0:1]
    def backward_space(k):
        at = slice(k * LH * TOK, (k + 1) * LH * TOK)
        out_grad = og[k].reshape(TOK, LW)
        grads = jnp.concatenate([out_grad * m for m in nmask], axis=0)
        ogts[at, :] = grads
        share_grad = dot(v_nat[...], grads, NT)
        wide = pts[:, at].astype(F32)
        row_dot = jnp.sum(wide * share_grad, axis=0, keepdims=True)
        score_grad = (wide * (share_grad - row_dot)).astype(BF)
        gts[:, at] = score_grad
        dqt[k] = (per_head(kvt[:LW, :], score_grad) * SCALE).astype(BF)

    head_at = lax.broadcasted_iota(jnp.int32, (TOK, LW), 1) // HD
    nmask = [(head_at == h).astype(F32).astype(BF) for h in range(LH)]
    u3_num, u3_out = ticket(), sending(uv.at[1:NV])
    landed(og.at[0, 1:NV], og_num[0])
    landed(og.at[1], og_num[1])
    backward_space(0)
    backward_space(1)
    landed(og.at[3], og_num[3])
    landed(og.at[2], og_num[2])
    for j in order:
        push(uv.at[j], u3.at[v], "view", plus(v, -j, NV), u3_out, u3_num)
    backward_space(3)
    backward_space(2)
    u3[pl.ds(v, 1)] = uv[0:1]

    def partial_sums(k):
        at = pl.ds(pl.multiple_of(k * TOK, TOK), TOK)
        key_grad = dot(gts[at, :], qts[...], NT).astype(BF)
        value_grad = dot(pts[at, :], ogts[...], NN).astype(BF)
        part = dot(dqt[k], wqs_ref[:LW, :], TN)
        part += dot(key_grad, wqs_ref[LW : 2 * LW, :], NN)
        return part + dot(value_grad, wqs_ref[2 * LW :, :], NN)

    rf_num, late_num = [ticket() for _ in halves], [ticket() for _ in halves]
    near_num = ticket()
    rs_out = sending(rsend)
    rsend[0] = partial_sums(2).astype(BF)
    for h, part in enumerate(halves):
        push(rsend.at[0, part], rf.at[part], "space", s_next, rs_out, rf_num[h])
    rsend[1] = partial_sums(1 + 2 * core).astype(BF)
    push(rsend.at[1], rs.at[0], "space", s_prev, rs_out, near_num)
    late = partial_sums(3 - 2 * core)
    total = partial_sums(0)
    normed, factor = rms(xc[:, 0].reshape(TOK, D).astype(F32))
    for h, part in enumerate(halves):
        landed(rf.at[part], rf_num[h])
        rsend[2, part] = (late[part] + rf[part].astype(F32)).astype(BF)
        push(rsend.at[2, part], rs.at[1, part], "space", s_next, rs_out, late_num[h])
    landed(rs.at[0], near_num)
    total += rs[0].astype(F32)
    for h, part in enumerate(halves):
        landed(rs.at[1, part], late_num[h])
    total += rs[1].astype(F32)
    landed(u3.at[1:NV], u3_num)
    out_ref[...] = finish(u3[...].reshape(TOK, D), normed, factor, total)

    for ref, number in left:
        gone(ref, number)


def on_device(latents, cotangent, wqs, wos, wqv, wov, wqt, wot):
    vmem = pl.BlockSpec(memory_space=pltpu.VMEM)
    hbm = pl.BlockSpec(memory_space=pltpu.HBM)

    def buf(*shape, dtype=BF):
        return pltpu.VMEM(shape, dtype)

    wide = NSP * LH * TOK
    out = pl.pallas_call(
        body,
        out_shape=jax.ShapeDtypeStruct((TOK, D), BF),
        in_specs=[hbm] * 8,
        out_specs=vmem,
        scratch_shapes=[
            buf(NV, 2, CH, D),
            buf(3 * LW, D),
            buf(NSP, TOK, D),
            buf(NSP * TOK, LW),
            buf(NSP * TOK, LW),
            buf(LW, wide),
            buf(2 * LW, NSP * TOK),
            buf(NSP * TOK, wide),
            buf(NSP * TOK, wide),
            buf(wide, LW),
            buf(NSP, LW, TOK),
            buf(NSP, NV, CH, LW),
            buf(NSP, NV, CH, LW),
        ]
        + [buf(NV, 2, CH, D)]
        + [buf(NV, CH, D)] * 8
        + [
            buf(NSP, NV, CH, LW),
            buf(NSP, NV, CH, LW),
            buf(3, TOK, D),
            buf(2, TOK, D),
            buf(TOK, D),
            buf(TOK, GH * TOK, dtype=F32),
            buf(GROUPS, GW, TOK),
            buf(GROUPS, GW, TOK),
            buf(GROUPS, TOK, GW),
            buf(GROUPS, GW, GH * TOK),
            buf(GROUPS, TOK, GH * TOK),
            buf(9, D, D),
            pltpu.SemaphoreType.DMA((NSEM,)),
            pltpu.SemaphoreType.DMA((NSEM,)),
            pltpu.SemaphoreType.DMA((8,)),
        ],
        compiler_params=pltpu.CompilerParams(
            collective_id=0, has_side_effects=True, vmem_limit_bytes=VMEM
        ),
        name="block_backward",
    )(
        latents.reshape(NV, CH, D),
        cotangent.reshape(NV, CH, D),
        wqs.reshape(3 * LW, D),
        wos[None],
        wqv,
        wov[None],
        wqt,
        wot[None],
    )
    return out[None, None]


def solution(mesh):
    in_specs = (
        P("view", "tm", "space", None),
        P("view", "tm", "space", None),
        P(None, "space", None),
        P("space", None),
        P(None, "space", None),
        P("space", None),
        P(None, "space", None),
        P("space", None),
    )
    return jax.shard_map(
        on_device,
        mesh=mesh,
        in_specs=in_specs,
        out_specs=P("view", "tm", "space", None),
        check_vma=False,
    )
```

```python
import jax
import jax.numpy as jnp
from jax import lax
from jax.experimental import pallas as pl
from jax.experimental.pallas import tpu as pltpu
from jax.sharding import PartitionSpec as P

MESH = pl.DeviceIdType.MESH
BF = jnp.bfloat16
F32 = jnp.float32
NN = ((1,), (0,))
NT = ((1,), (1,))
TN = ((0,), (0,))

D = 768
TOK = 128
NSP = 4
NV = 8
NT_ = 8
CH = 16
HD = 64
LH = 3
LW = LH * HD
GH = 4
GW = GH * HD
GROUPS = D // GW
SCALE = HD**-0.5
NSEM = 64
VMEM = 859 * 65536


def dot(a, b, dims):
    return lax.dot_general(a, b, (dims, ((), ())), preferred_element_type=F32)


def rms(values):
    factor = lax.rsqrt(jnp.mean(values * values, axis=-1, keepdims=True) + 1e-06)
    return values * factor, factor


def finish(upstream, normed, factor, normed_grad):
    inner = jnp.mean(normed_grad * normed, axis=-1, keepdims=True)
    return (upstream.astype(F32) + factor * (normed_grad - normed * inner)).astype(BF)


def softmax0(scores):
    top = jnp.max(scores, axis=0, keepdims=True)
    expo = jnp.exp(scores - top)
    return expo * (1.0 / jnp.sum(expo, axis=0, keepdims=True))


def head_masks(rows):
    head = lax.broadcasted_iota(jnp.int32, (rows, TOK), 0) // HD
    return [(head == h).astype(F32).astype(BF) for h in range(rows // HD)]


def stacked(values, masks):
    return jnp.concatenate([values * m for m in masks], axis=1)


def per_head(left, right):
    heads = left.shape[0] // HD
    return jnp.concatenate(
        [
            dot(left[h * HD : (h + 1) * HD], right[:, h * TOK : (h + 1) * TOK], NN)
            for h in range(heads)
        ],
        axis=0,
    )


def body(
    x_in, cot_in, wqs_in, wos_in, wqv_in, wov_in, wqt_in, wot_in,
    out_ref,
    xc, wqs_ref,
    nb, k_nat, v_nat, qts, kvt, pts, gts, ogts, dqt, ats, att,
    xb, x2, xt, x3, c2, ut, u2, uv, u3, ogs, og, rsend, rs, rf,
    bias, kt_v, vt_v, v_v, qts_v, pt_v,
    whole,
    send_sem, recv_sem, local_sem,
):
    t = lax.axis_index("tm")
    v = lax.axis_index("view")
    s = lax.axis_index("space")
    core = lax.rem(t, 2)
    sibling = t + 1 - 2 * core
    y = lax.rem(v, 4)
    half = lax.rem(y, 2)
    step = 1 - 2 * core
    y_next = v - y + lax.rem(y + step + 4, 4)
    s_next = lax.rem(s + step + 4, 4)
    s_prev = lax.rem(s - step + 4, 4)

    def plus(me, k, n):
        return lax.rem(me + k + n, n)

    bits = [t % 2, t // 2 % 2, t // 4]

    def paired(m):
        return t + sum((1 - 2 * bits[at]) * 2**at for at in range(3) if m >> at & 1)

    tm_order = (6, 7, 4, 5, 2, 3, 1)
    left = []
    count = [0]

    def ticket():
        count[0] += 1
        return count[0] - 1

    def remote(src, dst, axis, index, number, arrival):
        to = {axis: index} if isinstance(axis, str) else dict(zip(axis, index))
        return pltpu.make_async_remote_copy(
            src_ref=src,
            dst_ref=dst,
            send_sem=send_sem.at[number],
            recv_sem=recv_sem.at[arrival],
            device_id=to,
            device_id_type=MESH,
        )

    def push(src, dst, axis, index, number, arrival):
        remote(src, dst, axis, index, number, arrival).start()

    def landed(ref, arrival):
        remote(ref, ref, "tm", sibling, 0, arrival).wait_recv()

    def gone(ref, number):
        remote(ref, ref, "tm", sibling, number, 0).wait_send()

    def sending(ref):
        left.append((ref, ticket()))
        return left[-1][1]

    def rows(owner, c, h, size):
        return pl.ds(pl.multiple_of(owner * LW + c * 96 + h * 48, 16), size)

    class Gather:
        def __init__(self, first, end):
            self.first, self.end = first, end
            self.others = [plus(s, -1, 4), plus(s, 1, 4), plus(s, 2, 4)]
            self.out = [sending(self.bytes_of(size)) for size in (96, 48, 144, 288)]
            self.near, self.far, self.y_near, self.y_far, self.sib = [ticket() for _ in range(5)]

        def bytes_of(self, size):
            return whole.at[self.first : self.end, 0:size, :]

        def piece(self, owner, c, h, size=48):
            return whole.at[self.first : self.end, rows(owner, c, h, size), :]

        def a(self):
            mine = self.piece(s, core, half)
            push(mine, mine, "space", plus(s, 1, 4), self.out[0], self.near)
            push(mine, mine, "space", plus(s, -1, 4), self.out[0], self.near)

        def b(self):
            landed(self.bytes_of(96), self.near)
            far = self.piece(s_prev, core, half)
            push(far, far, "space", s_next, self.out[1], self.far)
            for at in range(2):
                part = self.piece(self.others[at], core, half)
                push(part, part, "view", y_next, self.out[2], self.y_near)

        def c(self):
            landed(self.bytes_of(48), self.far)
            part = self.piece(self.others[2], core, half)
            push(part, part, "view", y_next, self.out[2], self.y_far)

        def d(self):
            landed(self.bytes_of(96), self.y_near)
            for at in range(3):
                if at == 2:
                    landed(self.bytes_of(48), self.y_far)
                part = self.piece(self.others[at], core, 0, 96)
                push(part, part, "tm", sibling, self.out[3], self.sib)

        def e(self):
            landed(self.bytes_of(288), self.sib)

    g_a, g_b, g_c = Gather(0, 4), Gather(4, 6), Gather(6, 9)
    wos, wqv, wov = whole.at[0:1], whole.at[1:4], whole.at[4:5]
    wot, wqt = whole.at[5:6], whole.at[6:9]
    own = pl.ds(pl.multiple_of(s * LW, 16), LW)

    loads = [
        pltpu.make_async_copy(src, dst, local_sem.at[at])
        for at, (src, dst) in enumerate(
            (
                (x_in, xc.at[:, 0]),
                (wqs_in, wqs_ref),
                (cot_in, xc.at[:, 1]),
                (wos_in, wos.at[:, own, :]),
                (wqv_in, wqv.at[:, own, :]),
                (wov_in, wov.at[:, own, :]),
                (wot_in, wot.at[:, own, :]),
                (wqt_in, wqt.at[:, own, :]),
            )
        )
    ]
    for copy in loads:
        copy.start()

    barrier = pltpu.get_barrier_semaphore()
    for k in range(NSP):
        for j in range(NV):
            if k or j:
                pl.semaphore_signal(
                    barrier,
                    inc=1,
                    device_id={"view": plus(v, j, NV), "space": plus(s, k, NSP)},
                    device_id_type=MESH,
                )
    for k in range(1, NT_):
        pl.semaphore_signal(barrier, inc=1, device_id={"tm": plus(t, k, NT_)}, device_id_type=MESH)

    loads[0].wait()
    x_rows = xc[:, 0].reshape(TOK, D)
    normed, _ = rms(x_rows.astype(F32))
    nb[0] = normed.astype(BF)
    key_at = lax.broadcasted_iota(jnp.int32, (TOK, GH * TOK), 0)
    query_at = lax.broadcasted_iota(jnp.int32, (TOK, GH * TOK), 1)
    bias[...] = jnp.where(lax.rem(key_at, CH) == lax.rem(query_at, CH), 0.0, -1e30)
    lmask = head_masks(LW)
    gmask = head_masks(GW)
    pl.semaphore_wait(barrier, NSP * NV + NT_ - 2)

    halves = [slice(0, TOK // 2), slice(TOK // 2, TOK)]
    n_near, n_far = [ticket() for _ in halves], [ticket() for _ in halves]
    n_out = sending(nb.at[0:2]), sending(nb.at[0])
    for h, part in enumerate(halves):
        for k in (1, 3):
            push(nb.at[0, part], nb.at[k, part], "space", plus(s, k, NSP), n_out[0], n_near[h])
    for copy in loads[1:]:
        copy.wait()
    order = (4, 3, 5, 2, 6, 1, 7)
    x2_num, x2_out = ticket(), sending(xb.at[1:NV])
    for j in order:
        to = plus(v, j, NV)
        push(xc.at[to], xb.at[j], "view", to, x2_out, x2_num)
    xb[0] = xc[v]

    def project_space(k):
        tokens = nb[k]
        packed = dot(wqs_ref[...], tokens, NT)
        at = slice(k * TOK, (k + 1) * TOK)
        query = packed[:LW].astype(BF) * jnp.asarray(SCALE, BF)
        qts[:, k * LH * TOK : (k + 1) * LH * TOK] = stacked(query, lmask)
        kvt[:, at] = packed[LW:].astype(BF)
        k_nat[at, :] = jnp.transpose(packed[LW : 2 * LW]).astype(BF)
        v_nat[at, :] = jnp.transpose(packed[2 * LW :]).astype(BF)

    project_space(0)
    for h, part in enumerate(halves):
        landed(nb.at[0], n_near[h])
        push(nb.at[1 + 2 * core, part], nb.at[2, part], "space", s_next, n_out[1], n_far[h])
    g_a.a()
    project_space(1)
    project_space(3)
    for h, part in enumerate(halves):
        landed(nb.at[2, part], n_far[h])
    project_space(2)

    a_num = [ticket() for _ in range(NSP)]
    a_out = sending(ats.at[0, 1:NV]), sending(ats.at[1:NSP])

    def attend_space(k):
        at = slice(k * LH * TOK, (k + 1) * LH * TOK)
        shares = softmax0(dot(k_nat[...], qts[:, at], NN)).astype(BF)
        pts[:, at] = shares
        out = jnp.transpose(per_head(kvt[LW:, :], shares)).astype(BF)
        ats[k] = out.reshape(NV, CH, LW)

    def send_attended(k):
        for j in order + (0,):
            to = (plus(v, j, NV), plus(s, -k, NSP))
            if k or j:
                push(ats.at[k, to[0]], att.at[s, j], ("view", "space"), to, a_out[min(k, 1)], a_num[k])
            else:
                att[pl.ds(s, 1), 0:1] = ats[0:1, pl.ds(v, 1)]

    attend_space(2)
    attend_space(1)
    send_attended(2)
    send_attended(1)
    g_a.b()
    g_b.a()
    attend_space(3)
    attend_space(0)
    send_attended(3)
    send_attended(0)
    g_a.c()
    g_b.b()
    g_c.a()
    g_a.d()
    g_b.c()

    def slot_of(view):
        return lax.rem(v - view + NV, NV)

    g_b.d()
    landed(xb.at[1:NV], x2_num)
    for k in (2, 1, 3):
        landed(att.at[plus(s, k, NSP)], a_num[k])
    landed(att.at[s, 1:NV], a_num[0])
    c2_num, c2_out = ticket(), sending(c2.at[1:NT_])
    for m in tm_order:
        push(xb.at[slot_of(paired(m)), 1], c2.at[m], "tm", paired(m), c2_out, c2_num)
    c2[0] = xb[slot_of(t), 1]
    g_c.b()
    g_a.e()
    term = dot(att[0].reshape(TOK, LW), wos[0, :LW, :], NN)
    for h in range(1, NSP):
        term += dot(att[h].reshape(TOK, LW), wos[0, h * LW : (h + 1) * LW, :], NN)
    x2[...] = (xb[:, 0].reshape(TOK, D).astype(F32) + term).astype(BF).reshape(NV, CH, D)
    rows_view = x2[...].reshape(TOK, D)
    normed, _ = rms(rows_view.astype(F32))
    tokens = normed.astype(BF)

    def attend_small(w, g):
        lanes = slice(g * GW, (g + 1) * GW)
        query = dot(w[0, lanes, :], tokens, NT).astype(BF) * jnp.asarray(SCALE, BF)
        key_t = dot(w[1, lanes, :], tokens, NT).astype(BF)
        value_t = dot(w[2, lanes, :], tokens, NT).astype(BF)
        queries = stacked(query, gmask)
        shares = softmax0(dot(key_t, queries, TN) + bias[...]).astype(BF)
        return queries, key_t, value_t, shares

    def backward_small(queries, key_t, value, shares, grads):
        share_grad = dot(value, grads, NN)
        wide = shares.astype(F32)
        row_dot = jnp.sum(wide * share_grad, axis=0, keepdims=True)
        score_grad = (wide * (share_grad - row_dot)).astype(BF)
        query_grad = (per_head(key_t, score_grad) * SCALE).astype(BF)
        key_grad = dot(score_grad, queries, NT).astype(BF)
        value_grad = dot(shares, grads, NT).astype(BF)
        return jnp.transpose(query_grad), key_grad, value_grad

    def normed_grad_of(parts, w):
        columns = [part[at] for at in range(3) for part in parts]
        return dot(jnp.concatenate(columns, axis=1), w[...].reshape(3 * D, D), NN)

    outs = []
    for g in range(GROUPS):
        queries, key_t, value_t, shares = attend_small(wqv, g)
        qts_v[g], kt_v[g], vt_v[g], pt_v[g] = queries, key_t, value_t, shares
        outs.append(per_head(value_t, shares).astype(BF))
    g_c.c()
    g_b.e()
    term = dot(jnp.concatenate(outs, axis=0), wov[0], TN)
    xt[...] = (rows_view.astype(F32) + term).astype(BF).reshape(NV, CH, D)

    x3_num, x3_out = ticket(), sending(x3.at[1:NT_])
    for m in tm_order:
        push(xt.at[slot_of(paired(m))], x3.at[m], "tm", paired(m), x3_out, x3_num)
    x3[0] = xt[slot_of(t)]
    g_c.d()
    landed(c2.at[1:NT_], c2_num)
    upstream = c2[...].reshape(TOK, D)
    out_grads = dot(wot[0], upstream, NT).astype(BF)
    grads_t = [stacked(out_grads[g * GW : (g + 1) * GW], gmask) for g in range(GROUPS)]
    for g in range(GROUPS):
        v_v[g] = jnp.transpose(vt_v[g])
    landed(x3.at[1:NT_], x3_num)
    g_c.e()
    rows_time = x3[...].reshape(TOK, D)
    normed, factor = rms(rows_time.astype(F32))
    tokens = normed.astype(BF)

    parts = []
    for g in range(GROUPS):
        queries, key_t, value_t, shares = attend_small(wqt, g)
        parts.append(backward_small(queries, key_t, jnp.transpose(value_t), shares, grads_t[g]))
    total = normed_grad_of(parts, wqt)
    ut[...] = finish(upstream, normed, factor, total).reshape(NT_, CH, D)

    u2_num, u2_out = ticket(), sending(ut.at[1:NT_])
    here = slot_of(t)
    for m in tm_order:
        push(ut.at[m], u2.at[here], "tm", paired(m), u2_out, u2_num)
    u2[pl.ds(here, 1)] = ut[0:1]
    normed, factor = rms(x2[...].reshape(TOK, D).astype(F32))
    for ref, number in left[:-1]:
        gone(ref, number)
    del left[:-1]
    landed(u2.at[1:NT_], u2_num)
    upstream = u2[...].reshape(TOK, D)
    parts = []
    for g in range(GROUPS):
        out_grad = dot(wov[0, g * GW : (g + 1) * GW, :], upstream, NT).astype(BF)
        saved = qts_v[g], kt_v[g], v_v[g], pt_v[g]
        parts.append(backward_small(*saved, stacked(out_grad, gmask)))
    upstream = finish(upstream, normed, factor, normed_grad_of(parts, wqv))
    uv[...] = upstream.reshape(NV, CH, D)

    out_grad = dot(wos[0], upstream, NT)
    for h in range(NSP):
        part = jnp.transpose(out_grad[h * LW : (h + 1) * LW]).astype(BF)
        ogs[h] = part.reshape(NV, CH, LW)
    og_num = [ticket() for _ in range(NSP)]
    og_out = sending(ogs.at[0, 1:NV]), sending(ogs.at[1:NSP])
    for k in (2, 1, 3, 0):
        for j in order + (0,):
            to = (plus(v, -j, NV), plus(s, k, NSP))
            if k or j:
                push(ogs.at[to[1], j], og.at[k, v], ("view", "space"), to, og_out[min(k, 1)], og_num[k])
    og[0:1, pl.ds(v, 1)] = ogs[pl.ds(s, 1), 0:1]
    def backward_space(k):
        at = slice(k * LH * TOK, (k + 1) * LH * TOK)
        out_grad = og[k].reshape(TOK, LW)
        grads = jnp.concatenate([out_grad * m for m in nmask], axis=0)
        ogts[at, :] = grads
        share_grad = dot(v_nat[...], grads, NT)
        wide = pts[:, at].astype(F32)
        row_dot = jnp.sum(wide * share_grad, axis=0, keepdims=True)
        score_grad = (wide * (share_grad - row_dot)).astype(BF)
        gts[:, at] = score_grad
        dqt[k] = (per_head(kvt[:LW, :], score_grad) * SCALE).astype(BF)

    head_at = lax.broadcasted_iota(jnp.int32, (TOK, LW), 1) // HD
    nmask = [(head_at == h).astype(F32).astype(BF) for h in range(LH)]
    u3_num, u3_out = ticket(), sending(uv.at[1:NV])
    landed(og.at[0, 1:NV], og_num[0])
    for k in (1, 3, 2):
        landed(og.at[k], og_num[k])
    for j in order:
        push(uv.at[j], u3.at[v], "view", plus(v, -j, NV), u3_out, u3_num)
    for k in range(NSP):
        backward_space(k)
    u3[pl.ds(v, 1)] = uv[0:1]

    def partial_sums(k):
        at = pl.ds(pl.multiple_of(k * TOK, TOK), TOK)
        key_grad = dot(gts[at, :], qts[...], NT).astype(BF)
        value_grad = dot(pts[at, :], ogts[...], NN).astype(BF)
        part = dot(dqt[k], wqs_ref[:LW, :], TN)
        part += dot(key_grad, wqs_ref[LW : 2 * LW, :], NN)
        return part + dot(value_grad, wqs_ref[2 * LW :, :], NN)

    rf_num, late_num = [ticket() for _ in halves], [ticket() for _ in halves]
    near_num = ticket()
    rs_out = sending(rsend)
    rsend[0] = partial_sums(2).astype(BF)
    for h, part in enumerate(halves):
        push(rsend.at[0, part], rf.at[part], "space", s_next, rs_out, rf_num[h])
    rsend[1] = partial_sums(1 + 2 * core).astype(BF)
    push(rsend.at[1], rs.at[0], "space", s_prev, rs_out, near_num)
    late = partial_sums(3 - 2 * core)
    total = partial_sums(0)
    normed, factor = rms(xc[:, 0].reshape(TOK, D).astype(F32))
    for h, part in enumerate(halves):
        landed(rf.at[part], rf_num[h])
        rsend[2, part] = (late[part] + rf[part].astype(F32)).astype(BF)
        push(rsend.at[2, part], rs.at[1, part], "space", s_next, rs_out, late_num[h])
    landed(rs.at[0], near_num)
    total += rs[0].astype(F32)
    for h, part in enumerate(halves):
        landed(rs.at[1, part], late_num[h])
    total += rs[1].astype(F32)
    landed(u3.at[1:NV], u3_num)
    out_ref[...] = finish(u3[...].reshape(TOK, D), normed, factor, total)

    for ref, number in left:
        gone(ref, number)


def on_device(latents, cotangent, wqs, wos, wqv, wov, wqt, wot):
    vmem = pl.BlockSpec(memory_space=pltpu.VMEM)
    hbm = pl.BlockSpec(memory_space=pltpu.HBM)

    def buf(*shape, dtype=BF):
        return pltpu.VMEM(shape, dtype)

    wide = NSP * LH * TOK
    out = pl.pallas_call(
        body,
        out_shape=jax.ShapeDtypeStruct((TOK, D), BF),
        in_specs=[hbm] * 8,
        out_specs=vmem,
        scratch_shapes=[
            buf(NV, 2, CH, D),
            buf(3 * LW, D),
            buf(NSP, TOK, D),
            buf(NSP * TOK, LW),
            buf(NSP * TOK, LW),
            buf(LW, wide),
            buf(2 * LW, NSP * TOK),
            buf(NSP * TOK, wide),
            buf(NSP * TOK, wide),
            buf(wide, LW),
            buf(NSP, LW, TOK),
            buf(NSP, NV, CH, LW),
            buf(NSP, NV, CH, LW),
        ]
        + [buf(NV, 2, CH, D)]
        + [buf(NV, CH, D)] * 8
        + [
            buf(NSP, NV, CH, LW),
            buf(NSP, NV, CH, LW),
            buf(3, TOK, D),
            buf(2, TOK, D),
            buf(TOK, D),
            buf(TOK, GH * TOK, dtype=F32),
            buf(GROUPS, GW, TOK),
            buf(GROUPS, GW, TOK),
            buf(GROUPS, TOK, GW),
            buf(GROUPS, GW, GH * TOK),
            buf(GROUPS, TOK, GH * TOK),
            buf(9, D, D),
            pltpu.SemaphoreType.DMA((NSEM,)),
            pltpu.SemaphoreType.DMA((NSEM,)),
            pltpu.SemaphoreType.DMA((8,)),
        ],
        compiler_params=pltpu.CompilerParams(
            collective_id=0, has_side_effects=True, vmem_limit_bytes=VMEM
        ),
        name="block_backward",
    )(
        latents.reshape(NV, CH, D),
        cotangent.reshape(NV, CH, D),
        wqs.reshape(3 * LW, D),
        wos[None],
        wqv,
        wov[None],
        wqt,
        wot[None],
    )
    return out[None, None]


def solution(mesh):
    in_specs = (
        P("view", "tm", "space", None),
        P("view", "tm", "space", None),
        P(None, "space", None),
        P("space", None),
        P(None, "space", None),
        P("space", None),
        P(None, "space", None),
        P("space", None),
    )
    return jax.shard_map(
        on_device,
        mesh=mesh,
        in_specs=in_specs,
        out_specs=P("view", "tm", "space", None),
        check_vma=False,
    )
```
